32 devices in a mesh: dp: 4 (over z), pipe: 2 (over core), tensor: 4 (over y, x).
Axes of the slice: x: 2, y: 2, z: 4, core: 2. Of those that a mesh axis runs over, the one named last changes fastest.
Arguments:
- heads_out: bfloat16 [2, 512, 4096], P('pipe', 'dp', 'tensor'), may hold values from -6 to 6
- out_proj: bfloat16 [2, 4096, 4096], P('pipe', 'tensor', 'dp'), may hold values from -0.09375 to 0.09375
- encoder: bfloat16 [2, 512, 4096], P('pipe', None, 'dp'), may hold values from -0.09375 to 0.09375
- decoder: bfloat16 [2, 512, 4096], P('pipe', None, 'tensor'), may hold values from -1.767767 to 1.767767
- norm_gain: float32 [2, 4096], P('pipe', 'tensor'), may hold values from 0.25 to 1.75
- send_encoder: bfloat16 [2, 4096, 128], P('pipe', 'tensor'), may hold values from -0.1875 to 0.1875
- recv_decoder: bfloat16 [2, 128, 4096], P('pipe', None, 'tensor'), may hold values from -3.535534 to 3.535534
- input_code: bfloat16 [512, 512], P('dp', 'tensor'), may hold values from -40 to 40
- code_cotangent: bfloat16 [512, 512], P('dp', 'tensor'), may hold values from -4 to 4
Outputs:
- sent_codes: bfloat16 [2, 512, 512], P('pipe', 'dp', 'tensor')
- returned_codes: bfloat16 [2, 512, 512], P('pipe', 'dp', 'tensor')
- heads_grad: bfloat16 [2, 512, 4096], P('pipe', 'dp', 'tensor')
- proj_grad: bfloat16 [2, 4096, 4096], P('pipe', 'tensor', 'dp')
- encoder_grad: bfloat16 [2, 512, 4096], P('pipe', 'tensor', 'dp')
- decoder_grad: bfloat16 [2, 512, 4096], P('pipe', 'dp', 'tensor')
- gain_grad: float32 [2, 4096], P('pipe', 'tensor')
- send_grad: bfloat16 [2, 4096, 128], P('pipe', 'tensor')
- recv_grad: bfloat16 [2, 128, 4096], P('pipe', None, 'tensor')
The draws below stay inside these ranges and needn't reach their ends.
All inputs are finite; a program needn't handle non-finite values.
Results may differ from the reference program's by a relative error of at most 0.035.
Values may be sent and summed in bfloat16 or wider, within the bound.
No kernel may reach another device: no remote copies, remote signals or barrier semaphores. Data moves between devices by JAX's collectives and lax.ppermute only.
A program may use at most 64 MiB of HBM per device.

```python
import math
import jax
import jax.numpy as jnp
from jax import lax

D = 4096
C = 512
TOK_DEV = 128
SECTIONS = 2
TOKENS = 512
GROUPS = 4
HW = 4096
BLOCKS = 4
DB = 1024
CB = 128
N_TENSOR = 4


def column_law(key, row_extent, breadth, fan_in):
    first_key, second_key = jax.random.split(key)
    entries = jnp.clip(jax.random.normal(first_key, (SECTIONS, row_extent, breadth), jnp.float32), -4.0, 4.0)
    spread = math.log(10.0)
    levels = jax.random.uniform(second_key, (SECTIONS, 1, breadth), jnp.float32)
    rising = jnp.exp(math.log(3.0) * jnp.arange(breadth, dtype=jnp.float32) / breadth)
    return (entries * jnp.exp(spread * levels) * rising / (3.0 * math.sqrt(fan_in))).astype(jnp.bfloat16)


def draw_decoder(key, part):
    return column_law(jax.random.fold_in(key, 5), C, D, C)


def draw_recv_decoder(key, part):
    return column_law(jax.random.fold_in(key, 7), CB, D, CB)


def draw_input_code(key, part):
    first_key, second_key = jax.random.split(jax.random.fold_in(key, 11))
    entries = jnp.clip(jax.random.normal(first_key, (TOKENS, C), jnp.float32), -4.0, 4.0)
    spread = math.log(10.0)
    levels = jax.random.uniform(second_key, (TOKENS, 1), jnp.float32)
    return (entries * jnp.exp(spread * levels)).astype(jnp.bfloat16)


def draw_code_cotangent(key, part):
    first_key = jax.random.fold_in(jax.random.fold_in(key, 23), 0)
    entries = jnp.clip(jax.random.normal(first_key, (TOKENS, C), jnp.float32), -4.0, 4.0)
    return entries.astype(jnp.bfloat16)


def shard_levels(rng, extent, cuts, smallest, high):
    level = 1.0
    for axis_at, shards_of in cuts:
        steps = jax.random.uniform(jax.random.fold_in(jax.random.fold_in(rng, 6), axis_at), (shards_of,), jnp.float32, smallest / len(cuts), high / len(cuts))
        level = level * jnp.repeat(jnp.exp(steps), extent[axis_at] // shards_of).reshape((-1,) + (1,) * (len(extent) - 1 - axis_at))
    return level


def scatter_about(key, dims, scale, limit, cuts=(), kind=jnp.bfloat16):
    values = scale * jax.random.normal(key, dims, jnp.float32)
    if cuts:
        values = values * shard_levels(key, dims, cuts, -0.22, 0.18)
    return jnp.clip(values, -limit, limit).astype(kind)


def setup_inputs(seed: int = 0) -> dict:
    keys = jax.random.split(jax.random.key(seed), 10)
    return {
        "heads_out": scatter_about(keys[0], (SECTIONS, TOKENS, HW), 1.0, 6.0, ((0, 2), (1, 4), (2, 4))),
        "out_proj": scatter_about(keys[1], (SECTIONS, HW, D), HW ** -0.5, 0.09375, ((0, 2), (1, 4), (2, 4))),
        "encoder": scatter_about(keys[2], (SECTIONS, C, D), D ** -0.5, 0.09375, ((0, 2), (2, 4))),
        "decoder": draw_decoder(jax.random.fold_in(keys[9], 71), 0),
        "norm_gain": jnp.clip(1.0 + 0.15 * jax.random.normal(keys[4], (SECTIONS, D), jnp.float32), 0.25, 1.75),
        "send_encoder": scatter_about(keys[5], (SECTIONS, D, CB), (D // N_TENSOR) ** -0.5, 0.1875, ((0, 2), (1, 4))),
        "recv_decoder": draw_recv_decoder(jax.random.fold_in(keys[9], 71), 0),
        "input_code": draw_input_code(jax.random.fold_in(keys[9], 71), 0),
        "code_cotangent": draw_code_cotangent(jax.random.fold_in(keys[9], 71), 0),
    }


epsilon = 1e-05
highest_precision = lax.Precision.HIGHEST

def rounded(values):
    return lax.optimization_barrier(values.astype(jnp.bfloat16)).astype(jnp.float32)

def group_sum(left_rows, right_rows):
    left_groups = left_rows.astype(jnp.float32).reshape(GROUPS, TOK_DEV, -1)
    right_groups = right_rows.astype(jnp.float32).reshape(GROUPS, TOK_DEV, -1)
    group_terms = jnp.einsum('kta,ktb->kab', left_groups, right_groups, precision=highest_precision)
    return lax.optimization_barrier(jnp.sum(rounded(group_terms), axis=0))

def apply_blocks(left_rows, stacked_parts):
    tokens_all = left_rows.shape[0]
    section_parts = left_rows.astype(jnp.float32).reshape(tokens_all, BLOCKS, stacked_parts.shape[1])
    final_output = jnp.einsum('laj,ajd->lad', section_parts, stacked_parts.astype(jnp.float32), precision=highest_precision)
    return final_output.reshape(tokens_all, -1)

def reference(heads_out, out_proj, encoder, decoder, norm_gain, send_encoder, recv_decoder, input_code, code_cotangent):
    head_block = HW // BLOCKS
    mix_codes = []
    folds = []
    for layer_num in range(SECTIONS):
        fold = jnp.dot(out_proj[layer_num], encoder[layer_num].T, preferred_element_type=jnp.float32)
        folds.append(fold)
        summed = jnp.zeros((TOKENS, C), jnp.float32)
        for block_num in range(BLOCKS):
            row_span = slice(block_num * head_block, (block_num + 1) * head_block)
            piece = jnp.dot(heads_out[layer_num][:, row_span].astype(jnp.float32), fold[row_span], precision=highest_precision)
            summed = summed + rounded(piece)
        mix_codes.append(summed.astype(jnp.bfloat16))
    received = input_code
    saved_entries = []
    sent_list = []
    for layer_num in range(SECTIONS):
        attention = jnp.dot(mix_codes[layer_num], decoder[layer_num], preferred_element_type=jnp.float32)
        recv_blocks = recv_decoder[layer_num].reshape(CB, BLOCKS, DB).transpose(1, 0, 2)
        mixed_rows = apply_blocks(received, recv_blocks) + attention
        row_scale = lax.rsqrt(lax.optimization_barrier(jnp.mean(mixed_rows * mixed_rows, axis=1, keepdims=True)) + epsilon)
        normed = mixed_rows * row_scale
        out_rows = (normed * norm_gain[layer_num]).astype(jnp.bfloat16)
        send_blocks = send_encoder[layer_num].reshape(BLOCKS, DB, CB)
        sent_code = apply_blocks(out_rows, send_blocks).astype(jnp.bfloat16)
        saved_entries.append((received, row_scale, normed, out_rows, recv_blocks, send_blocks))
        sent_list.append(sent_code)
        received = sent_code
    returned_list = [None] * SECTIONS
    heads_list = [None] * SECTIONS
    proj_list = [None] * SECTIONS
    encoder_list = [None] * SECTIONS
    decoder_list = [None] * SECTIONS
    gain_list = [None] * SECTIONS
    send_list = [None] * SECTIONS
    recv_list = [None] * SECTIONS
    incoming = code_cotangent
    for layer_num in reversed(range(SECTIONS)):
        received, row_scale, normed, out_rows, recv_blocks, send_blocks = saved_entries[layer_num]
        grad_norm = apply_blocks(incoming, send_blocks.transpose(0, 2, 1))
        gain_terms = lax.optimization_barrier(jnp.sum((grad_norm * normed).reshape(GROUPS, TOK_DEV, D), axis=1))
        gain_list[layer_num] = lax.optimization_barrier(jnp.sum(rounded(gain_terms), axis=0))
        scaled = grad_norm * norm_gain[layer_num]
        inner_sum = lax.optimization_barrier(jnp.mean(scaled * normed, axis=1, keepdims=True))
        grad_mixed = (row_scale * (scaled - normed * inner_sum)).astype(jnp.bfloat16)
        grad_code = apply_blocks(grad_mixed, recv_blocks.transpose(0, 2, 1)).astype(jnp.bfloat16)
        returned_list[layer_num] = grad_code
        send_full = group_sum(out_rows, incoming).reshape(BLOCKS, DB, BLOCKS, CB)
        send_list[layer_num] = jnp.concatenate([send_full[block_num, :, block_num, :] for block_num in range(BLOCKS)], axis=0).astype(jnp.bfloat16)
        recv_full = group_sum(received, grad_mixed).reshape(BLOCKS, CB, BLOCKS, DB)
        recv_list[layer_num] = jnp.concatenate([recv_full[block_num, :, block_num, :] for block_num in range(BLOCKS)], axis=1).astype(jnp.bfloat16)
        code_sum = jnp.zeros((TOKENS, C), jnp.float32)
        for block_num in range(BLOCKS):
            col_span = slice(block_num * DB, (block_num + 1) * DB)
            code_sum = code_sum + rounded(jnp.dot(grad_mixed[:, col_span], decoder[layer_num][:, col_span].T, preferred_element_type=jnp.float32))
        code_grad = code_sum.astype(jnp.bfloat16)
        decoder_list[layer_num] = group_sum(mix_codes[layer_num], grad_mixed).astype(jnp.bfloat16)
        head_sum = group_sum(heads_out[layer_num], code_grad).astype(jnp.bfloat16)
        proj_list[layer_num] = jnp.dot(head_sum, encoder[layer_num], preferred_element_type=jnp.float32).astype(jnp.bfloat16)
        encoder_list[layer_num] = jnp.dot(head_sum.T, out_proj[layer_num], preferred_element_type=jnp.float32).astype(jnp.bfloat16)
        heads_list[layer_num] = jnp.dot(code_grad.astype(jnp.float32), folds[layer_num].T, precision=highest_precision).astype(jnp.bfloat16)
        incoming = grad_code
    return (jnp.stack(sent_list), jnp.stack(returned_list), jnp.stack(heads_list), jnp.stack(proj_list), jnp.stack(encoder_list), jnp.stack(decoder_list), jnp.stack(gain_list), jnp.stack(send_list), jnp.stack(recv_list))
```

```python
import jax
import jax.numpy as jnp
from jax import lax
from jax.sharding import PartitionSpec as P

epsilon = 1e-05
f32 = jnp.float32
bf16 = jnp.bfloat16


def shift(shard, axis, by):
    devices = lax.axis_size(axis)
    return lax.ppermute(shard, axis, [(i, (i + by) % devices) for i in range(devices)])


def move(shard, axis, by):
    devices = lax.axis_size(axis)
    pairs = [(i, i + by) for i in range(devices) if 0 <= i + by < devices]
    return lax.ppermute(shard, axis, pairs)


def gathered(shard, axis):
    return [shard] + [shift(shard, axis, -k) for k in range(1, lax.axis_size(axis))]


def scatter_sum(blocks, axis):
    total = blocks[0].astype(f32)
    for k in range(1, len(blocks)):
        total = total + shift(blocks[k].astype(bf16), axis, k).astype(f32)
    return total


def small_sum(rows, axis):
    total = rows
    for k in range(1, lax.axis_size(axis)):
        total = total + shift(rows, axis, k)
    return total


def rolled_rows(matrix, index, count):
    size = matrix.shape[0] // count
    doubled = jnp.concatenate([matrix, matrix[:-size]])
    return lax.dynamic_slice_in_dim(doubled, index * size, matrix.shape[0])


def dot(left, right, over):
    return lax.dot_general(left, right, ((over[0], over[1]), ((), ())), preferred_element_type=f32)


def on_device(
    heads_out,
    out_proj,
    encoder,
    decoder,
    norm_gain,
    send_encoder,
    recv_decoder,
    input_code,
    code_cotangent,
):
    sections = lax.axis_size("pipe")
    section = lax.axis_index("pipe")
    groups = lax.axis_size("dp")
    parts = lax.axis_size("tensor")
    part = lax.axis_index("tensor")
    group = lax.axis_index("dp")
    width = norm_gain.shape[1] * parts
    proj = out_proj[0]
    enc = rolled_rows(encoder[0], part, parts)
    dec = rolled_rows(decoder[0], part, parts)
    gain = norm_gain[0]
    send = send_encoder[0]
    recv = recv_decoder[0]
    tokens = input_code.shape[0]
    code_cols = input_code.shape[1]

    head_rows = jnp.concatenate(gathered(heads_out[0], "dp"))
    received = jnp.concatenate(gathered(input_code, "dp"))
    incoming = jnp.concatenate(gathered(code_cotangent, "dp"))

    local_fold = dot(proj, enc, ((1,), (1,)))
    local_fold = local_fold.astype(bf16)
    partial = dot(head_rows, local_fold, ((1,), (0,)))
    over_parts = scatter_sum(
        [partial[:, k * code_cols : (k + 1) * code_cols] for k in range(parts)], "tensor"
    )
    own_code = scatter_sum(
        [over_parts[k * tokens : (k + 1) * tokens] for k in range(groups)], "dp"
    ).astype(bf16)
    code_block = jnp.concatenate(gathered(own_code, "dp"))
    mix_code = jnp.concatenate(gathered(code_block, "tensor"), axis=1)
    fold_in, mix_code = lax.optimization_barrier((local_fold, mix_code))
    fold = lax.psum(fold_in, "dp")
    attention = dot(mix_code, dec, ((1,), (0,)))

    for turn in range(sections):
        if turn > 0:
            received = jnp.where(section == turn, move(sent, "pipe", 1), received)
        mixed = attention + dot(received, recv, ((1,), (0,)))
        totals = small_sum(jnp.sum(mixed * mixed, axis=1), "tensor")
        row_scale = lax.rsqrt(totals / width + epsilon)[:, None]
        scaled_rows = (mixed * gain).astype(bf16)
        sent = (row_scale * dot(scaled_rows, send, ((1,), (0,)))).astype(bf16)
    normed = mixed * row_scale
    out_rows = (normed * gain).astype(bf16)
    for turn in range(sections):
        if turn > 0:
            incoming = jnp.where(
                section == sections - 1 - turn, move(returned, "pipe", -1), incoming
            )
        grad_norm = dot(incoming, send, ((1,), (1,)))
        scaled = grad_norm * gain
        inner = small_sum(jnp.sum(scaled * normed, axis=1), "tensor")[:, None] / width
        grad_mixed = (row_scale * (scaled - normed * inner)).astype(bf16)
        returned = dot(grad_mixed, recv, ((1,), (1,))).astype(bf16)

    code_term = dot(grad_mixed, dec, ((1,), (1,)))
    code_block = scatter_sum(
        [code_term[:, k * code_cols : (k + 1) * code_cols] for k in range(parts)], "tensor"
    ).astype(bf16)
    code_blocks = gathered(code_block, "tensor")
    code_grad = jnp.concatenate(code_blocks, axis=1)
    head_sum = dot(head_rows, code_grad, ((0,), (0,))).astype(bf16)
    enc_term = dot(head_sum, proj, ((0,), (0,)))
    enc_grad = scatter_sum(
        [enc_term[k * code_cols : (k + 1) * code_cols] for k in range(parts)], "tensor"
    ).astype(bf16)
    proj_grad = dot(head_sum, enc, ((1,), (0,))).astype(bf16)
    heads_grad = dot(code_grad[:tokens], fold, ((1,), (1,))).astype(bf16)

    codes = mix_code.shape[1]
    mine = lax.rem(group * (codes // groups) + codes - part * code_cols, codes)
    mix_cols = lax.dynamic_slice_in_dim(mix_code, mine, codes // groups, 1)
    dec_grad = dot(mix_cols, grad_mixed, ((0,), (0,))).astype(bf16)
    gain_grad = jnp.sum(grad_norm * normed, axis=0)
    send_grad = dot(out_rows, incoming, ((0,), (0,))).astype(bf16)
    recv_grad = dot(received, grad_mixed, ((0,), (0,))).astype(bf16)
    return (
        sent[None, :tokens],
        returned[None, :tokens],
        heads_grad[None],
        proj_grad[None],
        enc_grad[None],
        dec_grad[None],
        gain_grad[None],
        send_grad[None],
        recv_grad[None],
    )


def solution(mesh):
    return jax.shard_map(
        on_device,
        mesh=mesh,
        in_specs=(
            P("pipe", "dp", "tensor"),
            P("pipe", "tensor", "dp"),
            P("pipe", None, "dp"),
            P("pipe", None, "tensor"),
            P("pipe", "tensor"),
            P("pipe", "tensor", None),
            P("pipe", None, "tensor"),
            P("dp", "tensor"),
            P("dp", "tensor"),
        ),
        out_specs=(
            P("pipe", "dp", "tensor"),
            P("pipe", "dp", "tensor"),
            P("pipe", "dp", "tensor"),
            P("pipe", "tensor", "dp"),
            P("pipe", "tensor", "dp"),
            P("pipe", "dp", "tensor"),
            P("pipe", "tensor"),
            P("pipe", "tensor", None),
            P("pipe", None, "tensor"),
        ),
        check_vma=False,
    )
```

```python
import jax
import jax.numpy as jnp
from jax import lax
from jax.sharding import PartitionSpec as P

epsilon = 1e-05
f32 = jnp.float32
bf16 = jnp.bfloat16


def shift(shard, axis, by):
    devices = lax.axis_size(axis)
    return lax.ppermute(shard, axis, [(i, (i + by) % devices) for i in range(devices)])


def move(shard, axis, by):
    devices = lax.axis_size(axis)
    pairs = [(i, i + by) for i in range(devices) if 0 <= i + by < devices]
    return lax.ppermute(shard, axis, pairs)


def exchanged(blocks, axis):
    return lax.all_to_all(blocks, axis, 0, 0)


def spread(shard, axis):
    copies = jnp.broadcast_to(shard[None], (lax.axis_size(axis),) + shard.shape)
    return exchanged(copies, axis)


def summed(blocks, axis):
    return jnp.sum(exchanged(jnp.stack(blocks).astype(bf16), axis).astype(f32), axis=0)


def gathered(shard, axis):
    return [shard] + [shift(shard, axis, -k) for k in range(1, lax.axis_size(axis))]


def scatter_sum(blocks, axis):
    total = blocks[0].astype(f32)
    for k in range(1, len(blocks)):
        total = total + shift(blocks[k].astype(bf16), axis, k).astype(f32)
    return total


def small_sum(rows, axis):
    return jnp.sum(spread(rows, axis), axis=0)


def dot(left, right, over):
    return lax.dot_general(left, right, ((over[0], over[1]), ((), ())), preferred_element_type=f32)


def on_device(
    heads_out,
    out_proj,
    encoder,
    decoder,
    norm_gain,
    send_encoder,
    recv_decoder,
    input_code,
    code_cotangent,
):
    sections = lax.axis_size("pipe")
    section = lax.axis_index("pipe")
    groups = lax.axis_size("dp")
    parts = lax.axis_size("tensor")
    group = lax.axis_index("dp")
    width = norm_gain.shape[1] * parts
    proj = out_proj[0]
    enc = encoder[0]
    dec = decoder[0]
    gain = norm_gain[0]
    send = send_encoder[0]
    recv = recv_decoder[0]
    tokens = input_code.shape[0]
    code_cols = input_code.shape[1]

    head_rows = jnp.concatenate(gathered(heads_out[0], "dp"))
    received = jnp.concatenate(gathered(input_code, "dp"))
    incoming = jnp.concatenate(gathered(code_cotangent, "dp"))

    local_fold = dot(proj, enc, ((1,), (1,)))
    local_fold = local_fold.astype(bf16)
    partial = dot(head_rows, local_fold, ((1,), (0,)))
    over_parts = summed(
        [partial[:, k * code_cols : (k + 1) * code_cols] for k in range(parts)], "tensor"
    )
    own_code = scatter_sum(
        [over_parts[k * tokens : (k + 1) * tokens] for k in range(groups)], "dp"
    ).astype(bf16)
    code_block = jnp.concatenate(gathered(own_code, "dp"))
    mix_code = jnp.concatenate(list(spread(code_block, "tensor")), axis=1)
    fold_in, mix_code = lax.optimization_barrier((local_fold, mix_code))
    fold = lax.psum(fold_in, "dp")
    attention = dot(mix_code, dec, ((1,), (0,)))

    for turn in range(sections):
        if turn > 0:
            received = jnp.where(section == turn, move(sent, "pipe", 1), received)
        mixed = attention + dot(received, recv, ((1,), (0,)))
        totals = small_sum(jnp.sum(mixed * mixed, axis=1), "tensor")
        row_scale = lax.rsqrt(totals / width + epsilon)[:, None]
        scaled_rows = (mixed * gain).astype(bf16)
        sent = (row_scale * dot(scaled_rows, send, ((1,), (0,)))).astype(bf16)
    normed = mixed * row_scale
    out_rows = (normed * gain).astype(bf16)
    for turn in range(sections):
        if turn > 0:
            incoming = jnp.where(
                section == sections - 1 - turn, move(returned, "pipe", -1), incoming
            )
        grad_norm = dot(incoming, send, ((1,), (1,)))
        scaled = grad_norm * gain
        inner = small_sum(jnp.sum(scaled * normed, axis=1), "tensor")[:, None] / width
        grad_mixed = (row_scale * (scaled - normed * inner)).astype(bf16)
        returned = dot(grad_mixed, recv, ((1,), (1,))).astype(bf16)

    code_term = dot(grad_mixed, dec, ((1,), (1,)))
    code_block = summed(
        [code_term[:, k * code_cols : (k + 1) * code_cols] for k in range(parts)], "tensor"
    ).astype(bf16)
    code_grad = jnp.concatenate(list(spread(code_block, "tensor")), axis=1)
    head_sum = dot(head_rows, code_grad, ((0,), (0,))).astype(bf16)
    enc_term = dot(head_sum, proj, ((0,), (0,)))
    enc_grad = summed(
        [enc_term[k * code_cols : (k + 1) * code_cols] for k in range(parts)], "tensor"
    ).astype(bf16)
    proj_grad = dot(head_sum, enc, ((1,), (0,))).astype(bf16)
    heads_grad = dot(code_grad[:tokens], fold, ((1,), (1,))).astype(bf16)

    codes = mix_code.shape[1]
    mix_cols = lax.dynamic_slice_in_dim(mix_code, group * (codes // groups), codes // groups, 1)
    dec_grad = dot(mix_cols, grad_mixed, ((0,), (0,))).astype(bf16)
    gain_grad = jnp.sum(grad_norm * normed, axis=0)
    send_grad = dot(out_rows, incoming, ((0,), (0,))).astype(bf16)
    recv_grad = dot(received, grad_mixed, ((0,), (0,))).astype(bf16)
    return (
        sent[None, :tokens],
        returned[None, :tokens],
        heads_grad[None],
        proj_grad[None],
        enc_grad[None],
        dec_grad[None],
        gain_grad[None],
        send_grad[None],
        recv_grad[None],
    )


def solution(mesh):
    return jax.shard_map(
        on_device,
        mesh=mesh,
        in_specs=(
            P("pipe", "dp", "tensor"),
            P("pipe", "tensor", "dp"),
            P("pipe", None, "dp"),
            P("pipe", None, "tensor"),
            P("pipe", "tensor"),
            P("pipe", "tensor", None),
            P("pipe", None, "tensor"),
            P("dp", "tensor"),
            P("dp", "tensor"),
        ),
        out_specs=(
            P("pipe", "dp", "tensor"),
            P("pipe", "dp", "tensor"),
            P("pipe", "dp", "tensor"),
            P("pipe", "tensor", "dp"),
            P("pipe", "tensor", "dp"),
            P("pipe", "dp", "tensor"),
            P("pipe", "tensor"),
            P("pipe", "tensor", None),
            P("pipe", None, "tensor"),
        ),
        check_vma=False,
    )
```

```python
import jax
import jax.numpy as jnp
from jax import lax
from jax.sharding import PartitionSpec as P

epsilon = 1e-05
f32 = jnp.float32
bf16 = jnp.bfloat16


def shift(shard, axis, by):
    devices = lax.axis_size(axis)
    return lax.ppermute(shard, axis, [(i, (i + by) % devices) for i in range(devices)])


def move(shard, axis, by):
    devices = lax.axis_size(axis)
    pairs = [(i, i + by) for i in range(devices) if 0 <= i + by < devices]
    return lax.ppermute(shard, axis, pairs)


def gathered(shard, axis):
    return [shard] + [shift(shard, axis, -k) for k in range(1, lax.axis_size(axis))]


def scatter_sum(blocks, axis):
    total = blocks[0].astype(f32)
    for k in range(1, len(blocks)):
        total = total + shift(blocks[k].astype(bf16), axis, k).astype(f32)
    return total


def place(axis, k):
    return lax.rem(lax.axis_index(axis) + k, lax.axis_size(axis))


def block(array, axis, k, dim):
    size = array.shape[dim] // lax.axis_size(axis)
    return lax.dynamic_slice_in_dim(array, place(axis, k) * size, size, dim)


def laid(blocks, axis, dim):
    size = blocks[0].shape[dim]
    shape = list(blocks[0].shape)
    shape[dim] = size * len(blocks)
    whole = jnp.zeros(shape, blocks[0].dtype)
    for k, part in enumerate(blocks):
        whole = lax.dynamic_update_slice_in_dim(whole, part, place(axis, k) * size, dim)
    return whole


def diagonal(blocks, axis):
    rows, cols = blocks[0].shape
    whole = jnp.zeros((rows * len(blocks), cols * len(blocks)), blocks[0].dtype)
    for k, part in enumerate(blocks):
        at = place(axis, k)
        whole = lax.dynamic_update_slice(whole, part, (at * rows, at * cols))
    return whole


def dot(left, right, over):
    return lax.dot_general(left, right, ((over[0], over[1]), ((), ())), preferred_element_type=f32)


def on_device(
    heads_out,
    out_proj,
    encoder,
    decoder,
    norm_gain,
    send_encoder,
    recv_decoder,
    input_code,
    code_cotangent,
):
    sections = lax.axis_size("pipe")
    section = lax.axis_index("pipe")
    groups = lax.axis_size("dp")
    parts = lax.axis_size("tensor")
    group = lax.axis_index("dp")
    width = norm_gain.shape[1] * parts
    proj = out_proj[0]
    enc = encoder[0]
    dec = decoder[0]
    gain = norm_gain[0]
    send = send_encoder[0]
    recv = recv_decoder[0]
    tokens, code_cols = input_code.shape
    codes = dec.shape[0]
    per_part = codes // parts

    head_rows = jnp.concatenate(gathered(heads_out[0], "dp"))
    ends = jnp.concatenate(gathered(jnp.concatenate([input_code, code_cotangent], 1), "dp"))
    end_blocks = gathered(ends, "tensor")
    received = laid([b[:, :code_cols] for b in end_blocks], "tensor", 1)
    incoming = laid([b[:, code_cols:] for b in end_blocks], "tensor", 1)

    send_gain = (send.astype(f32) * gain[:, None]).astype(bf16)
    decoders = jnp.concatenate([dec, recv])
    code_gram = dot(dec, dec, ((1,), (1,)))
    side = jnp.concatenate(
        [
            dot(recv, decoders, ((1,), (1,))),
            dot(send_gain, decoders, ((0,), (1,))),
        ],
        axis=1,
    ).astype(bf16)
    gram_rows = scatter_sum([block(code_gram, "tensor", k, 0) for k in range(parts)], "tensor")
    gram = laid(gathered(gram_rows.astype(bf16), "tensor"), "tensor", 0)
    sides = gathered(side, "tensor")
    both = codes + code_cols
    recv_code = laid([b[:, :codes] for b in sides], "tensor", 0)
    recv_recv = diagonal([b[:, codes:both] for b in sides], "tensor")
    send_code = laid([b[:, both : both + codes] for b in sides], "tensor", 0)
    send_recv = diagonal([b[:, both + codes :] for b in sides], "tensor")

    local_fold = dot(proj, enc, ((1,), (1,))).astype(bf16)
    partial = dot(head_rows, local_fold, ((1,), (0,)))
    code_block = scatter_sum([block(partial, "tensor", k, 1) for k in range(parts)], "tensor")
    code_block = code_block.astype(bf16)
    mix_block = code_block.astype(f32)
    for k in range(1, groups):
        other = shift(code_block, "dp", -k).astype(f32)
        mix_block = mix_block + jnp.concatenate([other[-k * tokens :], other[: -k * tokens]])
    mix_code = laid(gathered(mix_block.astype(bf16), "tensor"), "tensor", 1)

    mix_gram = dot(mix_code, gram, ((1,), (0,)))
    mix_recv = dot(mix_code, recv_code, ((1,), (1,)))
    mix_send = dot(mix_code, send_code, ((1,), (1,)))
    mix_square = jnp.sum(mix_gram * mix_code.astype(f32), axis=1, keepdims=True)

    for turn in range(sections):
        if turn > 0:
            received = jnp.where(section == turn, move(sent, "pipe", 1), received)
        recv_square = dot(received, recv_recv, ((1,), (0,)))
        code_mixed = mix_recv + recv_square
        totals = mix_square + jnp.sum(
            received.astype(f32) * (mix_recv + code_mixed), axis=1, keepdims=True
        )
        row_scale = lax.rsqrt(jnp.maximum(totals, 0.0) / width + epsilon)
        unscaled = mix_send + dot(received, send_recv, ((1,), (1,)))
        sent = (row_scale * unscaled).astype(bf16)
    for turn in range(sections):
        if turn > 0:
            incoming = jnp.where(
                section == sections - 1 - turn, move(returned, "pipe", -1), incoming
            )
        inner = row_scale * jnp.sum(incoming.astype(f32) * unscaled, axis=1, keepdims=True) / width
        back = dot(incoming, send_recv, ((1,), (0,)))
        returned = (row_scale * (back - row_scale * inner * code_mixed)).astype(bf16)
    code_mixed = mix_gram + dot(received, recv_code, ((1,), (0,)))
    back = dot(incoming, send_code, ((1,), (0,)))
    code_grad = (row_scale * (back - row_scale * inner * code_mixed)).astype(bf16)

    heads_term = dot(code_grad, local_fold, ((1,), (1,)))
    heads_grad = scatter_sum(
        [heads_term[k * tokens : (k + 1) * tokens] for k in range(groups)], "dp"
    ).astype(bf16)
    head_sum = dot(head_rows, code_grad, ((0,), (0,))).astype(bf16)
    enc_term = dot(head_sum, proj, ((0,), (0,)))
    enc_grad = scatter_sum([block(enc_term, "tensor", k, 0) for k in range(parts)], "tensor")
    proj_grad = dot(head_sum, enc, ((1,), (0,))).astype(bf16)

    received_here = block(received, "tensor", 0, 1)
    incoming_here = block(incoming, "tensor", 0, 1)
    mixed = dot(mix_code, dec, ((1,), (0,))) + dot(received_here, recv, ((1,), (0,)))
    normed = mixed * row_scale
    out_rows = (normed * gain).astype(bf16)
    grad_norm = dot(incoming_here, send, ((1,), (1,)))
    grad_mixed = (row_scale * (grad_norm * gain - normed * inner)).astype(bf16)
    mix_cols = block(mix_code, "dp", 0, 1)
    dec_grad = dot(mix_cols, grad_mixed, ((0,), (0,))).astype(bf16)
    gain_grad = jnp.sum(grad_norm * normed, axis=0)
    send_grad = dot(out_rows, incoming_here, ((0,), (0,))).astype(bf16)
    recv_grad = dot(received_here, grad_mixed, ((0,), (0,))).astype(bf16)
    return (
        block(sent[:tokens], "tensor", 0, 1)[None],
        block(returned[:tokens], "tensor", 0, 1)[None],
        heads_grad[None],
        proj_grad[None],
        enc_grad.astype(bf16)[None],
        dec_grad[None],
        gain_grad[None],
        send_grad[None],
        recv_grad[None],
    )


def solution(mesh):
    return jax.shard_map(
        on_device,
        mesh=mesh,
        in_specs=(
            P("pipe", "dp", "tensor"),
            P("pipe", "tensor", "dp"),
            P("pipe", None, "dp"),
            P("pipe", None, "tensor"),
            P("pipe", "tensor"),
            P("pipe", "tensor", None),
            P("pipe", None, "tensor"),
            P("dp", "tensor"),
            P("dp", "tensor"),
        ),
        out_specs=(
            P("pipe", "dp", "tensor"),
            P("pipe", "dp", "tensor"),
            P("pipe", "dp", "tensor"),
            P("pipe", "tensor", "dp"),
            P("pipe", "tensor", "dp"),
            P("pipe", "dp", "tensor"),
            P("pipe", "tensor"),
            P("pipe", "tensor", None),
            P("pipe", None, "tensor"),
        ),
        check_vma=False,
    )
```

```python
import functools

import jax
import jax.numpy as jnp
from jax import lax
from jax.experimental import pallas as pl
from jax.experimental.pallas import tpu as pltpu
from jax.sharding import PartitionSpec as P

epsilon = 1e-05
f32 = jnp.float32
bf16 = jnp.bfloat16
NN = ((1,), (0,))
NT = ((1,), (1,))
TN = ((0,), (0,))


def shift(shard, axis, by):
    devices = lax.axis_size(axis)
    return lax.ppermute(shard, axis, [(i, (i + by) % devices) for i in range(devices)])


def move(shard, axis, by):
    devices = lax.axis_size(axis)
    pairs = [(i, i + by) for i in range(devices) if 0 <= i + by < devices]
    return lax.ppermute(shard, axis, pairs)


def gathered(shard, axis):
    return [shard] + [shift(shard, axis, -k) for k in range(1, lax.axis_size(axis))]


def scattered(blocks, axis):
    return [blocks[0]] + [shift(blocks[k], axis, k) for k in range(1, len(blocks))]


def total(blocks):
    result = blocks[0].astype(f32)
    for part in blocks[1:]:
        result = result + part.astype(f32)
    return result


def block(array, axis, dim):
    size = array.shape[dim] // lax.axis_size(axis)
    return lax.dynamic_slice_in_dim(array, lax.axis_index(axis) * size, size, dim)


def dot(left, right, over):
    return lax.dot_general(left, right, (over, ((), ())), preferred_element_type=f32)


def run(kernel, results, where, groups_of_args, scratch=(), flops=0):
    counts = [len(group) for group in groups_of_args]
    flat = [array for group in groups_of_args for array in group]
    out_count = len(results)

    def body(where_ref, *refs):
        ins, at = [], 0
        for count in counts:
            ins.append(refs[at : at + count])
            at += count
        kernel(where_ref, ins, refs[at : at + out_count], refs[at + out_count :])

    size = sum(a.size * a.dtype.itemsize for a in list(flat) + list(results)) if flops else 0
    return pl.pallas_call(
        body,
        out_shape=[jax.ShapeDtypeStruct(r.shape, r.dtype) for r in results],
        in_specs=[pl.BlockSpec(memory_space=pltpu.SMEM)]
        + [pl.BlockSpec(memory_space=pltpu.VMEM)] * len(flat),
        out_specs=[pl.BlockSpec(memory_space=pltpu.VMEM)] * out_count,
        scratch_shapes=list(scratch),
        compiler_params=pltpu.CompilerParams(vmem_limit_bytes=56 << 20),
        cost_estimate=pl.CostEstimate(flops=flops, bytes_accessed=size, transcendentals=0),
    )(where, *flat)


def like(shape, dtype=bf16):
    return jax.ShapeDtypeStruct(shape, dtype)


def by_rows(rows, step):
    chunk = min(rows, 512)
    if rows == chunk:
        step(slice(0, rows))
        return

    @pl.loop(0, rows // chunk)
    def _(index):
        step(pl.ds(pl.multiple_of(index * chunk, chunk), chunk))


def gram_kernel(where, ins, outs, scratch):
    ((dec, recv, send, gain),) = ins
    side, gram = outs
    codes, relay = dec.shape[0], recv.shape[0]
    for ref, rows in ((dec, slice(0, codes)), (recv, slice(codes, codes + relay))):
        values = ref[...]
        gained = (values.astype(f32) * gain[...]).astype(bf16)
        side[rows, :relay] = dot(values, recv[...], NT).astype(bf16)
        side[rows, relay:] = dot(gained, send[...], NN).astype(bf16)
    rows = gram.shape[0]
    mine = dec[pl.ds(pl.multiple_of(where[1] * rows, rows), rows), :]
    gram[...] = dot(mine, dec[...], NT).astype(bf16)


def fold_kernel(where, ins, outs, scratch):
    ((proj, enc),) = ins
    outs[0][...] = dot(proj[...], enc[...], NT).astype(bf16)


def partial_kernel(where, ins, outs, scratch):
    heads, (fold,) = ins
    (whole,) = scratch
    tokens = heads[0].shape[0]
    cols = outs[0].shape[1]
    parts = len(outs)
    together = 4 if len(heads) % 4 == 0 else 1
    for first in range(0, len(heads), together):
        rows = slice(first * tokens, (first + together) * tokens)
        values = jnp.concatenate([h[...] for h in heads[first : first + together]])
        whole[...] = dot(values, fold[...], NN)
        for k in range(parts):
            at = lax.rem(where[0] + k, parts) * cols
            outs[k][rows, :] = whole[:, pl.ds(pl.multiple_of(at, cols), cols)].astype(bf16)


def forward(received, code_mix, code_send, square, products, width):
    relay = products.shape[1] // 2
    count = received.shape[1] // relay
    mixed, unscaled = [], []
    for k in range(count):
        cols = slice(k * relay, (k + 1) * relay)
        both = dot(received[:, cols], products[cols, :], NN)
        mixed.append(code_mix[:, cols] + both[:, :relay])
        unscaled.append(code_send[:, cols] + both[:, relay:])
    mixed = jnp.concatenate(mixed, axis=1)
    unscaled = jnp.concatenate(unscaled, axis=1)
    totals = square + jnp.sum(received.astype(f32) * (code_mix + mixed), axis=1, keepdims=True)
    row_scale = lax.rsqrt(jnp.maximum(totals, 0.0) / width + epsilon)
    return mixed, unscaled, row_scale


def backward(incoming, mixed, unscaled, row_scale, products, width):
    relay = products.shape[1] // 2
    count = incoming.shape[1] // relay
    inner = row_scale * jnp.sum(incoming.astype(f32) * unscaled, axis=1, keepdims=True) / width
    returned = []
    for k in range(count):
        cols = slice(k * relay, (k + 1) * relay)
        back = dot(incoming[:, cols], products[cols, relay:], NT)
        returned.append(row_scale * (back - row_scale * inner * mixed[:, cols]))
    return inner, jnp.concatenate(returned, axis=1).astype(bf16)


def first_kernel(width, where, ins, outs, scratch):
    mix_blocks, sides, grams, end_blocks = ins
    mix, ends, products, weights, mix_gram, mix_recv, mix_send, square, sent = outs
    (gram,) = scratch
    codes = mix.shape[1]
    relay = products.shape[1] // 2
    parts = len(mix_blocks)
    cols = codes // parts
    for k in range(parts):
        at = lax.rem(where[0] + k, parts) * cols
        mix[:, pl.ds(pl.multiple_of(at, cols), cols)] = mix_blocks[k][...]
        here = slice(k * relay, (k + 1) * relay)
        ends[:, here] = end_blocks[k][...]
        products[here, :] = sides[k][codes:, :]
        weights[:, here] = sides[k][:codes, :relay]
        there = slice((parts + k) * relay, (parts + k + 1) * relay)
        weights[:, there] = sides[k][:codes, relay:]
    rows = grams[0].shape[0]
    for k in range(len(grams)):
        at = lax.rem(where[1] + k, len(grams)) * rows
        gram[pl.ds(pl.multiple_of(at, rows), rows), :] = grams[k][...]

    def step(at):
        codes_here = mix[at, :]
        in_gram = dot(codes_here, gram[...], NN)
        sums = jnp.sum(in_gram * codes_here.astype(f32), axis=1, keepdims=True)
        in_relay = dot(codes_here, weights[...], NN)
        in_recv = in_relay[:, : parts * relay]
        in_send = in_relay[:, parts * relay :]
        mix_gram[at, :] = in_gram
        mix_recv[at, :] = in_recv
        mix_send[at, :] = in_send
        square[at, :] = sums
        mixed, unscaled, row_scale = forward(
            ends[at, :], in_recv, in_send, sums, products[...], width
        )
        sent[at, :] = (row_scale * unscaled).astype(bf16)

    by_rows(mix.shape[0], step)


def forward_kernel(width, turn, last, where, ins, outs, scratch):
    ((moved, received, ends, mix_recv, mix_send, square, products),) = ins
    live = where[2] == turn

    def step(at):
        values = jnp.where(live, moved[at, :], received[at, :])
        mixed, unscaled, row_scale = forward(
            values, mix_recv[at, :], mix_send[at, :], square[at, :], products[...], width
        )
        outs[0][at, :] = values
        outs[1][at, :] = (row_scale * unscaled).astype(bf16)
        if last:
            inner, returned = backward(
                ends[at, :], mixed, unscaled, row_scale, products[...], width
            )
            outs[2][at, :] = mixed
            outs[3][at, :] = unscaled
            outs[4][at, :] = row_scale
            outs[5][at, :] = returned

    by_rows(moved.shape[0], step)


def backward_kernel(width, live_section, last, where, ins, outs, scratch):
    (moved, incoming, received, mixed, unscaled, row_scale, mix_gram, products, weights, fold), = ins
    live = where[2] == live_section
    half = weights.shape[1] // 2
    codes = weights.shape[0]
    tokens = outs[4].shape[0] if last else 0

    def step(at):
        values = jnp.where(live, moved[at, :], incoming[at, :])
        scale = row_scale[at, :]
        inner, returned = backward(
            values, mixed[at, :], unscaled[at, :], scale, products[...], width
        )
        outs[0][at, :] = values
        outs[1][at, :] = returned
        if last:
            outs[2][at, :] = inner
            in_mixed = mix_gram[at, :] + dot(received[at, :], weights[:, :half], NT)
            back = dot(values, weights[:, half:], NT)
            outs[3][at, :] = (scale * (back - scale * inner * in_mixed)).astype(bf16)

    by_rows(moved.shape[0], step)
    if last:
        for k, out in enumerate(outs[4:]):
            rows = slice(k * tokens, (k + 1) * tokens)
            out[...] = dot(outs[3][rows, :], fold[...], NT).astype(bf16)


def head_kernel(where, ins, outs, scratch):
    heads, (code_grad, proj) = ins
    head_sum, enc_blocks = outs[0], outs[1:]
    (whole,) = scratch
    tokens = heads[0].shape[0]
    together = 4 if len(heads) % 4 == 0 else 1
    sums = None
    for first in range(0, len(heads), together):
        rows = slice(first * tokens, (first + together) * tokens)
        values = jnp.concatenate([h[...] for h in heads[first : first + together]])
        term = dot(code_grad[rows, :], values, TN)
        sums = term if sums is None else sums + term
    head_sum[...] = sums.astype(bf16)
    whole[...] = dot(head_sum[...], proj[...], NN)
    size = enc_blocks[0].shape[0]
    for k, out in enumerate(enc_blocks):
        at = lax.rem(where[0] + k, len(enc_blocks)) * size
        out[...] = whole[pl.ds(pl.multiple_of(at, size), size), :].astype(bf16)


def on_device(
    heads_out,
    out_proj,
    encoder,
    decoder,
    norm_gain,
    send_encoder,
    recv_decoder,
    input_code,
    code_cotangent,
):
    sections = lax.axis_size("pipe")
    section = lax.axis_index("pipe")
    groups = lax.axis_size("dp")
    parts = lax.axis_size("tensor")
    width = norm_gain.shape[1] * parts
    proj = out_proj[0]
    enc = encoder[0]
    dec = decoder[0]
    gain = norm_gain
    send = send_encoder[0]
    recv = recv_decoder[0]
    tokens, relay = input_code.shape
    codes, features = dec.shape
    cols = codes // parts
    rows = tokens * groups
    head_cols, model_cols = proj.shape
    where = jnp.stack([lax.axis_index("tensor"), lax.axis_index("dp"), section]).astype(jnp.int32)

    heads = gathered(heads_out[0], "dp")
    side, gram = run(
        gram_kernel,
        [like((codes + relay, 2 * relay)), like((codes // groups, codes))],
        where,
        [(dec, recv, send, gain)],
    )
    (fold,) = run(fold_kernel, [like((head_cols, codes))], where, [(proj, enc)])
    fold, side, gram = lax.optimization_barrier((fold, side, gram))
    sides = gathered(side, "tensor")
    grams = gathered(gram, "tensor")

    partials = run(
        partial_kernel,
        [like((rows, cols))] * parts,
        where,
        [heads, (fold,)],
        scratch=[pltpu.VMEM((min(groups, 4) * tokens, codes), f32)],
        flops=2 * rows * head_cols * codes,
    )
    end = jnp.where(section == 0, input_code, code_cotangent)
    end = jnp.concatenate(gathered(end, "dp"))
    gram = total(grams).astype(bf16)
    grams = gathered(gram, "dp")
    code_block = total(scattered(partials, "tensor")).astype(bf16)
    end, code_block = lax.optimization_barrier((end, code_block))
    others = gathered(code_block, "dp")
    end_blocks = gathered(end, "tensor")
    mix_block = code_block.astype(f32)
    for k in range(1, groups):
        other = others[k].astype(f32)
        mix_block = mix_block + jnp.concatenate([other[-k * tokens :], other[: -k * tokens]])
    mix_blocks = gathered(mix_block.astype(bf16), "tensor")

    square_flops = 2 * rows * codes * codes
    wide = parts * relay
    mix, ends, products, weights, mix_gram, mix_recv, mix_send, square, sent = run(
        functools.partial(first_kernel, width),
        [
            like((rows, codes)),
            like((rows, wide)),
            like((wide, 2 * relay)),
            like((codes, 2 * wide)),
            like((rows, codes), f32),
            like((rows, wide), f32),
            like((rows, wide), f32),
            like((rows, 1), f32),
            like((rows, wide)),
        ],
        where,
        [mix_blocks, sides, grams, end_blocks],
        scratch=[pltpu.VMEM((codes, codes), bf16)],
        flops=3 * square_flops,
    )
    received = ends
    for turn in range(1, sections):
        last = turn == sections - 1
        shapes = [like((rows, wide)), like((rows, wide))]
        if last:
            shapes += [like((rows, wide), f32)] * 2 + [like((rows, 1), f32), like((rows, wide))]
        moved = move(sent, "pipe", 1)
        results = run(
            functools.partial(forward_kernel, width, turn, last),
            shapes,
            where,
            [(moved, received, ends, mix_recv, mix_send, square, products)],
            flops=square_flops,
        )
        received, sent = results[:2]
    mixed, unscaled, row_scale, returned = results[2:]
    incoming = ends
    for turn in range(1, sections):
        last = turn == sections - 1
        shapes = [like((rows, wide)), like((rows, wide))]
        if last:
            shapes += [like((rows, 1), f32), like((rows, codes))]
            shapes += [like((tokens, head_cols))] * groups
        moved = move(returned, "pipe", -1)
        results = run(
            functools.partial(backward_kernel, width, sections - 1 - turn, last),
            shapes,
            where,
            [
                (
                    moved,
                    incoming,
                    received,
                    mixed,
                    unscaled,
                    row_scale,
                    mix_gram,
                    products,
                    weights,
                    fold,
                )
            ],
            flops=3 * square_flops,
        )
        incoming, returned = results[:2]
    inner, code_grad, *head_blocks = results[2:]

    heads_grad = total(scattered(head_blocks, "dp")).astype(bf16)
    head_sum, *enc_blocks = run(
        head_kernel,
        [like((codes, head_cols))] + [like((cols, model_cols))] * parts,
        where,
        [heads, (code_grad, proj)],
        scratch=[pltpu.VMEM((codes, model_cols), f32)],
        flops=2 * head_cols * codes * (rows + model_cols),
    )
    head_sum, mix, *enc_blocks = lax.optimization_barrier((head_sum, mix, *enc_blocks))
    enc_grad = total(scattered(enc_blocks, "tensor")).astype(bf16)
    proj_grad = dot(head_sum, enc, TN).astype(bf16)

    received_here = received[:, :relay]
    incoming_here = incoming[:, :relay]
    mixed = dot(mix, dec, NN) + dot(received_here, recv, NN)
    normed = mixed * row_scale
    out_rows = (normed * gain).astype(bf16)
    grad_norm = dot(incoming_here, send, NT)
    grad_mixed = (row_scale * (grad_norm * gain - normed * inner)).astype(bf16)
    dec_grad = dot(block(mix, "dp", 1), grad_mixed, TN).astype(bf16)
    gain_grad = jnp.sum(grad_norm * normed, axis=0)
    send_grad = dot(out_rows, incoming_here, TN).astype(bf16)
    recv_grad = dot(received_here, grad_mixed, TN).astype(bf16)
    return (
        sent[None, :tokens, :relay],
        returned[None, :tokens, :relay],
        heads_grad[None],
        proj_grad[None],
        enc_grad[None],
        dec_grad[None],
        gain_grad[None],
        send_grad[None],
        recv_grad[None],
    )


def solution(mesh):
    return jax.shard_map(
        on_device,
        mesh=mesh,
        in_specs=(
            P("pipe", "dp", "tensor"),
            P("pipe", "tensor", "dp"),
            P("pipe", None, "dp"),
            P("pipe", None, "tensor"),
            P("pipe", "tensor"),
            P("pipe", "tensor", None),
            P("pipe", None, "tensor"),
            P("dp", "tensor"),
            P("dp", "tensor"),
        ),
        out_specs=(
            P("pipe", "dp", "tensor"),
            P("pipe", "dp", "tensor"),
            P("pipe", "dp", "tensor"),
            P("pipe", "tensor", "dp"),
            P("pipe", "tensor", "dp"),
            P("pipe", "dp", "tensor"),
            P("pipe", "tensor"),
            P("pipe", "tensor", None),
            P("pipe", None, "tensor"),
        ),
        check_vma=False,
    )
```

```python
import functools

import jax
import jax.numpy as jnp
from jax import lax
from jax.experimental import pallas as pl
from jax.experimental.pallas import tpu as pltpu
from jax.sharding import PartitionSpec as P

epsilon = 1e-05
f32 = jnp.float32
bf16 = jnp.bfloat16
NN = ((1,), (0,))
NT = ((1,), (1,))
TN = ((0,), (0,))


def swap(shard, axis, by):
    return lax.ppermute(shard, axis, [(i, i ^ by) for i in range(lax.axis_size(axis))])


def move(shard, axis, by):
    devices = lax.axis_size(axis)
    pairs = [(i, i + by) for i in range(devices) if 0 <= i + by < devices]
    return lax.ppermute(shard, axis, pairs)


def gathered(shard, axis):
    return [shard] + [swap(shard, axis, k) for k in range(1, lax.axis_size(axis))]


def scattered(blocks, axis):
    return [blocks[0]] + [swap(blocks[k], axis, k) for k in range(1, len(blocks))]


def group_sum(rows, axis):
    groups = lax.axis_size(axis)
    size = rows.shape[0] // groups
    step = groups // 2
    while step:
        other = swap(rows, axis, step)
        other = [other[(k ^ step) * size : ((k ^ step) + 1) * size] for k in range(groups)]
        rows = (rows.astype(f32) + jnp.concatenate(other).astype(f32)).astype(bf16)
        step //= 2
    return rows


def halved_sum(kept, given, axis, size):
    step = 1
    while True:
        kept = (kept.astype(f32) + swap(given, axis, step).astype(f32)).astype(bf16)
        step *= 2
        if step == lax.axis_size(axis):
            return kept
        blocks = [kept[at : at + size] for at in range(0, kept.shape[0], size)]
        kept, given = jnp.concatenate(blocks[::2]), jnp.concatenate(blocks[1::2])


def total(blocks):
    result = blocks[0].astype(f32)
    for part in blocks[1:]:
        result = result + part.astype(f32)
    return result


def block(array, axis, dim):
    size = array.shape[dim] // lax.axis_size(axis)
    return lax.dynamic_slice_in_dim(array, lax.axis_index(axis) * size, size, dim)


def dot(left, right, over):
    return lax.dot_general(left, right, (over, ((), ())), preferred_element_type=f32)


def run(kernel, results, where, groups_of_args, scratch=(), flops=0):
    counts = [len(group) for group in groups_of_args]
    flat = [array for group in groups_of_args for array in group]
    out_count = len(results)

    def body(where_ref, *refs):
        ins, at = [], 0
        for count in counts:
            ins.append(refs[at : at + count])
            at += count
        kernel(where_ref, ins, refs[at : at + out_count], refs[at + out_count :])

    size = sum(a.size * a.dtype.itemsize for a in list(flat) + list(results)) if flops else 0
    return pl.pallas_call(
        body,
        out_shape=[jax.ShapeDtypeStruct(r.shape, r.dtype) for r in results],
        in_specs=[pl.BlockSpec(memory_space=pltpu.SMEM)]
        + [pl.BlockSpec(memory_space=pltpu.VMEM)] * len(flat),
        out_specs=[pl.BlockSpec(memory_space=pltpu.VMEM)] * out_count,
        scratch_shapes=list(scratch),
        compiler_params=pltpu.CompilerParams(vmem_limit_bytes=56 << 20),
        cost_estimate=pl.CostEstimate(flops=flops, bytes_accessed=size, transcendentals=0),
    )(where, *flat)


def like(shape, dtype=bf16):
    return jax.ShapeDtypeStruct(shape, dtype)


def by_rows(rows, step):
    chunk = min(rows, 512)
    if rows == chunk:
        step(slice(0, rows))
        return

    @pl.loop(0, rows // chunk)
    def _(index):
        step(pl.ds(pl.multiple_of(index * chunk, chunk), chunk))


def gram_kernel(where, ins, outs, scratch):
    ((dec, recv, send, gain),) = ins
    (whole,) = scratch
    codes, relay = dec.shape[0], recv.shape[0]
    cols = codes // len(outs)
    wide = 2 * relay
    head = cols * codes // wide
    whole[...] = dot(dec[...], dec[...], NT)
    for k, out in enumerate(outs):
        rows = pl.ds(pl.multiple_of((where[0] ^ k) * cols, cols), cols)
        for j in range(codes // wide):
            piece = whole[rows, j * wide : (j + 1) * wide]
            out[j * cols : (j + 1) * cols, :] = piece.astype(bf16)
    for ref, rows in ((dec, slice(head, head + codes)), (recv, slice(head + codes, None))):
        values = ref[...]
        gained = (values.astype(f32) * gain[...]).astype(bf16)
        plain = dot(values, recv[...], NT).astype(bf16)
        scaled = dot(gained, send[...], NN).astype(bf16)
        for out in outs:
            out[rows, :relay] = plain
            out[rows, relay:] = scaled


def setup_kernel(where, ins, outs, scratch):
    packs, ends = ins
    payload, products, weights = outs
    parts = len(packs)
    wide = products.shape[1]
    relay = wide // 2
    codes = weights.shape[0]
    cols = codes // parts
    head = cols * codes // wide
    for j in range(codes // wide):
        rows = slice(j * cols, (j + 1) * cols)
        gram = packs[0][rows, :].astype(f32)
        for pack in packs[1:]:
            gram = gram + pack[rows, :].astype(f32)
        gram = gram.astype(bf16)
        payload[2 * j * cols : (2 * j + 1) * cols, :] = gram[:, :relay]
        payload[(2 * j + 1) * cols : (2 * j + 2) * cols, :] = gram[:, relay:]
    start = 2 * head
    for end in ends:
        payload[start : start + end.shape[0], :] = end[...]
        start += end.shape[0]
    for k, pack in enumerate(packs):
        here = slice(k * relay, (k + 1) * relay)
        products[here, :] = pack[head + codes :, :]
        weights[:, here] = pack[head : head + codes, :relay]
        there = slice((parts + k) * relay, (parts + k + 1) * relay)
        weights[:, there] = pack[head : head + codes, relay:]


def fold_kernel(where, ins, outs, scratch):
    ((proj, enc),) = ins
    outs[0][...] = dot(proj[...], enc[...], NT).astype(bf16)


def partial_kernel(where, ins, outs, scratch):
    heads, (fold,) = ins
    (whole,) = scratch
    tokens = heads[0].shape[0]
    cols = outs[0].shape[1]
    parts = len(outs)
    together = 4 if len(heads) % 4 == 0 else 1
    for first in range(0, len(heads), together):
        rows = slice(first * tokens, (first + together) * tokens)
        values = jnp.concatenate([h[...] for h in heads[first : first + together]])
        whole[...] = dot(values, fold[...], NN)
        for k in range(parts):
            at = (where[0] ^ k) * cols
            outs[k][rows, :] = whole[:, pl.ds(pl.multiple_of(at, cols), cols)].astype(bf16)


def forward(received, code_mix, code_send, square, products, width):
    relay = products.shape[1] // 2
    count = received.shape[1] // relay
    mixed, unscaled = [], []
    for k in range(count):
        cols = slice(k * relay, (k + 1) * relay)
        both = dot(received[:, cols], products[cols, :], NN)
        mixed.append(code_mix[:, cols] + both[:, :relay])
        unscaled.append(code_send[:, cols] + both[:, relay:])
    mixed = jnp.concatenate(mixed, axis=1)
    unscaled = jnp.concatenate(unscaled, axis=1)
    totals = square + jnp.sum(received.astype(f32) * (code_mix + mixed), axis=1, keepdims=True)
    row_scale = lax.rsqrt(jnp.maximum(totals, 0.0) / width + epsilon)
    return mixed, unscaled, row_scale


def backward(incoming, mixed, unscaled, row_scale, products, width):
    relay = products.shape[1] // 2
    count = incoming.shape[1] // relay
    inner = row_scale * jnp.sum(incoming.astype(f32) * unscaled, axis=1, keepdims=True) / width
    returned = []
    for k in range(count):
        cols = slice(k * relay, (k + 1) * relay)
        back = dot(incoming[:, cols], products[cols, relay:], NT)
        returned.append(row_scale * (back - row_scale * inner * mixed[:, cols]))
    return inner, jnp.concatenate(returned, axis=1).astype(bf16)


def first_kernel(width, where, ins, outs, scratch):
    mix_blocks, payloads, (products, weights) = ins
    mix, ends, mix_gram, mix_recv, mix_send, square, sent = outs
    (gram,) = scratch
    codes = mix.shape[1]
    relay = products.shape[1] // 2
    parts = len(mix_blocks)
    cols = codes // parts
    for k in range(parts):
        at = pl.multiple_of((where[0] ^ k) * cols, cols)
        mix[:, pl.ds(at, cols)] = mix_blocks[k][...]
        ends[:, k * relay : (k + 1) * relay] = payloads[k][cols * codes // relay :, :]
        for j in range(codes // relay):
            piece = payloads[k][j * cols : (j + 1) * cols, :]
            gram[pl.ds(at, cols), j * relay : (j + 1) * relay] = piece

    def step(at):
        codes_here = mix[at, :]
        in_gram = dot(codes_here, gram[...], NN)
        sums = jnp.sum(in_gram * codes_here.astype(f32), axis=1, keepdims=True)
        in_relay = dot(codes_here, weights[...], NN)
        in_recv = in_relay[:, : parts * relay]
        in_send = in_relay[:, parts * relay :]
        mix_gram[at, :] = in_gram
        mix_recv[at, :] = in_recv
        mix_send[at, :] = in_send
        square[at, :] = sums
        mixed, unscaled, row_scale = forward(
            ends[at, :], in_recv, in_send, sums, products[...], width
        )
        sent[at, :] = (row_scale * unscaled).astype(bf16)

    by_rows(mix.shape[0], step)


def forward_kernel(width, turn, last, where, ins, outs, scratch):
    ((moved, received, ends, mix_recv, mix_send, square, products),) = ins
    live = where[2] == turn

    def step(at):
        values = jnp.where(live, moved[at, :], received[at, :])
        mixed, unscaled, row_scale = forward(
            values, mix_recv[at, :], mix_send[at, :], square[at, :], products[...], width
        )
        outs[0][at, :] = values
        outs[1][at, :] = (row_scale * unscaled).astype(bf16)
        if last:
            inner, returned = backward(
                ends[at, :], mixed, unscaled, row_scale, products[...], width
            )
            outs[2][at, :] = mixed
            outs[3][at, :] = unscaled
            outs[4][at, :] = row_scale
            outs[5][at, :] = returned

    by_rows(moved.shape[0], step)


def backward_kernel(width, live_section, last, tokens, where, ins, outs, scratch):
    (moved, incoming, received, mixed, unscaled, row_scale, mix_gram, products, weights, fold), = ins
    live = where[2] == live_section
    half = weights.shape[1] // 2

    def step(at):
        values = jnp.where(live, moved[at, :], incoming[at, :])
        scale = row_scale[at, :]
        inner, returned = backward(
            values, mixed[at, :], unscaled[at, :], scale, products[...], width
        )
        outs[0][at, :] = values
        outs[1][at, :] = returned
        if last:
            outs[2][at, :] = inner
            in_mixed = mix_gram[at, :] + dot(received[at, :], weights[:, :half], NT)
            back = dot(values, weights[:, half:], NT)
            outs[3][at, :] = (scale * (back - scale * inner * in_mixed)).astype(bf16)

    by_rows(moved.shape[0], step)
    if last:
        kept, given = outs[4:]
        groups = 2 * kept.shape[0] // tokens
        for k in range(groups):
            rows = slice(k * tokens, (k + 1) * tokens)
            there = slice(k // 2 * tokens, (k // 2 + 1) * tokens)
            term = dot(outs[3][rows, :], fold[...], NT).astype(bf16)
            (given if k % 2 else kept)[there, :] = term


def head_kernel(where, ins, outs, scratch):
    heads, (code_grad, proj) = ins
    head_sum, enc_blocks = outs[0], outs[1:]
    (whole,) = scratch
    tokens = heads[0].shape[0]
    together = 4 if len(heads) % 4 == 0 else 1
    sums = None
    for first in range(0, len(heads), together):
        rows = slice(first * tokens, (first + together) * tokens)
        values = jnp.concatenate([h[...] for h in heads[first : first + together]])
        term = dot(code_grad[rows, :], values, TN)
        sums = term if sums is None else sums + term
    head_sum[...] = sums.astype(bf16)
    whole[...] = dot(head_sum[...], proj[...], NN)
    size = enc_blocks[0].shape[0]
    for k, out in enumerate(enc_blocks):
        at = (where[0] ^ k) * size
        out[...] = whole[pl.ds(pl.multiple_of(at, size), size), :].astype(bf16)


def proj_kernel(where, ins, outs, scratch):
    ((head_sum, enc),) = ins
    outs[0][...] = dot(head_sum[...], enc[...], TN).astype(bf16)


def feature_kernel(where, ins, outs, scratch):
    (mix, mix_cols, received, incoming, row_scale, inner, dec, recv, send, gain), = ins
    sums = scratch
    relay = recv.shape[0]
    for ref in sums:
        ref[...] = jnp.zeros_like(ref)

    def step(at):
        received_here = received[at, :relay]
        incoming_here = incoming[at, :relay]
        scale = row_scale[at, :]
        mixed = dot(mix[at, :], dec[...], NN) + dot(received_here, recv[...], NN)
        normed = mixed * scale
        out_rows = (normed * gain[...]).astype(bf16)
        grad_norm = dot(incoming_here, send[...], NT)
        grad_mixed = scale * (grad_norm * gain[...] - normed * inner[at, :])
        grad_mixed = grad_mixed.astype(bf16)
        sums[0][...] += dot(mix_cols[at, :], grad_mixed, TN)
        sums[1][...] += jnp.sum(grad_norm * normed, axis=0, keepdims=True)
        sums[2][...] += dot(out_rows, incoming_here, TN)
        sums[3][...] += dot(received_here, grad_mixed, TN)

    by_rows(mix.shape[0], step)
    for out, ref in zip(outs, sums):
        out[...] = ref[...].astype(out.dtype)


def on_device(
    heads_out,
    out_proj,
    encoder,
    decoder,
    norm_gain,
    send_encoder,
    recv_decoder,
    input_code,
    code_cotangent,
):
    sections = lax.axis_size("pipe")
    section = lax.axis_index("pipe")
    groups = lax.axis_size("dp")
    parts = lax.axis_size("tensor")
    width = norm_gain.shape[1] * parts
    proj = out_proj[0]
    enc = encoder[0]
    dec = decoder[0]
    gain = norm_gain
    send = send_encoder[0]
    recv = recv_decoder[0]
    tokens, relay = input_code.shape
    codes, features = dec.shape
    cols = codes // parts
    rows = tokens * groups
    head_cols, model_cols = proj.shape
    where = jnp.stack([lax.axis_index("tensor"), lax.axis_index("dp"), section]).astype(jnp.int32)

    heads = gathered(heads_out[0], "dp")
    end = jnp.where(section == 0, input_code, code_cotangent)
    ends = gathered(end, "dp")
    packs = run(
        gram_kernel,
        [like((cols * codes // (2 * relay) + codes + relay, 2 * relay))] * parts,
        where,
        [(dec, recv, send, gain)],
        scratch=[pltpu.VMEM((codes, codes), f32)],
    )
    (fold,) = run(fold_kernel, [like((head_cols, codes))], where, [(proj, enc)])
    fold, _ = lax.optimization_barrier((fold, packs[0]))
    packs = scattered(packs, "tensor")

    partials = run(
        partial_kernel,
        [like((rows, cols))] * parts,
        where,
        [heads, (fold,)],
        scratch=[pltpu.VMEM((min(groups, 4) * tokens, codes), f32)],
        flops=2 * rows * head_cols * codes,
    )
    wide = parts * relay
    payload, products, weights = run(
        setup_kernel,
        [
            like((cols * codes // relay + rows, relay)),
            like((wide, 2 * relay)),
            like((codes, 2 * wide)),
        ],
        where,
        [packs, ends],
    )
    code_block = total(scattered(partials, "tensor")).astype(bf16)
    payload, code_block = lax.optimization_barrier((payload, code_block))
    payloads = gathered(payload, "tensor")
    mix_blocks = gathered(group_sum(code_block, "dp"), "tensor")

    square_flops = 2 * rows * codes * codes
    mix, ends, mix_gram, mix_recv, mix_send, square, sent = run(
        functools.partial(first_kernel, width),
        [
            like((rows, codes)),
            like((rows, wide)),
            like((rows, codes), f32),
            like((rows, wide), f32),
            like((rows, wide), f32),
            like((rows, 1), f32),
            like((rows, wide)),
        ],
        where,
        [mix_blocks, payloads, (products, weights)],
        scratch=[pltpu.VMEM((codes, codes), bf16)],
        flops=3 * square_flops,
    )
    received = ends
    for turn in range(1, sections):
        last = turn == sections - 1
        shapes = [like((rows, wide)), like((rows, wide))]
        if last:
            shapes += [like((rows, wide), f32)] * 2 + [like((rows, 1), f32), like((rows, wide))]
        moved = move(sent, "pipe", 1)
        results = run(
            functools.partial(forward_kernel, width, turn, last),
            shapes,
            where,
            [(moved, received, ends, mix_recv, mix_send, square, products)],
            flops=square_flops,
        )
        received, sent = results[:2]
    mixed, unscaled, row_scale, returned = results[2:]
    incoming = ends
    for turn in range(1, sections):
        last = turn == sections - 1
        shapes = [like((rows, wide)), like((rows, wide))]
        if last:
            shapes += [like((rows, 1), f32), like((rows, codes))]
            shapes += [like((rows // 2, head_cols))] * 2
        moved = move(returned, "pipe", -1)
        results = run(
            functools.partial(backward_kernel, width, sections - 1 - turn, last, tokens),
            shapes,
            where,
            [
                (
                    moved,
                    incoming,
                    received,
                    mixed,
                    unscaled,
                    row_scale,
                    mix_gram,
                    products,
                    weights,
                    fold,
                )
            ],
            flops=3 * square_flops,
        )
        incoming, returned = results[:2]
    inner, code_grad, kept, given = results[2:]

    heads_grad = halved_sum(kept, given, "dp", tokens)
    head_sum, *enc_blocks = run(
        head_kernel,
        [like((codes, head_cols))] + [like((cols, model_cols))] * parts,
        where,
        [heads, (code_grad, proj)],
        scratch=[pltpu.VMEM((codes, model_cols), f32)],
        flops=2 * head_cols * codes * (rows + model_cols),
    )
    head_sum, mix, *enc_blocks = lax.optimization_barrier((head_sum, mix, *enc_blocks))
    enc_grad = total(scattered(enc_blocks, "tensor")).astype(bf16)
    (proj_grad,) = run(proj_kernel, [like((head_cols, model_cols))], where, [(head_sum, enc)])
    shapes = [(codes // groups, features), (1, features), (features, relay), (relay, features)]
    dec_grad, gain_grad, send_grad, recv_grad = run(
        feature_kernel,
        [like(shape, f32 if k == 1 else bf16) for k, shape in enumerate(shapes)],
        where,
        [
            (
                mix,
                block(mix, "dp", 1),
                received,
                incoming,
                row_scale,
                inner,
                dec,
                recv,
                send,
                gain,
            )
        ],
        scratch=[pltpu.VMEM(shape, f32) for shape in shapes],
    )
    sent, returned, enc_grad = lax.optimization_barrier((sent, returned, enc_grad))
    return (
        sent[None, :tokens, :relay],
        returned[None, :tokens, :relay],
        heads_grad[None],
        proj_grad[None],
        enc_grad[None],
        dec_grad[None],
        gain_grad,
        send_grad[None],
        recv_grad[None],
    )


def solution(mesh):
    return jax.shard_map(
        on_device,
        mesh=mesh,
        in_specs=(
            P("pipe", "dp", "tensor"),
            P("pipe", "tensor", "dp"),
            P("pipe", None, "dp"),
            P("pipe", None, "tensor"),
            P("pipe", "tensor"),
            P("pipe", "tensor", None),
            P("pipe", None, "tensor"),
            P("dp", "tensor"),
            P("dp", "tensor"),
        ),
        out_specs=(
            P("pipe", "dp", "tensor"),
            P("pipe", "dp", "tensor"),
            P("pipe", "dp", "tensor"),
            P("pipe", "tensor", "dp"),
            P("pipe", "tensor", "dp"),
            P("pipe", "dp", "tensor"),
            P("pipe", "tensor"),
            P("pipe", "tensor", None),
            P("pipe", None, "tensor"),
        ),
        check_vma=False,
    )
```

```python
import functools

import jax
import jax.numpy as jnp
from jax import lax
from jax.experimental import pallas as pl
from jax.experimental.pallas import tpu as pltpu
from jax.sharding import PartitionSpec as P

epsilon = 1e-05
f32 = jnp.float32
bf16 = jnp.bfloat16
NN = ((1,), (0,))
NT = ((1,), (1,))
TN = ((0,), (0,))


def swap(shard, axis, by):
    return lax.ppermute(shard, axis, [(i, i ^ by) for i in range(lax.axis_size(axis))])


def move(shard, axis, by):
    devices = lax.axis_size(axis)
    pairs = [(i, i + by) for i in range(devices) if 0 <= i + by < devices]
    return lax.ppermute(shard, axis, pairs)


def gathered(shard, axis):
    return [shard] + [swap(shard, axis, k) for k in range(1, lax.axis_size(axis))]


def scattered(blocks, axis):
    return [blocks[0]] + [swap(blocks[k], axis, k) for k in range(1, len(blocks))]


def group_sum(rows, axis):
    groups = lax.axis_size(axis)
    size = rows.shape[0] // groups
    step = groups // 2
    while step:
        other = swap(rows, axis, step)
        other = [other[(k ^ step) * size : ((k ^ step) + 1) * size] for k in range(groups)]
        rows = (rows.astype(f32) + jnp.concatenate(other).astype(f32)).astype(bf16)
        step //= 2
    return rows


def halved_sum(kept, given, after, axis, size):
    step = 1
    while True:
        kept = (kept.astype(f32) + swap(given, axis, step).astype(f32)).astype(bf16)
        if step == 1:
            kept, after = lax.optimization_barrier((kept, after))
        step *= 2
        if step == lax.axis_size(axis):
            return kept, after
        blocks = [kept[at : at + size] for at in range(0, kept.shape[0], size)]
        kept, given = jnp.concatenate(blocks[::2]), jnp.concatenate(blocks[1::2])


def total(blocks):
    result = blocks[0].astype(f32)
    for part in blocks[1:]:
        result = result + part.astype(f32)
    return result


def block(array, axis, dim):
    size = array.shape[dim] // lax.axis_size(axis)
    return lax.dynamic_slice_in_dim(array, lax.axis_index(axis) * size, size, dim)


def dot(left, right, over):
    return lax.dot_general(left, right, (over, ((), ())), preferred_element_type=f32)


def run(kernel, results, where, groups_of_args, scratch=(), flops=0):
    counts = [len(group) for group in groups_of_args]
    flat = [array for group in groups_of_args for array in group]
    out_count = len(results)

    def body(where_ref, *refs):
        ins, at = [], 0
        for count in counts:
            ins.append(refs[at : at + count])
            at += count
        kernel(where_ref, ins, refs[at : at + out_count], refs[at + out_count :])

    size = sum(a.size * a.dtype.itemsize for a in list(flat) + list(results))
    return pl.pallas_call(
        body,
        out_shape=[jax.ShapeDtypeStruct(r.shape, r.dtype) for r in results],
        in_specs=[pl.BlockSpec(memory_space=pltpu.SMEM)]
        + [pl.BlockSpec(memory_space=pltpu.VMEM)] * len(flat),
        out_specs=[pl.BlockSpec(memory_space=pltpu.VMEM)] * out_count,
        scratch_shapes=list(scratch),
        compiler_params=pltpu.CompilerParams(vmem_limit_bytes=size + (12 << 20)),
        cost_estimate=pl.CostEstimate(flops=flops, bytes_accessed=size if flops else 0, transcendentals=0),
    )(where, *flat)


def like(shape, dtype=bf16):
    return jax.ShapeDtypeStruct(shape, dtype)


def by_rows(rows, step):
    chunk = min(rows, 512)
    if rows == chunk:
        step(slice(0, rows))
        return

    @pl.loop(0, rows // chunk)
    def _(index):
        step(pl.ds(pl.multiple_of(index * chunk, chunk), chunk))


def gram_kernel(where, ins, outs, scratch):
    ((dec, recv, send, gain),) = ins
    (whole,) = scratch
    codes, relay = dec.shape[0], recv.shape[0]
    cols = codes // len(outs)
    wide = 2 * relay
    head = cols * codes // wide
    whole[...] = dot(dec[...], dec[...], NT)
    for k, out in enumerate(outs):
        rows = pl.ds(pl.multiple_of((where[0] ^ k) * cols, cols), cols)
        for j in range(codes // wide):
            piece = whole[rows, j * wide : (j + 1) * wide]
            out[j * cols : (j + 1) * cols, :] = piece.astype(bf16)
    for ref, rows in ((dec, slice(head, head + codes)), (recv, slice(head + codes, None))):
        values = ref[...]
        gained = (values.astype(f32) * gain[...]).astype(bf16)
        plain = dot(values, recv[...], NT).astype(bf16)
        scaled = dot(gained, send[...], NN).astype(bf16)
        for out in outs:
            out[rows, :relay] = plain
            out[rows, relay:] = scaled


def setup_kernel(where, ins, outs, scratch):
    packs, ends = ins
    payload, products, weights = outs
    parts = len(packs)
    wide = products.shape[1]
    relay = wide // 2
    codes = weights.shape[0]
    cols = codes // parts
    head = cols * codes // wide
    for j in range(codes // wide):
        rows = slice(j * cols, (j + 1) * cols)
        gram = packs[0][rows, :].astype(f32)
        for pack in packs[1:]:
            gram = gram + pack[rows, :].astype(f32)
        gram = gram.astype(bf16)
        payload[2 * j * cols : (2 * j + 1) * cols, :] = gram[:, :relay]
        payload[(2 * j + 1) * cols : (2 * j + 2) * cols, :] = gram[:, relay:]
    start = 2 * head
    for end in ends:
        payload[start : start + end.shape[0], :] = end[...]
        start += end.shape[0]
    for k, pack in enumerate(packs):
        here = slice(k * relay, (k + 1) * relay)
        products[here, :] = pack[head + codes :, :]
        weights[:, here] = pack[head : head + codes, :relay]
        there = slice((parts + k) * relay, (parts + k + 1) * relay)
        weights[:, there] = pack[head : head + codes, relay:]


def fold_kernel(where, ins, outs, scratch):
    ((proj, enc),) = ins
    outs[0][...] = dot(proj[...], enc[...], NT).astype(bf16)


def partial_kernel(where, ins, outs, scratch):
    heads, (fold,) = ins
    (whole,) = scratch
    tokens = heads[0].shape[0]
    cols = outs[0].shape[1]
    parts = len(outs)
    together = 4 if len(heads) % 4 == 0 else 1
    for first in range(0, len(heads), together):
        rows = slice(first * tokens, (first + together) * tokens)
        values = jnp.concatenate([h[...] for h in heads[first : first + together]])
        whole[...] = dot(values, fold[...], NN)
        for k in range(parts):
            at = (where[0] ^ k) * cols
            outs[k][rows, :] = whole[:, pl.ds(pl.multiple_of(at, cols), cols)].astype(bf16)


def forward(received, code_mix, code_send, square, products, width):
    relay = products.shape[1] // 2
    count = received.shape[1] // relay
    mixed, unscaled = [], []
    for k in range(count):
        cols = slice(k * relay, (k + 1) * relay)
        both = dot(received[:, cols], products[cols, :], NN)
        mixed.append(code_mix[:, cols] + both[:, :relay])
        unscaled.append(code_send[:, cols] + both[:, relay:])
    mixed = jnp.concatenate(mixed, axis=1)
    unscaled = jnp.concatenate(unscaled, axis=1)
    totals = square + jnp.sum(received.astype(f32) * (code_mix + mixed), axis=1, keepdims=True)
    row_scale = lax.rsqrt(jnp.maximum(totals, 0.0) / width + epsilon)
    return mixed, unscaled, row_scale


def backward(incoming, mixed, unscaled, row_scale, products, width):
    relay = products.shape[1] // 2
    count = incoming.shape[1] // relay
    inner = row_scale * jnp.sum(incoming.astype(f32) * unscaled, axis=1, keepdims=True) / width
    returned = []
    for k in range(count):
        cols = slice(k * relay, (k + 1) * relay)
        back = dot(incoming[:, cols], products[cols, relay:], NT)
        returned.append(row_scale * (back - row_scale * inner * mixed[:, cols]))
    return inner, jnp.concatenate(returned, axis=1).astype(bf16)


def first_kernel(width, where, ins, outs, scratch):
    mix_blocks, payloads, (products, weights) = ins
    mix, ends, mix_gram, mix_recv, mix_send, square, sent = outs
    (gram,) = scratch
    codes = mix.shape[1]
    relay = products.shape[1] // 2
    parts = len(mix_blocks)
    cols = codes // parts
    for k in range(parts):
        at = pl.multiple_of((where[0] ^ k) * cols, cols)
        mix[:, pl.ds(at, cols)] = mix_blocks[k][...]
        ends[:, k * relay : (k + 1) * relay] = payloads[k][cols * codes // relay :, :]
        for j in range(codes // relay):
            piece = payloads[k][j * cols : (j + 1) * cols, :]
            gram[pl.ds(at, cols), j * relay : (j + 1) * relay] = piece

    def step(at):
        codes_here = mix[at, :]
        in_gram = dot(codes_here, gram[...], NN)
        sums = jnp.sum(in_gram * codes_here.astype(f32), axis=1, keepdims=True)
        in_relay = dot(codes_here, weights[...], NN)
        in_recv = in_relay[:, : parts * relay]
        in_send = in_relay[:, parts * relay :]
        mix_gram[at, :] = in_gram
        mix_recv[at, :] = in_recv
        mix_send[at, :] = in_send
        square[at, :] = sums
        mixed, unscaled, row_scale = forward(
            ends[at, :], in_recv, in_send, sums, products[...], width
        )
        sent[at, :] = (row_scale * unscaled).astype(bf16)

    by_rows(mix.shape[0], step)


def forward_kernel(width, turn, last, where, ins, outs, scratch):
    ((moved, received, ends, mix_recv, mix_send, square, products),) = ins
    live = where[2] == turn

    def step(at):
        values = jnp.where(live, moved[at, :], received[at, :])
        mixed, unscaled, row_scale = forward(
            values, mix_recv[at, :], mix_send[at, :], square[at, :], products[...], width
        )
        outs[0][at, :] = values
        outs[1][at, :] = (row_scale * unscaled).astype(bf16)
        if last:
            inner, returned = backward(
                ends[at, :], mixed, unscaled, row_scale, products[...], width
            )
            outs[2][at, :] = mixed
            outs[3][at, :] = unscaled
            outs[4][at, :] = row_scale
            outs[5][at, :] = returned

    by_rows(moved.shape[0], step)


def backward_kernel(width, live_section, last, tokens, where, ins, outs, scratch):
    (moved, incoming, received, mixed, unscaled, row_scale, mix_gram, products, weights, fold), = ins
    live = where[2] == live_section
    half = weights.shape[1] // 2

    def step(at):
        values = jnp.where(live, moved[at, :], incoming[at, :])
        scale = row_scale[at, :]
        inner, returned = backward(
            values, mixed[at, :], unscaled[at, :], scale, products[...], width
        )
        outs[0][at, :] = values
        outs[1][at, :] = returned
        if last:
            outs[2][at, :] = inner
            in_mixed = mix_gram[at, :] + dot(received[at, :], weights[:, :half], NT)
            back = dot(values, weights[:, half:], NT)
            outs[3][at, :] = (scale * (back - scale * inner * in_mixed)).astype(bf16)

    by_rows(moved.shape[0], step)
    if last:
        kept, given = outs[4:]
        groups = 2 * kept.shape[0] // tokens
        for k in range(groups):
            rows = slice(k * tokens, (k + 1) * tokens)
            there = slice(k // 2 * tokens, (k // 2 + 1) * tokens)
            term = dot(outs[3][rows, :], fold[...], NT).astype(bf16)
            (given if k % 2 else kept)[there, :] = term


def head_kernel(where, ins, outs, scratch):
    heads, (code_grad, proj) = ins
    head_sum, enc_blocks = outs[0], outs[1:]
    (whole,) = scratch
    tokens = heads[0].shape[0]
    together = 4 if len(heads) % 4 == 0 else 1
    sums = None
    for first in range(0, len(heads), together):
        rows = slice(first * tokens, (first + together) * tokens)
        values = jnp.concatenate([h[...] for h in heads[first : first + together]])
        term = dot(code_grad[rows, :], values, TN)
        sums = term if sums is None else sums + term
    head_sum[...] = sums.astype(bf16)
    whole[...] = dot(head_sum[...], proj[...], NN)
    size = enc_blocks[0].shape[0]
    for k, out in enumerate(enc_blocks):
        at = (where[0] ^ k) * size
        out[...] = whole[pl.ds(pl.multiple_of(at, size), size), :].astype(bf16)


def proj_kernel(where, ins, outs, scratch):
    ((head_sum, enc),) = ins
    outs[0][...] = dot(head_sum[...], enc[...], TN).astype(bf16)


def feature_kernel(where, ins, outs, scratch):
    (mix, mix_cols, received, incoming, row_scale, inner, dec, recv, send, gain), = ins
    sums = scratch
    relay = recv.shape[0]
    for ref in sums:
        ref[...] = jnp.zeros_like(ref)

    def step(at):
        received_here = received[at, :relay]
        incoming_here = incoming[at, :relay]
        scale = row_scale[at, :]
        mixed = dot(mix[at, :], dec[...], NN) + dot(received_here, recv[...], NN)
        normed = mixed * scale
        out_rows = (normed * gain[...]).astype(bf16)
        grad_norm = dot(incoming_here, send[...], NT)
        grad_mixed = scale * (grad_norm * gain[...] - normed * inner[at, :])
        grad_mixed = grad_mixed.astype(bf16)
        sums[0][...] += dot(mix_cols[at, :], grad_mixed, TN)
        sums[1][...] += jnp.sum(grad_norm * normed, axis=0, keepdims=True)
        sums[2][...] += dot(out_rows, incoming_here, TN)
        sums[3][...] += dot(received_here, grad_mixed, TN)

    by_rows(mix.shape[0], step)
    for out, ref in zip(outs, sums):
        out[...] = ref[...].astype(out.dtype)


def on_device(
    heads_out,
    out_proj,
    encoder,
    decoder,
    norm_gain,
    send_encoder,
    recv_decoder,
    input_code,
    code_cotangent,
):
    sections = lax.axis_size("pipe")
    section = lax.axis_index("pipe")
    groups = lax.axis_size("dp")
    parts = lax.axis_size("tensor")
    width = norm_gain.shape[1] * parts
    proj = out_proj[0]
    enc = encoder[0]
    dec = decoder[0]
    gain = norm_gain
    send = send_encoder[0]
    recv = recv_decoder[0]
    tokens, relay = input_code.shape
    codes, features = dec.shape
    cols = codes // parts
    rows = tokens * groups
    head_cols, model_cols = proj.shape
    where = jnp.stack([lax.axis_index("tensor"), lax.axis_index("dp"), section]).astype(jnp.int32)

    heads = gathered(heads_out[0], "dp")
    end = jnp.where(section == 0, input_code, code_cotangent)
    ends = gathered(end, "dp")
    packs = run(
        gram_kernel,
        [like((cols * codes // (2 * relay) + codes + relay, 2 * relay))] * parts,
        where,
        [(dec, recv, send, gain)],
        scratch=[pltpu.VMEM((codes, codes), f32)],
    )
    enc, *_ = lax.optimization_barrier((enc, *ends))
    (fold,) = run(fold_kernel, [like((head_cols, codes))], where, [(proj, enc)])
    fold, _ = lax.optimization_barrier((fold, packs[0]))
    packs = scattered(packs, "tensor")

    partials = run(
        partial_kernel,
        [like((rows, cols))] * parts,
        where,
        [heads, (fold,)],
        scratch=[pltpu.VMEM((min(groups, 4) * tokens, codes), f32)],
        flops=2 * rows * head_cols * codes,
    )
    wide = parts * relay
    payload, products, weights = run(
        setup_kernel,
        [
            like((cols * codes // relay + rows, relay)),
            like((wide, 2 * relay)),
            like((codes, 2 * wide)),
        ],
        where,
        [packs, ends],
    )
    arrived = scattered(partials, "tensor")
    arrived, *_ = lax.optimization_barrier((arrived, *packs))
    code_block = total(arrived).astype(bf16)
    payloads = gathered(payload, "tensor")
    mix_block = group_sum(code_block, "dp")
    mix_block, *_ = lax.optimization_barrier((mix_block, *payloads))
    mix_blocks = gathered(mix_block, "tensor")

    square_flops = 2 * rows * codes * codes
    mix, ends, mix_gram, mix_recv, mix_send, square, sent = run(
        functools.partial(first_kernel, width),
        [
            like((rows, codes)),
            like((rows, wide)),
            like((rows, codes), f32),
            like((rows, wide), f32),
            like((rows, wide), f32),
            like((rows, 1), f32),
            like((rows, wide)),
        ],
        where,
        [mix_blocks, payloads, (products, weights)],
        scratch=[pltpu.VMEM((codes, codes), bf16)],
        flops=3 * square_flops,
    )
    received = ends
    for turn in range(1, sections):
        last = turn == sections - 1
        shapes = [like((rows, wide)), like((rows, wide))]
        if last:
            shapes += [like((rows, wide), f32)] * 2 + [like((rows, 1), f32), like((rows, wide))]
        moved = move(sent, "pipe", 1)
        results = run(
            functools.partial(forward_kernel, width, turn, last),
            shapes,
            where,
            [(moved, received, ends, mix_recv, mix_send, square, products)],
            flops=square_flops,
        )
        received, sent = results[:2]
    mixed, unscaled, row_scale, returned = results[2:]
    incoming = ends
    for turn in range(1, sections):
        last = turn == sections - 1
        shapes = [like((rows, wide)), like((rows, wide))]
        if last:
            shapes += [like((rows, 1), f32), like((rows, codes))]
            shapes += [like((rows // 2, head_cols))] * 2
        moved = move(returned, "pipe", -1)
        results = run(
            functools.partial(backward_kernel, width, sections - 1 - turn, last, tokens),
            shapes,
            where,
            [
                (
                    moved,
                    incoming,
                    received,
                    mixed,
                    unscaled,
                    row_scale,
                    mix_gram,
                    products,
                    weights,
                    fold,
                )
            ],
            flops=3 * square_flops,
        )
        incoming, returned = results[:2]
    inner, code_grad, kept, given = results[2:]

    heads_grad, row_scale = halved_sum(kept, given, row_scale, "dp", tokens)
    head_sum, *enc_blocks = run(
        head_kernel,
        [like((codes, head_cols))] + [like((cols, model_cols))] * parts,
        where,
        [heads, (code_grad, proj)],
        scratch=[pltpu.VMEM((codes, model_cols), f32)],
        flops=2 * head_cols * codes * (rows + model_cols),
    )
    head_sum, mix, *enc_blocks = lax.optimization_barrier((head_sum, mix, *enc_blocks))
    enc_grad = total(scattered(enc_blocks, "tensor")).astype(bf16)
    (proj_grad,) = run(proj_kernel, [like((head_cols, model_cols))], where, [(head_sum, enc)])
    shapes = [(codes // groups, features), (1, features), (features, relay), (relay, features)]
    dec_grad, gain_grad, send_grad, recv_grad = run(
        feature_kernel,
        [like(shape, f32 if k == 1 else bf16) for k, shape in enumerate(shapes)],
        where,
        [
            (
                mix,
                block(mix, "dp", 1),
                received,
                incoming,
                row_scale,
                inner,
                dec,
                recv,
                send,
                gain,
            )
        ],
        scratch=[pltpu.VMEM(shape, f32) for shape in shapes],
    )
    sent, returned, enc_grad = lax.optimization_barrier((sent, returned, enc_grad))
    return (
        sent[None, :tokens, :relay],
        returned[None, :tokens, :relay],
        heads_grad[None],
        proj_grad[None],
        enc_grad[None],
        dec_grad[None],
        gain_grad,
        send_grad[None],
        recv_grad[None],
    )


def solution(mesh):
    return jax.shard_map(
        on_device,
        mesh=mesh,
        in_specs=(
            P("pipe", "dp", "tensor"),
            P("pipe", "tensor", "dp"),
            P("pipe", None, "dp"),
            P("pipe", None, "tensor"),
            P("pipe", "tensor"),
            P("pipe", "tensor", None),
            P("pipe", None, "tensor"),
            P("dp", "tensor"),
            P("dp", "tensor"),
        ),
        out_specs=(
            P("pipe", "dp", "tensor"),
            P("pipe", "dp", "tensor"),
            P("pipe", "dp", "tensor"),
            P("pipe", "tensor", "dp"),
            P("pipe", "tensor", "dp"),
            P("pipe", "dp", "tensor"),
            P("pipe", "tensor"),
            P("pipe", "tensor", None),
            P("pipe", None, "tensor"),
        ),
        check_vma=False,
    )
```

```python
import functools

import jax
import jax.numpy as jnp
from jax import lax
from jax.experimental import pallas as pl
from jax.experimental.pallas import tpu as pltpu
from jax.sharding import PartitionSpec as P

epsilon = 1e-05
f32 = jnp.float32
bf16 = jnp.bfloat16
NN = ((1,), (0,))
NT = ((1,), (1,))
TN = ((0,), (0,))


def swap(shard, axis, by):
    return lax.ppermute(shard, axis, [(i, i ^ by) for i in range(lax.axis_size(axis))])


def move(shard, axis, by):
    devices = lax.axis_size(axis)
    pairs = [(i, i + by) for i in range(devices) if 0 <= i + by < devices]
    return lax.ppermute(shard, axis, pairs)


def gathered(shard, axis):
    return [shard] + [swap(shard, axis, k) for k in range(1, lax.axis_size(axis))]


def scattered(blocks, axis):
    return [blocks[0]] + [swap(blocks[k], axis, k) for k in range(1, len(blocks))]


def group_sum(rows, after, axis, where):
    groups = lax.axis_size(axis)
    step = groups // 2
    while step:
        other = swap(rows, axis, step)
        if step == 1:
            other, *_ = lax.optimization_barrier((other, *after))
        kernel = functools.partial(moved_sum_kernel, groups, step)
        (rows,) = run(kernel, [like(rows.shape)], where, [(rows, other)])
        step //= 2
    return rows


def halved_sum(kept, given, after, axis, size, where):
    count = kept.shape[0] // size
    step = 1
    while True:
        other = swap(given, axis, step)
        if step == 1:
            other, after = lax.optimization_barrier((other, after))
        if count == 1:
            return total([kept, other], where), after
        half = like((count // 2 * size, kept.shape[1]))
        kept, given = run(
            functools.partial(halved_kernel, size), [half, half], where, [(kept, other)]
        )
        step *= 2
        count //= 2


def total(blocks, where):
    return run(total_kernel, [like(blocks[0].shape)], where, [blocks])[0]


def block(array, axis, dim):
    size = array.shape[dim] // lax.axis_size(axis)
    return lax.dynamic_slice_in_dim(array, lax.axis_index(axis) * size, size, dim)


def dot(left, right, over):
    return lax.dot_general(left, right, (over, ((), ())), preferred_element_type=f32)


def run(kernel, results, where, groups_of_args, scratch=(), flops=0):
    counts = [len(group) for group in groups_of_args]
    flat = [array for group in groups_of_args for array in group]
    out_count = len(results)

    def body(where_ref, *refs):
        ins, at = [], 0
        for count in counts:
            ins.append(refs[at : at + count])
            at += count
        kernel(where_ref, ins, refs[at : at + out_count], refs[at + out_count :])

    size = sum(a.size * a.dtype.itemsize for a in list(flat) + list(results))
    return pl.pallas_call(
        body,
        out_shape=[jax.ShapeDtypeStruct(r.shape, r.dtype) for r in results],
        in_specs=[pl.BlockSpec(memory_space=pltpu.SMEM)]
        + [pl.BlockSpec(memory_space=pltpu.VMEM)] * len(flat),
        out_specs=[pl.BlockSpec(memory_space=pltpu.VMEM)] * out_count,
        scratch_shapes=list(scratch),
        compiler_params=pltpu.CompilerParams(vmem_limit_bytes=(10 << 20) if size < (10 << 20) else size + (12 << 20)),
        cost_estimate=pl.CostEstimate(flops=flops, bytes_accessed=size if flops else 0, transcendentals=0),
    )(where, *flat)


def like(shape, dtype=bf16):
    return jax.ShapeDtypeStruct(shape, dtype)


def by_rows(rows, step):
    chunk = min(rows, 512)
    if rows == chunk:
        step(slice(0, rows))
        return

    @pl.loop(0, rows // chunk)
    def _(index):
        step(pl.ds(pl.multiple_of(index * chunk, chunk), chunk))


def total_kernel(where, ins, outs, scratch):
    (blocks,) = ins
    result = blocks[0][...].astype(f32)
    for part in blocks[1:]:
        result = result + part[...].astype(f32)
    outs[0][...] = result.astype(bf16)


def moved_sum_kernel(groups, step, where, ins, outs, scratch):
    ((mine, other),) = ins
    size = mine.shape[0] // groups
    for k in range(groups):
        here = slice(k * size, (k + 1) * size)
        there = slice((k ^ step) * size, ((k ^ step) + 1) * size)
        value = mine[here, :].astype(f32) + other[there, :].astype(f32)
        outs[0][here, :] = value.astype(bf16)


def halved_kernel(size, where, ins, outs, scratch):
    ((mine, other),) = ins
    for k in range(mine.shape[0] // size):
        here = slice(k * size, (k + 1) * size)
        there = slice(k // 2 * size, (k // 2 + 1) * size)
        value = mine[here, :].astype(f32) + other[here, :].astype(f32)
        outs[k % 2][there, :] = value.astype(bf16)


def gram_kernel(where, ins, outs, scratch):
    ((dec, recv, send, gain),) = ins
    (whole,) = scratch
    codes, relay = dec.shape[0], recv.shape[0]
    cols = codes // len(outs)
    wide = 2 * relay
    head = cols * codes // wide
    whole[...] = dot(dec[...], dec[...], NT)
    for k, out in enumerate(outs):
        rows = pl.ds(pl.multiple_of((where[0] ^ k) * cols, cols), cols)
        for j in range(codes // wide):
            piece = whole[rows, j * wide : (j + 1) * wide]
            out[j * cols : (j + 1) * cols, :] = piece.astype(bf16)
    for ref, rows in ((dec, slice(head, head + codes)), (recv, slice(head + codes, None))):
        values = ref[...]
        gained = (values.astype(f32) * gain[...]).astype(bf16)
        plain = dot(values, recv[...], NT).astype(bf16)
        scaled = dot(gained, send[...], NN).astype(bf16)
        for out in outs:
            out[rows, :relay] = plain
            out[rows, relay:] = scaled


def setup_kernel(where, ins, outs, scratch):
    packs, ends = ins
    payload, products, weights = outs
    parts = len(packs)
    wide = products.shape[1]
    relay = wide // 2
    codes = weights.shape[0]
    cols = codes // parts
    head = cols * codes // wide
    for j in range(codes // wide):
        rows = slice(j * cols, (j + 1) * cols)
        gram = packs[0][rows, :].astype(f32)
        for pack in packs[1:]:
            gram = gram + pack[rows, :].astype(f32)
        gram = gram.astype(bf16)
        payload[2 * j * cols : (2 * j + 1) * cols, :] = gram[:, :relay]
        payload[(2 * j + 1) * cols : (2 * j + 2) * cols, :] = gram[:, relay:]
    start = 2 * head
    for end in ends:
        payload[start : start + end.shape[0], :] = end[:, end.shape[1] - relay :]
        start += end.shape[0]
    for k, pack in enumerate(packs):
        here = slice(k * relay, (k + 1) * relay)
        products[here, :] = pack[head + codes :, :]
        weights[:, here] = pack[head : head + codes, :relay]
        there = slice((parts + k) * relay, (parts + k + 1) * relay)
        weights[:, there] = pack[head : head + codes, relay:]


def fold_kernel(where, ins, outs, scratch):
    ((proj, enc),) = ins
    outs[0][...] = dot(proj[...], enc[...], NT).astype(bf16)


def partial_kernel(where, ins, outs, scratch):
    heads, (fold,) = ins
    (whole,) = scratch
    tokens, width = heads[0].shape[0], fold.shape[0]
    cols = outs[0].shape[1]
    parts = len(outs)
    together = 4 if len(heads) % 4 == 0 else 1
    for first in range(0, len(heads), together):
        rows = slice(first * tokens, (first + together) * tokens)
        values = jnp.concatenate([h[:, :width] for h in heads[first : first + together]])
        whole[...] = dot(values, fold[...], NN)
        for k in range(parts):
            at = (where[0] ^ k) * cols
            outs[k][rows, :] = whole[:, pl.ds(pl.multiple_of(at, cols), cols)].astype(bf16)


def forward(received, code_mix, code_send, square, products, width):
    relay = products.shape[1] // 2
    count = received.shape[1] // relay
    mixed, unscaled = [], []
    for k in range(count):
        cols = slice(k * relay, (k + 1) * relay)
        both = dot(received[:, cols], products[cols, :], NN)
        mixed.append(code_mix[:, cols] + both[:, :relay])
        unscaled.append(code_send[:, cols] + both[:, relay:])
    mixed = jnp.concatenate(mixed, axis=1)
    unscaled = jnp.concatenate(unscaled, axis=1)
    totals = square + jnp.sum(received.astype(f32) * (code_mix + mixed), axis=1, keepdims=True)
    row_scale = lax.rsqrt(jnp.maximum(totals, 0.0) / width + epsilon)
    return mixed, unscaled, row_scale


def backward(incoming, mixed, unscaled, row_scale, products, width):
    relay = products.shape[1] // 2
    count = incoming.shape[1] // relay
    inner = row_scale * jnp.sum(incoming.astype(f32) * unscaled, axis=1, keepdims=True) / width
    returned = []
    for k in range(count):
        cols = slice(k * relay, (k + 1) * relay)
        back = dot(incoming[:, cols], products[cols, relay:], NT)
        returned.append(row_scale * (back - row_scale * inner * mixed[:, cols]))
    return inner, jnp.concatenate(returned, axis=1).astype(bf16)


def first_kernel(width, where, ins, outs, scratch):
    mix_blocks, payloads, (products, weights) = ins
    mix, ends, mix_gram, mix_recv, mix_send, square, sent = outs
    (gram,) = scratch
    codes = mix.shape[1]
    relay = products.shape[1] // 2
    parts = len(mix_blocks)
    cols = codes // parts
    for k in range(parts):
        at = pl.multiple_of((where[0] ^ k) * cols, cols)
        mix[:, pl.ds(at, cols)] = mix_blocks[k][...]
        ends[:, k * relay : (k + 1) * relay] = payloads[k][cols * codes // relay :, :]
        for j in range(codes // relay):
            piece = payloads[k][j * cols : (j + 1) * cols, :]
            gram[pl.ds(at, cols), j * relay : (j + 1) * relay] = piece

    def step(at):
        codes_here = mix[at, :]
        in_gram = dot(codes_here, gram[...], NN)
        sums = jnp.sum(in_gram * codes_here.astype(f32), axis=1, keepdims=True)
        in_relay = dot(codes_here, weights[...], NN)
        in_recv = in_relay[:, : parts * relay]
        in_send = in_relay[:, parts * relay :]
        mix_gram[at, :] = in_gram
        mix_recv[at, :] = in_recv
        mix_send[at, :] = in_send
        square[at, :] = sums
        mixed, unscaled, row_scale = forward(
            ends[at, :], in_recv, in_send, sums, products[...], width
        )
        sent[at, :] = (row_scale * unscaled).astype(bf16)

    by_rows(mix.shape[0], step)


def forward_kernel(width, turn, last, where, ins, outs, scratch):
    ((moved, received, ends, mix_recv, mix_send, square, products),) = ins
    live = where[2] == turn

    def step(at):
        values = jnp.where(live, moved[at, :], received[at, :])
        mixed, unscaled, row_scale = forward(
            values, mix_recv[at, :], mix_send[at, :], square[at, :], products[...], width
        )
        outs[0][at, :] = values
        outs[1][at, :] = (row_scale * unscaled).astype(bf16)
        if last:
            inner, returned = backward(
                ends[at, :], mixed, unscaled, row_scale, products[...], width
            )
            outs[2][at, :] = mixed
            outs[3][at, :] = unscaled
            outs[4][at, :] = row_scale
            outs[5][at, :] = returned

    by_rows(moved.shape[0], step)
    if last:
        outs[6][...] = outs[1][: outs[6].shape[0], : outs[6].shape[1]]


def backward_kernel(width, live_section, last, tokens, where, ins, outs, scratch):
    (moved, incoming, received, mixed, unscaled, row_scale, mix_gram, products, weights, fold), = ins
    live = where[2] == live_section
    half = weights.shape[1] // 2

    def step(at):
        values = jnp.where(live, moved[at, :], incoming[at, :])
        scale = row_scale[at, :]
        inner, returned = backward(
            values, mixed[at, :], unscaled[at, :], scale, products[...], width
        )
        outs[0][at, :] = values
        outs[1][at, :] = returned
        if last:
            outs[2][at, :] = inner
            in_mixed = mix_gram[at, :] + dot(received[at, :], weights[:, :half], NT)
            back = dot(values, weights[:, half:], NT)
            outs[3][at, :] = (scale * (back - scale * inner * in_mixed)).astype(bf16)

    by_rows(moved.shape[0], step)
    if last:
        outs[6][...] = outs[1][: outs[6].shape[0], : outs[6].shape[1]]
        kept, given = outs[4:6]
        groups = 2 * kept.shape[0] // tokens
        for k in range(groups):
            rows = slice(k * tokens, (k + 1) * tokens)
            there = slice(k // 2 * tokens, (k // 2 + 1) * tokens)
            term = dot(outs[3][rows, :], fold[...], NT).astype(bf16)
            (given if k % 2 else kept)[there, :] = term


def head_kernel(where, ins, outs, scratch):
    heads, (code_grad, proj) = ins
    head_sum, enc_blocks = outs[0], outs[1:]
    (whole,) = scratch
    tokens, width = heads[0].shape[0], proj.shape[0]
    together = 4 if len(heads) % 4 == 0 else 1
    sums = None
    for first in range(0, len(heads), together):
        rows = slice(first * tokens, (first + together) * tokens)
        values = jnp.concatenate([h[:, :width] for h in heads[first : first + together]])
        term = dot(code_grad[rows, :], values, TN)
        sums = term if sums is None else sums + term
    head_sum[...] = sums.astype(bf16)
    whole[...] = dot(head_sum[...], proj[...], NN)
    size = enc_blocks[0].shape[0]
    for k, out in enumerate(enc_blocks):
        at = (where[0] ^ k) * size
        out[...] = whole[pl.ds(pl.multiple_of(at, size), size), :].astype(bf16)


def proj_kernel(where, ins, outs, scratch):
    ((head_sum, enc),) = ins
    outs[0][...] = dot(head_sum[...], enc[...], TN).astype(bf16)


def feature_kernel(where, ins, outs, scratch):
    (mix, mix_cols, received, incoming, row_scale, inner, dec, recv, send, gain), = ins
    sums = scratch
    relay = recv.shape[0]
    size = sums[0].shape[0]
    cols = slice(None)
    if mix_cols.shape[1] > size:
        cols = pl.ds(pl.multiple_of(where[1] * size, size), size)
    for ref in sums:
        ref[...] = jnp.zeros_like(ref)

    def step(at):
        received_here = received[at, :relay]
        incoming_here = incoming[at, :relay]
        scale = row_scale[at, :]
        mixed = dot(mix[at, :], dec[...], NN) + dot(received_here, recv[...], NN)
        normed = mixed * scale
        out_rows = (normed * gain[...]).astype(bf16)
        grad_norm = dot(incoming_here, send[...], NT)
        grad_mixed = scale * (grad_norm * gain[...] - normed * inner[at, :])
        grad_mixed = grad_mixed.astype(bf16)
        sums[0][...] += dot(mix_cols[at, cols], grad_mixed, TN)
        sums[1][...] += jnp.sum(grad_norm * normed, axis=0, keepdims=True)
        sums[2][...] += dot(out_rows, incoming_here, TN)
        sums[3][...] += dot(received_here, grad_mixed, TN)

    by_rows(mix.shape[0], step)
    for out, ref in zip(outs, sums):
        out[...] = ref[...].astype(out.dtype)


def on_device(
    heads_out,
    out_proj,
    encoder,
    decoder,
    norm_gain,
    send_encoder,
    recv_decoder,
    input_code,
    code_cotangent,
):
    sections = lax.axis_size("pipe")
    section = lax.axis_index("pipe")
    groups = lax.axis_size("dp")
    parts = lax.axis_size("tensor")
    width = norm_gain.shape[1] * parts
    proj = out_proj[0]
    enc = encoder[0]
    dec = decoder[0]
    gain = norm_gain
    send = send_encoder[0]
    recv = recv_decoder[0]
    tokens, relay = input_code.shape
    codes, features = dec.shape
    cols = codes // parts
    rows = tokens * groups
    head_cols, model_cols = proj.shape
    where = jnp.stack([lax.axis_index("tensor"), lax.axis_index("dp"), section]).astype(jnp.int32)

    end = jnp.where(section == 0, input_code, code_cotangent)
    heads = gathered(jnp.concatenate([heads_out[0], end], axis=1), "dp")
    packs = run(
        gram_kernel,
        [like((cols * codes // (2 * relay) + codes + relay, 2 * relay))] * parts,
        where,
        [(dec, recv, send, gain)],
        scratch=[pltpu.VMEM((codes, codes), f32)],
    )
    (fold,) = run(fold_kernel, [like((head_cols, codes))], where, [(proj, enc)])
    fold, _ = lax.optimization_barrier((fold, packs[0]))
    packs = scattered(packs, "tensor")

    partials = run(
        partial_kernel,
        [like((rows, cols))] * parts,
        where,
        [heads, (fold,)],
        scratch=[pltpu.VMEM((min(groups, 4) * tokens, codes), f32)],
        flops=2 * rows * head_cols * codes,
    )
    wide = parts * relay
    payload, products, weights = run(
        setup_kernel,
        [
            like((cols * codes // relay + rows, relay)),
            like((wide, 2 * relay)),
            like((codes, 2 * wide)),
        ],
        where,
        [packs, heads],
    )
    partials = list(partials)
    partials[3], *_ = lax.optimization_barrier((partials[3], *packs))
    code_block = total(scattered(partials, "tensor"), where)
    payloads = gathered(payload, "tensor")
    mix_block = group_sum(code_block, payloads, "dp", where)
    mix_blocks = gathered(mix_block, "tensor")

    square_flops = 2 * rows * codes * codes
    mix, ends, mix_gram, mix_recv, mix_send, square, sent = run(
        functools.partial(first_kernel, width),
        [
            like((rows, codes)),
            like((rows, wide)),
            like((rows, codes), f32),
            like((rows, wide), f32),
            like((rows, wide), f32),
            like((rows, 1), f32),
            like((rows, wide)),
        ],
        where,
        [mix_blocks, payloads, (products, weights)],
        scratch=[pltpu.VMEM((codes, codes), bf16)],
        flops=3 * square_flops,
    )
    received = ends
    for turn in range(1, sections):
        last = turn == sections - 1
        shapes = [like((rows, wide)), like((rows, wide))]
        if last:
            shapes += [like((rows, wide), f32)] * 2 + [like((rows, 1), f32), like((rows, wide))]
            shapes += [like((tokens, relay))]
        moved = move(sent, "pipe", 1)
        results = run(
            functools.partial(forward_kernel, width, turn, last),
            shapes,
            where,
            [(moved, received, ends, mix_recv, mix_send, square, products)],
            flops=square_flops,
        )
        received, sent = results[:2]
    mixed, unscaled, row_scale, returned, sent = results[2:]
    incoming = ends
    for turn in range(1, sections):
        last = turn == sections - 1
        shapes = [like((rows, wide)), like((rows, wide))]
        if last:
            shapes += [like((rows, 1), f32), like((rows, codes))]
            shapes += [like((rows // 2, head_cols))] * 2 + [like((tokens, relay))]
        moved = move(returned, "pipe", -1)
        results = run(
            functools.partial(backward_kernel, width, sections - 1 - turn, last, tokens),
            shapes,
            where,
            [
                (
                    moved,
                    incoming,
                    received,
                    mixed,
                    unscaled,
                    row_scale,
                    mix_gram,
                    products,
                    weights,
                    fold,
                )
            ],
            flops=3 * square_flops,
        )
        incoming, returned = results[:2]
    inner, code_grad, kept, given, returned = results[2:]

    heads_grad, row_scale = halved_sum(kept, given, row_scale, "dp", tokens, where)
    head_sum, *enc_blocks = run(
        head_kernel,
        [like((codes, head_cols))] + [like((cols, model_cols))] * parts,
        where,
        [heads, (code_grad, proj)],
        scratch=[pltpu.VMEM((codes, model_cols), f32)],
        flops=2 * head_cols * codes * (rows + model_cols),
    )
    head_sum, mix, *enc_blocks = lax.optimization_barrier((head_sum, mix, *enc_blocks))
    enc_grad = total(scattered(enc_blocks, "tensor"), where)
    (proj_grad,) = run(proj_kernel, [like((head_cols, model_cols))], where, [(head_sum, enc)])
    shapes = [(codes // groups, features), (1, features), (features, relay), (relay, features)]
    dec_grad, gain_grad, send_grad, recv_grad = run(
        feature_kernel,
        [like(shape, f32 if k == 1 else bf16) for k, shape in enumerate(shapes)],
        where,
        [
            (
                mix,
                mix if codes // groups % 128 == 0 else block(mix, "dp", 1),
                received,
                incoming,
                row_scale,
                inner,
                dec,
                recv,
                send,
                gain,
            )
        ],
        scratch=[pltpu.VMEM(shape, f32) for shape in shapes],
    )
    return (
        sent[None],
        returned[None],
        heads_grad[None],
        proj_grad[None],
        enc_grad[None],
        dec_grad[None],
        gain_grad,
        send_grad[None],
        recv_grad[None],
    )


def solution(mesh):
    return jax.shard_map(
        on_device,
        mesh=mesh,
        in_specs=(
            P("pipe", "dp", "tensor"),
            P("pipe", "tensor", "dp"),
            P("pipe", None, "dp"),
            P("pipe", None, "tensor"),
            P("pipe", "tensor"),
            P("pipe", "tensor", None),
            P("pipe", None, "tensor"),
            P("dp", "tensor"),
            P("dp", "tensor"),
        ),
        out_specs=(
            P("pipe", "dp", "tensor"),
            P("pipe", "dp", "tensor"),
            P("pipe", "dp", "tensor"),
            P("pipe", "tensor", "dp"),
            P("pipe", "tensor", "dp"),
            P("pipe", "dp", "tensor"),
            P("pipe", "tensor"),
            P("pipe", "tensor", None),
            P("pipe", None, "tensor"),
        ),
        check_vma=False,
    )
```

```python
import functools

import jax
import jax.numpy as jnp
from jax import lax
from jax.experimental import pallas as pl
from jax.experimental.pallas import tpu as pltpu
from jax.sharding import PartitionSpec as P

epsilon = 1e-05
f32 = jnp.float32
bf16 = jnp.bfloat16
NN = ((1,), (0,))
NT = ((1,), (1,))
TN = ((0,), (0,))


def swap(shard, axis, by):
    return lax.ppermute(shard, axis, [(i, i ^ by) for i in range(lax.axis_size(axis))])


def move(shard, axis, by):
    devices = lax.axis_size(axis)
    pairs = [(i, i + by) for i in range(devices) if 0 <= i + by < devices]
    return lax.ppermute(shard, axis, pairs)


def gathered(shard, axis):
    return [shard] + [swap(shard, axis, k) for k in range(1, lax.axis_size(axis))]


def line_gathered(shard, axis):
    if lax.axis_size(axis) != 4:
        return gathered(shard, axis)
    far, near = swap(shard, axis, 2), swap(shard, axis, 1)
    shard, far, near = lax.optimization_barrier((shard, far, near))
    across = lax.ppermute(shard, axis, [(1, 2), (2, 1)])
    passed = lax.ppermute(far, axis, [(1, 0), (2, 3)])
    return [shard, near, far, (across, passed)]


def scattered(blocks, axis):
    return [blocks[0]] + [swap(blocks[k], axis, k) for k in range(1, len(blocks))]


def group_sum(rows, after, axis, where):
    groups = lax.axis_size(axis)
    step = groups // 2
    while step:
        other = swap(rows, axis, step)
        if step == 1:
            other, *_ = lax.optimization_barrier((other, *after))
        kernel = functools.partial(moved_sum_kernel, groups, step)
        (rows,) = run(kernel, [like(rows.shape)], where, [(rows, other)])
        step //= 2
    return rows


def halved_sum(kept, given, after, axis, size, where):
    count = kept.shape[0] // size
    step = 1
    while True:
        other = swap(given, axis, step)
        if step == 1:
            other, after = lax.optimization_barrier((other, after))
        if count == 1:
            return total([kept, other], where), after
        half = like((count // 2 * size, kept.shape[1]))
        kept, given = run(
            functools.partial(halved_kernel, size), [half, half], where, [(kept, other)]
        )
        step *= 2
        count //= 2


def total(blocks, where):
    return run(total_kernel, [like(blocks[0].shape)], where, [blocks])[0]


def ordered(blocks, axis):
    step = 1
    while step < len(blocks):
        odd = (lax.axis_index(axis) & step) > 0
        blocks = [jnp.where(odd, blocks[k ^ step], part) for k, part in enumerate(blocks)]
        step *= 2
    return jnp.concatenate(blocks, axis=1)


def block(array, axis, dim):
    size = array.shape[dim] // lax.axis_size(axis)
    return lax.dynamic_slice_in_dim(array, lax.axis_index(axis) * size, size, dim)


def dot(left, right, over):
    return lax.dot_general(left, right, (over, ((), ())), preferred_element_type=f32)


def run(kernel, results, where, groups_of_args, scratch=(), flops=0):
    counts = [len(group) for group in groups_of_args]
    flat = [array for group in groups_of_args for array in group]
    out_count = len(results)

    def body(where_ref, *refs):
        ins, at = [], 0
        for count in counts:
            ins.append(refs[at : at + count])
            at += count
        kernel(where_ref, ins, refs[at : at + out_count], refs[at + out_count :])

    size = sum(a.size * a.dtype.itemsize for a in list(flat) + list(results))
    return pl.pallas_call(
        body,
        out_shape=[jax.ShapeDtypeStruct(r.shape, r.dtype) for r in results],
        in_specs=[pl.BlockSpec(memory_space=pltpu.SMEM)]
        + [pl.BlockSpec(memory_space=pltpu.VMEM)] * len(flat),
        out_specs=[pl.BlockSpec(memory_space=pltpu.VMEM)] * out_count,
        scratch_shapes=list(scratch),
        compiler_params=pltpu.CompilerParams(vmem_limit_bytes=(10 << 20) if size < (10 << 20) else size + (12 << 20)),
        cost_estimate=pl.CostEstimate(flops=flops, bytes_accessed=size if flops else 0, transcendentals=0),
    )(where, *flat)


def like(shape, dtype=bf16):
    return jax.ShapeDtypeStruct(shape, dtype)


def by_rows(rows, step):
    chunk = min(rows, 512)
    if rows == chunk:
        step(slice(0, rows))
        return

    @pl.loop(0, rows // chunk)
    def _(index):
        step(pl.ds(pl.multiple_of(index * chunk, chunk), chunk))


def total_kernel(where, ins, outs, scratch):
    (blocks,) = ins
    result = blocks[0][...].astype(f32)
    for part in blocks[1:]:
        result = result + part[...].astype(f32)
    outs[0][...] = result.astype(bf16)


def moved_sum_kernel(groups, step, where, ins, outs, scratch):
    ((mine, other),) = ins
    size = mine.shape[0] // groups
    for k in range(groups):
        here = slice(k * size, (k + 1) * size)
        there = slice((k ^ step) * size, ((k ^ step) + 1) * size)
        value = mine[here, :].astype(f32) + other[there, :].astype(f32)
        outs[0][here, :] = value.astype(bf16)


def halved_kernel(size, where, ins, outs, scratch):
    ((mine, other),) = ins
    for k in range(mine.shape[0] // size):
        here = slice(k * size, (k + 1) * size)
        there = slice(k // 2 * size, (k // 2 + 1) * size)
        value = mine[here, :].astype(f32) + other[here, :].astype(f32)
        outs[k % 2][there, :] = value.astype(bf16)


def gram_kernel(where, ins, outs, scratch):
    ((dec, recv, send, gain),) = ins
    (whole,) = scratch
    codes, relay = dec.shape[0], recv.shape[0]
    cols = codes // len(outs)
    wide = 2 * relay
    head = cols * codes // wide
    whole[...] = dot(dec[...], dec[...], NT)
    for k, out in enumerate(outs):
        rows = pl.ds(pl.multiple_of((where[0] ^ k) * cols, cols), cols)
        for j in range(codes // wide):
            piece = whole[rows, j * wide : (j + 1) * wide]
            out[j * cols : (j + 1) * cols, :] = piece.astype(bf16)
    for ref, rows in ((dec, slice(head, head + codes)), (recv, slice(head + codes, None))):
        values = ref[...]
        gained = (values.astype(f32) * gain[...]).astype(bf16)
        plain = dot(values, recv[...], NT).astype(bf16)
        scaled = dot(gained, send[...], NN).astype(bf16)
        for out in outs:
            out[rows, :relay] = plain
            out[rows, relay:] = scaled


def setup_kernel(where, ins, outs, scratch):
    packs, ends = ins
    payload, products, weights = outs
    parts = len(packs)
    wide = products.shape[1]
    relay = wide // 2
    codes = weights.shape[0]
    cols = codes // parts
    head = cols * codes // wide
    for j in range(codes // wide):
        rows = slice(j * cols, (j + 1) * cols)
        gram = packs[0][rows, :].astype(f32)
        for pack in packs[1:]:
            gram = gram + pack[rows, :].astype(f32)
        gram = gram.astype(bf16)
        payload[2 * j * cols : (2 * j + 1) * cols, :] = gram[:, :relay]
        payload[(2 * j + 1) * cols : (2 * j + 2) * cols, :] = gram[:, relay:]
    start = 2 * head
    for end in ends:
        payload[start : start + end.shape[0], :] = end[:, end.shape[1] - relay :]
        start += end.shape[0]
    for k, pack in enumerate(packs):
        here = slice(k * relay, (k + 1) * relay)
        products[here, :] = pack[head + codes :, :]
        weights[:, here] = pack[head : head + codes, :relay]
        there = slice((parts + k) * relay, (parts + k + 1) * relay)
        weights[:, there] = pack[head : head + codes, relay:]


def rows_kernel(where, ins, outs, scratch):
    ((heads, first, last),) = ins
    width = heads.shape[1]
    outs[0][:, :width] = heads[...]
    outs[0][:, width:] = jnp.where(where[2] == 0, first[...], last[...])


def fold_kernel(groups, where, ins, outs, scratch):
    ((proj, enc),) = ins
    fold = outs[0]
    size = fold.shape[0] // groups
    fold[...] = dot(proj[...], enc[...], NT).astype(bf16)
    for k in range(groups):
        there = slice(k // 2 * size, (k // 2 + 1) * size)
        here = pl.ds(pl.multiple_of((where[1] ^ k) * size, size), size)
        outs[1 + k % 2][there, :] = fold[here, :]


def partial_kernel(where, ins, outs, scratch):
    heads, (fold,) = ins
    (whole,) = scratch
    tokens, width = heads[0].shape[0], fold.shape[0]
    cols = outs[0].shape[1]
    parts = len(outs)
    together = 4 if len(heads) % 4 == 0 else 1
    for first in range(0, len(heads), together):
        rows = slice(first * tokens, (first + together) * tokens)
        values = jnp.concatenate([h[:, :width] for h in heads[first : first + together]])
        whole[...] = dot(values, fold[...], NN)
        for k in range(parts):
            at = (where[0] ^ k) * cols
            outs[k][rows, :] = whole[:, pl.ds(pl.multiple_of(at, cols), cols)].astype(bf16)


def forward(received, code_mix, code_send, square, products, width):
    relay = products.shape[1] // 2
    count = received.shape[1] // relay
    mixed, unscaled = [], []
    for k in range(count):
        cols = slice(k * relay, (k + 1) * relay)
        both = dot(received[:, cols], products[cols, :], NN)
        mixed.append(code_mix[:, cols] + both[:, :relay])
        unscaled.append(code_send[:, cols] + both[:, relay:])
    mixed = jnp.concatenate(mixed, axis=1)
    unscaled = jnp.concatenate(unscaled, axis=1)
    totals = square + jnp.sum(received.astype(f32) * (code_mix + mixed), axis=1, keepdims=True)
    row_scale = lax.rsqrt(jnp.maximum(totals, 0.0) / width + epsilon)
    return mixed, unscaled, row_scale


def backward(incoming, mixed, unscaled, row_scale, products, width):
    relay = products.shape[1] // 2
    count = incoming.shape[1] // relay
    inner = row_scale * jnp.sum(incoming.astype(f32) * unscaled, axis=1, keepdims=True) / width
    returned = []
    for k in range(count):
        cols = slice(k * relay, (k + 1) * relay)
        back = dot(incoming[:, cols], products[cols, relay:], NT)
        returned.append(row_scale * (back - row_scale * inner * mixed[:, cols]))
    return inner, jnp.concatenate(returned, axis=1).astype(bf16)


def first_kernel(width, where, ins, outs, scratch):
    mix_blocks, payloads, (products, weights) = ins
    mix, ends, mix_gram, mix_recv, mix_send, square, sent = outs
    (gram,) = scratch
    codes = mix.shape[1]
    relay = products.shape[1] // 2
    parts = len(mix_blocks)
    cols = codes // parts
    for k in range(parts):
        at = pl.multiple_of((where[0] ^ k) * cols, cols)
        mix[:, pl.ds(at, cols)] = mix_blocks[k][...]
        ends[:, k * relay : (k + 1) * relay] = payloads[k][cols * codes // relay :, :]
        for j in range(codes // relay):
            piece = payloads[k][j * cols : (j + 1) * cols, :]
            gram[pl.ds(at, cols), j * relay : (j + 1) * relay] = piece

    def step(at):
        codes_here = mix[at, :]
        in_gram = dot(codes_here, gram[...], NN)
        sums = jnp.sum(in_gram * codes_here.astype(f32), axis=1, keepdims=True)
        in_relay = dot(codes_here, weights[...], NN)
        in_recv = in_relay[:, : parts * relay]
        in_send = in_relay[:, parts * relay :]
        mix_gram[at, :] = in_gram
        mix_recv[at, :] = in_recv
        mix_send[at, :] = in_send
        square[at, :] = sums
        mixed, unscaled, row_scale = forward(
            ends[at, :], in_recv, in_send, sums, products[...], width
        )
        sent[at, :] = (row_scale * unscaled).astype(bf16)

    by_rows(mix.shape[0], step)


def forward_kernel(width, turn, last, where, ins, outs, scratch):
    ((moved, received, ends, mix_recv, mix_send, square, products),) = ins
    live = where[2] == turn

    def step(at):
        values = jnp.where(live, moved[at, :], received[at, :])
        mixed, unscaled, row_scale = forward(
            values, mix_recv[at, :], mix_send[at, :], square[at, :], products[...], width
        )
        outs[0][at, :] = values
        outs[1][at, :] = (row_scale * unscaled).astype(bf16)
        if last:
            inner, returned = backward(
                ends[at, :], mixed, unscaled, row_scale, products[...], width
            )
            outs[2][at, :] = mixed
            outs[3][at, :] = unscaled
            outs[4][at, :] = row_scale
            outs[5][at, :] = returned

    by_rows(moved.shape[0], step)
    if last:
        outs[6][...] = outs[1][: outs[6].shape[0], : outs[6].shape[1]]


def backward_kernel(width, live_section, last, where, ins, outs, scratch):
    (moved, incoming, received, mixed, unscaled, row_scale, mix_gram, products, weights), = ins
    live = where[2] == live_section
    half = weights.shape[1] // 2

    def step(at):
        values = jnp.where(live, moved[at, :], incoming[at, :])
        scale = row_scale[at, :]
        inner, returned = backward(
            values, mixed[at, :], unscaled[at, :], scale, products[...], width
        )
        outs[0][at, :] = values
        outs[1][at, :] = returned
        if last:
            outs[2][at, :] = inner
            in_mixed = mix_gram[at, :] + dot(received[at, :], weights[:, :half], NT)
            back = dot(values, weights[:, half:], NT)
            outs[3][at, :] = (scale * (back - scale * inner * in_mixed)).astype(bf16)

    by_rows(moved.shape[0], step)
    if last:
        outs[4][...] = outs[1][: outs[4].shape[0], : outs[4].shape[1]]


def heads_kernel(where, ins, outs, scratch):
    ((code_grad, fold_rows),) = ins
    tokens = outs[0].shape[0]
    whole = dot(code_grad[...], fold_rows[...], NT)
    for k, out in enumerate(outs):
        out[...] = whole[k * tokens : (k + 1) * tokens, :].astype(bf16)


def laid_kernel(where, ins, outs, scratch):
    (blocks,) = ins
    size = blocks[0].shape[1]
    for k, part in enumerate(blocks):
        at = pl.multiple_of((where[1] ^ k) * size, size)
        outs[0][:, pl.ds(at, size)] = part[...]


def head_kernel(where, ins, outs, scratch):
    heads, (code_grad, proj) = ins
    head_sum, enc_blocks = outs[0], outs[1:]
    (whole,) = scratch
    tokens, width = heads[0].shape[0], proj.shape[0]
    together = 4 if len(heads) % 4 == 0 else 1
    sums = None
    for first in range(0, len(heads), together):
        rows = slice(first * tokens, (first + together) * tokens)
        values = jnp.concatenate([h[:, :width] for h in heads[first : first + together]])
        term = dot(code_grad[rows, :], values, TN)
        sums = term if sums is None else sums + term
    head_sum[...] = sums.astype(bf16)
    whole[...] = dot(head_sum[...], proj[...], NN)
    size = enc_blocks[0].shape[0]
    for k, out in enumerate(enc_blocks):
        at = (where[0] ^ k) * size
        out[...] = whole[pl.ds(pl.multiple_of(at, size), size), :].astype(bf16)


def proj_kernel(where, ins, outs, scratch):
    ((head_sum, enc),) = ins
    outs[0][...] = dot(head_sum[...], enc[...], TN).astype(bf16)


def feature_kernel(where, ins, outs, scratch):
    (mix, mix_cols, received, incoming, row_scale, inner, dec, recv, send, gain), = ins
    sums = scratch
    relay = recv.shape[0]
    size = sums[0].shape[0]
    cols = slice(None)
    if mix_cols.shape[1] > size:
        cols = pl.ds(pl.multiple_of(where[1] * size, size), size)
    for ref in sums:
        ref[...] = jnp.zeros_like(ref)

    def step(at):
        received_here = received[at, :relay]
        incoming_here = incoming[at, :relay]
        scale = row_scale[at, :]
        mixed = dot(mix[at, :], dec[...], NN) + dot(received_here, recv[...], NN)
        normed = mixed * scale
        out_rows = (normed * gain[...]).astype(bf16)
        grad_norm = dot(incoming_here, send[...], NT)
        grad_mixed = scale * (grad_norm * gain[...] - normed * inner[at, :])
        grad_mixed = grad_mixed.astype(bf16)
        sums[0][...] += dot(mix_cols[at, cols], grad_mixed, TN)
        sums[1][...] += jnp.sum(grad_norm * normed, axis=0, keepdims=True)
        sums[2][...] += dot(out_rows, incoming_here, TN)
        sums[3][...] += dot(received_here, grad_mixed, TN)

    by_rows(mix.shape[0], step)
    for out, ref in zip(outs, sums):
        out[...] = ref[...].astype(out.dtype)


def on_device(
    heads_out,
    out_proj,
    encoder,
    decoder,
    norm_gain,
    send_encoder,
    recv_decoder,
    input_code,
    code_cotangent,
):
    sections = lax.axis_size("pipe")
    section = lax.axis_index("pipe")
    groups = lax.axis_size("dp")
    parts = lax.axis_size("tensor")
    width = norm_gain.shape[1] * parts
    proj = out_proj[0]
    enc = encoder[0]
    dec = decoder[0]
    gain = norm_gain
    send = send_encoder[0]
    recv = recv_decoder[0]
    tokens, relay = input_code.shape
    codes, features = dec.shape
    cols = codes // parts
    rows = tokens * groups
    head_cols, model_cols = proj.shape
    where = jnp.stack([lax.axis_index("tensor"), lax.axis_index("dp"), section]).astype(jnp.int32)

    head_cols, model_cols = proj.shape
    (rows_here,) = run(
        rows_kernel,
        [like((tokens, head_cols + relay))],
        where,
        [(heads_out[0], input_code, code_cotangent)],
    )
    heads = line_gathered(rows_here, "dp")
    if isinstance(heads[-1], tuple):
        heads[-1] = total(heads[-1], where)
    packs = run(
        gram_kernel,
        [like((cols * codes // (2 * relay) + codes + relay, 2 * relay))] * parts,
        where,
        [(dec, recv, send, gain)],
        scratch=[pltpu.VMEM((codes, codes), f32)],
    )
    half = like((head_cols // 2, codes))
    fold, fold_kept, fold_given = run(
        functools.partial(fold_kernel, groups),
        [like((head_cols, codes)), half, half],
        where,
        [(proj, enc)],
    )
    fold, _ = lax.optimization_barrier((fold, packs[0]))
    packs = scattered(packs, "tensor")

    partials = run(
        partial_kernel,
        [like((rows, cols))] * parts,
        where,
        [heads, (fold,)],
        scratch=[pltpu.VMEM((min(groups, 4) * tokens, codes), f32)],
        flops=2 * rows * head_cols * codes,
    )
    partials = list(partials)
    partials[3], *_ = lax.optimization_barrier((partials[3], *packs))
    code_block = total(scattered(partials, "tensor"), where)
    wide = parts * relay
    packs, _ = lax.optimization_barrier((packs, code_block))
    payload, products, weights = run(
        setup_kernel,
        [
            like((cols * codes // relay + rows, relay)),
            like((wide, 2 * relay)),
            like((codes, 2 * wide)),
        ],
        where,
        [packs, heads],
    )
    payloads = gathered(payload, "tensor")
    mix_block = group_sum(code_block, payloads, "dp", where)
    fold_given, mix_block = lax.optimization_barrier((fold_given, mix_block))
    mix_blocks = gathered(mix_block, "tensor")

    square_flops = 2 * rows * codes * codes
    mix, ends, mix_gram, mix_recv, mix_send, square, sent = run(
        functools.partial(first_kernel, width),
        [
            like((rows, codes)),
            like((rows, wide)),
            like((rows, codes), f32),
            like((rows, wide), f32),
            like((rows, wide), f32),
            like((rows, 1), f32),
            like((rows, wide)),
        ],
        where,
        [mix_blocks, payloads, (products, weights)],
        scratch=[pltpu.VMEM((codes, codes), bf16)],
        flops=3 * square_flops,
    )
    fold_rows, sent = halved_sum(
        fold_kept, fold_given, sent, "dp", head_cols // groups, where
    )
    received = ends
    for turn in range(1, sections):
        last = turn == sections - 1
        shapes = [like((rows, wide)), like((rows, wide))]
        if last:
            shapes += [like((rows, wide), f32)] * 2 + [like((rows, 1), f32), like((rows, wide))]
            shapes += [like((tokens, relay))]
        moved = move(sent, "pipe", 1)
        results = run(
            functools.partial(forward_kernel, width, turn, last),
            shapes,
            where,
            [(moved, received, ends, mix_recv, mix_send, square, products)],
            flops=square_flops,
        )
        received, sent = results[:2]
    mixed, unscaled, row_scale, returned, sent = results[2:]
    incoming = ends
    for turn in range(1, sections):
        last = turn == sections - 1
        shapes = [like((rows, wide)), like((rows, wide))]
        if last:
            shapes += [like((rows, 1), f32), like((rows, codes))]
            shapes += [like((tokens, relay))]
        moved = move(returned, "pipe", -1)
        results = run(
            functools.partial(backward_kernel, width, sections - 1 - turn, last),
            shapes,
            where,
            [
                (
                    moved,
                    incoming,
                    received,
                    mixed,
                    unscaled,
                    row_scale,
                    mix_gram,
                    products,
                    weights,
                )
            ],
            flops=3 * square_flops,
        )
        incoming, returned = results[:2]
    inner, code_grad, returned = results[2:]

    head_sum, *enc_blocks = run(
        head_kernel,
        [like((codes, head_cols))] + [like((cols, model_cols))] * parts,
        where,
        [heads, (code_grad, proj)],
        scratch=[pltpu.VMEM((codes, model_cols), f32)],
        flops=2 * head_cols * codes * (rows + model_cols),
    )
    head_sum, mix, *enc_blocks = lax.optimization_barrier((head_sum, mix, *enc_blocks))
    enc_grad = total(scattered(enc_blocks, "tensor"), where)
    head_blocks = run(
        heads_kernel,
        [like((tokens, head_cols // groups))] * groups,
        where,
        [(code_grad, fold_rows)],
    )
    head_blocks = scattered(head_blocks, "dp")
    if head_cols // groups % 128 == 0:
        (heads_grad,) = run(laid_kernel, [like((tokens, head_cols))], where, [head_blocks])
    else:
        heads_grad = ordered(head_blocks, "dp")
    (proj_grad,) = run(proj_kernel, [like((head_cols, model_cols))], where, [(head_sum, enc)])
    shapes = [(codes // groups, features), (1, features), (features, relay), (relay, features)]
    dec_grad, gain_grad, send_grad, recv_grad = run(
        feature_kernel,
        [like(shape, f32 if k == 1 else bf16) for k, shape in enumerate(shapes)],
        where,
        [
            (
                mix,
                mix if codes // groups % 128 == 0 else block(mix, "dp", 1),
                received,
                incoming,
                row_scale,
                inner,
                dec,
                recv,
                send,
                gain,
            )
        ],
        scratch=[pltpu.VMEM(shape, f32) for shape in shapes],
    )
    return (
        sent[None],
        returned[None],
        heads_grad[None],
        proj_grad[None],
        enc_grad[None],
        dec_grad[None],
        gain_grad,
        send_grad[None],
        recv_grad[None],
    )


def solution(mesh):
    return jax.shard_map(
        on_device,
        mesh=mesh,
        in_specs=(
            P("pipe", "dp", "tensor"),
            P("pipe", "tensor", "dp"),
            P("pipe", None, "dp"),
            P("pipe", None, "tensor"),
            P("pipe", "tensor"),
            P("pipe", "tensor", None),
            P("pipe", None, "tensor"),
            P("dp", "tensor"),
            P("dp", "tensor"),
        ),
        out_specs=(
            P("pipe", "dp", "tensor"),
            P("pipe", "dp", "tensor"),
            P("pipe", "dp", "tensor"),
            P("pipe", "tensor", "dp"),
            P("pipe", "tensor", "dp"),
            P("pipe", "dp", "tensor"),
            P("pipe", "tensor"),
            P("pipe", "tensor", None),
            P("pipe", None, "tensor"),
        ),
        check_vma=False,
    )
```

```python
import functools

import jax
import jax.numpy as jnp
from jax import lax
from jax.experimental import pallas as pl
from jax.experimental.pallas import tpu as pltpu
from jax.sharding import PartitionSpec as P

epsilon = 1e-05
f32 = jnp.float32
bf16 = jnp.bfloat16
NN = ((1,), (0,))
NT = ((1,), (1,))
TN = ((0,), (0,))


def swap(shard, axis, by):
    return lax.ppermute(shard, axis, [(i, i ^ by) for i in range(lax.axis_size(axis))])


def move(shard, axis, by):
    devices = lax.axis_size(axis)
    pairs = [(i, i + by) for i in range(devices) if 0 <= i + by < devices]
    return lax.ppermute(shard, axis, pairs)


def gathered(shard, axis):
    return [shard] + [swap(shard, axis, k) for k in range(1, lax.axis_size(axis))]


def line_gathered(shard, axis):
    if lax.axis_size(axis) != 4:
        return gathered(shard, axis), []
    far, near = swap(shard, axis, 2), swap(shard, axis, 1)
    shard, far, near = lax.optimization_barrier((shard, far, near))
    across = lax.ppermute(shard, axis, [(1, 2), (2, 1)])
    passed = lax.ppermute(far, axis, [(1, 0), (2, 3)])
    return [shard, near, far], [across, passed]


def scattered(blocks, axis):
    return [blocks[0]] + [swap(blocks[k], axis, k) for k in range(1, len(blocks))]


def group_sum(rows, after, axis, where):
    groups = lax.axis_size(axis)
    step = groups // 2
    while step:
        other = swap(rows, axis, step)
        if step == 1:
            other, *_ = lax.optimization_barrier((other, *after))
        kernel = functools.partial(moved_sum_kernel, groups, step)
        (rows,) = run(kernel, [like(rows.shape)], where, [(rows, other)])
        step //= 2
    return rows


def halved_sum(kept, given, after, axis, size, where):
    count = kept.shape[0] // size
    step = 1
    while True:
        other = swap(given, axis, step)
        if step == 1:
            other, after = lax.optimization_barrier((other, after))
        if count == 1:
            return [kept, other], after
        half = like((count // 2 * size, kept.shape[1]))
        kept, given = run(
            functools.partial(halved_kernel, size), [half, half], where, [(kept, other)]
        )
        step *= 2
        count //= 2


def total(blocks, where):
    return run(total_kernel, [like(blocks[0].shape)], where, [blocks])[0]


def ordered(blocks, axis):
    step = 1
    while step < len(blocks):
        odd = (lax.axis_index(axis) & step) > 0
        blocks = [jnp.where(odd, blocks[k ^ step], part) for k, part in enumerate(blocks)]
        step *= 2
    return jnp.concatenate(blocks, axis=1)


def block(array, axis, dim):
    size = array.shape[dim] // lax.axis_size(axis)
    return lax.dynamic_slice_in_dim(array, lax.axis_index(axis) * size, size, dim)


def dot(left, right, over):
    return lax.dot_general(left, right, (over, ((), ())), preferred_element_type=f32)


def run(kernel, results, where, groups_of_args, scratch=(), flops=0, fetch=False):
    counts = [len(group) for group in groups_of_args]
    flat = [array for group in groups_of_args for array in group]
    out_count = len(results)
    scratch = list(scratch)
    own = len(scratch)
    space = pltpu.HBM if fetch else pltpu.VMEM
    if fetch:
        scratch += [pltpu.VMEM(array.shape, array.dtype) for array in flat]
        scratch.append(pltpu.SemaphoreType.DMA((len(flat),)))

    def body(where_ref, *refs):
        args, refs = refs[: len(flat)], refs[len(flat) :]
        outs, refs = refs[:out_count], refs[out_count:]
        if fetch:
            held, arrived = refs[own:-1], refs[-1]
            copies = [
                pltpu.make_async_copy(arg, here, arrived.at[k])
                for k, (arg, here) in enumerate(zip(args, held))
            ]
            for copy in copies:
                copy.start()
            for copy in copies:
                copy.wait()
            args = held
        ins, at = [], 0
        for count in counts:
            ins.append(args[at : at + count])
            at += count
        kernel(where_ref, ins, outs, refs[:own])

    size = sum(a.size * a.dtype.itemsize for a in list(flat) + list(results))
    limit = (10 << 20) if size < (10 << 20) else size + (12 << 20)
    return pl.pallas_call(
        body,
        out_shape=[jax.ShapeDtypeStruct(r.shape, r.dtype) for r in results],
        in_specs=[pl.BlockSpec(memory_space=pltpu.SMEM)]
        + [pl.BlockSpec(memory_space=space)] * len(flat),
        out_specs=[pl.BlockSpec(memory_space=pltpu.VMEM)] * out_count,
        scratch_shapes=scratch,
        compiler_params=pltpu.CompilerParams(vmem_limit_bytes=limit),
        cost_estimate=pl.CostEstimate(
            flops=flops, bytes_accessed=size if flops else 0, transcendentals=0
        ),
    )(where, *flat)


def like(shape, dtype=bf16):
    return jax.ShapeDtypeStruct(shape, dtype)


def by_rows(rows, step):
    chunk = min(rows, 512)
    if rows == chunk:
        step(slice(0, rows))
        return

    @pl.loop(0, rows // chunk)
    def _(index):
        step(pl.ds(pl.multiple_of(index * chunk, chunk), chunk))


def total_kernel(where, ins, outs, scratch):
    (blocks,) = ins
    result = blocks[0][...].astype(f32)
    for part in blocks[1:]:
        result = result + part[...].astype(f32)
    outs[0][...] = result.astype(bf16)


def moved_sum_kernel(groups, step, where, ins, outs, scratch):
    ((mine, other),) = ins
    size = mine.shape[0] // groups
    for k in range(groups):
        here = slice(k * size, (k + 1) * size)
        there = slice((k ^ step) * size, ((k ^ step) + 1) * size)
        value = mine[here, :].astype(f32) + other[there, :].astype(f32)
        outs[0][here, :] = value.astype(bf16)


def halved_kernel(size, where, ins, outs, scratch):
    ((mine, other),) = ins
    for k in range(mine.shape[0] // size):
        here = slice(k * size, (k + 1) * size)
        there = slice(k // 2 * size, (k // 2 + 1) * size)
        value = mine[here, :].astype(f32) + other[here, :].astype(f32)
        outs[k % 2][there, :] = value.astype(bf16)


def gram_kernel(where, ins, outs, scratch):
    ((dec, recv, send, gain),) = ins
    (whole,) = scratch
    codes, relay = dec.shape[0], recv.shape[0]
    cols = codes // len(outs)
    wide = 2 * relay
    head = cols * codes // wide
    whole[...] = dot(dec[...], dec[...], NT)
    for k, out in enumerate(outs):
        rows = pl.ds(pl.multiple_of((where[0] ^ k) * cols, cols), cols)
        for j in range(codes // wide):
            piece = whole[rows, j * wide : (j + 1) * wide]
            out[j * cols : (j + 1) * cols, :] = piece.astype(bf16)
    for ref, rows in ((dec, slice(head, head + codes)), (recv, slice(head + codes, None))):
        values = ref[...]
        gained = (values.astype(f32) * gain[...]).astype(bf16)
        plain = dot(values, recv[...], NT).astype(bf16)
        scaled = dot(gained, send[...], NN).astype(bf16)
        for out in outs:
            out[rows, :relay] = plain
            out[rows, relay:] = scaled


def setup_kernel(where, ins, outs, scratch):
    packs, ends = ins
    payload, products, weights = outs
    parts = len(packs)
    wide = products.shape[1]
    relay = wide // 2
    codes = weights.shape[0]
    cols = codes // parts
    head = cols * codes // wide
    for j in range(codes // wide):
        rows = slice(j * cols, (j + 1) * cols)
        gram = packs[0][rows, :].astype(f32)
        for pack in packs[1:]:
            gram = gram + pack[rows, :].astype(f32)
        gram = gram.astype(bf16)
        payload[2 * j * cols : (2 * j + 1) * cols, :] = gram[:, :relay]
        payload[(2 * j + 1) * cols : (2 * j + 2) * cols, :] = gram[:, relay:]
    start = 2 * head
    for end in ends:
        payload[start : start + end.shape[0], :] = end[...]
        start += end.shape[0]
    for k, pack in enumerate(packs):
        here = slice(k * relay, (k + 1) * relay)
        products[here, :] = pack[head + codes :, :]
        weights[:, here] = pack[head : head + codes, :relay]
        there = slice((parts + k) * relay, (parts + k + 1) * relay)
        weights[:, there] = pack[head : head + codes, relay:]


def fold_kernel(groups, where, ins, outs, scratch):
    ((proj, enc),) = ins
    fold = outs[0]
    size = fold.shape[0] // groups
    fold[...] = dot(proj[...], enc[...], NT).astype(bf16)
    for k in range(groups):
        there = slice(k // 2 * size, (k // 2 + 1) * size)
        here = pl.ds(pl.multiple_of((where[1] ^ k) * size, size), size)
        outs[1 + k % 2][there, :] = fold[here, :]


def partial_kernel(where, ins, outs, scratch):
    heads, pair, (fold,) = ins
    (whole,) = scratch
    if pair:
        outs, last = outs[:-1], outs[-1]
        last[...] = pair[0][...] + pair[1][...]
        heads = [*heads, last]
    tokens = heads[0].shape[0]
    cols = outs[0].shape[1]
    parts = len(outs)
    together = 4 if len(heads) % 4 == 0 else 1
    for first in range(0, len(heads), together):
        rows = slice(first * tokens, (first + together) * tokens)
        values = jnp.concatenate([h[...] for h in heads[first : first + together]])
        whole[...] = dot(values, fold[...], NN)
        for k in range(parts):
            at = (where[0] ^ k) * cols
            outs[k][rows, :] = whole[:, pl.ds(pl.multiple_of(at, cols), cols)].astype(bf16)


def forward(received, code_mix, code_send, square, products, width):
    relay = products.shape[1] // 2
    count = received.shape[1] // relay
    mixed, unscaled = [], []
    for k in range(count):
        cols = slice(k * relay, (k + 1) * relay)
        both = dot(received[:, cols], products[cols, :], NN)
        mixed.append(code_mix[:, cols] + both[:, :relay])
        unscaled.append(code_send[:, cols] + both[:, relay:])
    mixed = jnp.concatenate(mixed, axis=1)
    unscaled = jnp.concatenate(unscaled, axis=1)
    totals = square + jnp.sum(received.astype(f32) * (code_mix + mixed), axis=1, keepdims=True)
    row_scale = lax.rsqrt(jnp.maximum(totals, 0.0) / width + epsilon)
    return mixed, unscaled, row_scale


def backward(incoming, mixed, unscaled, row_scale, products, width):
    relay = products.shape[1] // 2
    count = incoming.shape[1] // relay
    inner = row_scale * jnp.sum(incoming.astype(f32) * unscaled, axis=1, keepdims=True) / width
    returned = []
    for k in range(count):
        cols = slice(k * relay, (k + 1) * relay)
        back = dot(incoming[:, cols], products[cols, relay:], NT)
        returned.append(row_scale * (back - row_scale * inner * mixed[:, cols]))
    return inner, jnp.concatenate(returned, axis=1).astype(bf16)


def first_kernel(width, where, ins, outs, scratch):
    mix_blocks, payloads, (products, weights) = ins
    mix, ends, mix_gram, mix_recv, mix_send, square, sent = outs
    (gram,) = scratch
    codes = mix.shape[1]
    relay = products.shape[1] // 2
    parts = len(mix_blocks)
    cols = codes // parts
    for k in range(parts):
        at = pl.multiple_of((where[0] ^ k) * cols, cols)
        mix[:, pl.ds(at, cols)] = mix_blocks[k][...]
        ends[:, k * relay : (k + 1) * relay] = payloads[k][cols * codes // relay :, :]
        for j in range(codes // relay):
            piece = payloads[k][j * cols : (j + 1) * cols, :]
            gram[pl.ds(at, cols), j * relay : (j + 1) * relay] = piece

    def step(at):
        codes_here = mix[at, :]
        in_gram = dot(codes_here, gram[...], NN)
        sums = jnp.sum(in_gram * codes_here.astype(f32), axis=1, keepdims=True)
        in_relay = dot(codes_here, weights[...], NN)
        in_recv = in_relay[:, : parts * relay]
        in_send = in_relay[:, parts * relay :]
        mix_gram[at, :] = in_gram
        mix_recv[at, :] = in_recv
        mix_send[at, :] = in_send
        square[at, :] = sums
        mixed, unscaled, row_scale = forward(
            ends[at, :], in_recv, in_send, sums, products[...], width
        )
        sent[at, :] = (row_scale * unscaled).astype(bf16)

    by_rows(mix.shape[0], step)


def forward_kernel(width, turn, last, where, ins, outs, scratch):
    ((moved, received, ends, mix_recv, mix_send, square, products),) = ins
    live = where[2] == turn

    def step(at):
        values = jnp.where(live, moved[at, :], received[at, :])
        mixed, unscaled, row_scale = forward(
            values, mix_recv[at, :], mix_send[at, :], square[at, :], products[...], width
        )
        outs[0][at, :] = values
        outs[1][at, :] = (row_scale * unscaled).astype(bf16)
        if last:
            inner, returned = backward(
                ends[at, :], mixed, unscaled, row_scale, products[...], width
            )
            outs[2][at, :] = mixed
            outs[3][at, :] = unscaled
            outs[4][at, :] = row_scale
            outs[5][at, :] = returned

    by_rows(moved.shape[0], step)
    if last:
        outs[6][...] = outs[1][: outs[6].shape[0], : outs[6].shape[1]]


def backward_kernel(width, live_section, last, where, ins, outs, scratch):
    (moved, incoming, received, mixed, unscaled, row_scale, mix_gram, products, weights), = ins
    live = where[2] == live_section
    half = weights.shape[1] // 2

    def step(at):
        values = jnp.where(live, moved[at, :], incoming[at, :])
        scale = row_scale[at, :]
        inner, returned = backward(
            values, mixed[at, :], unscaled[at, :], scale, products[...], width
        )
        outs[0][at, :] = values
        outs[1][at, :] = returned
        if last:
            outs[2][at, :] = inner
            in_mixed = mix_gram[at, :] + dot(received[at, :], weights[:, :half], NT)
            back = dot(values, weights[:, half:], NT)
            outs[3][at, :] = (scale * (back - scale * inner * in_mixed)).astype(bf16)

    by_rows(moved.shape[0], step)
    if last:
        outs[4][...] = outs[1][: outs[4].shape[0], : outs[4].shape[1]]


def heads_kernel(where, ins, outs, scratch):
    (code_grad,), terms = ins
    tokens = outs[0].shape[0]
    fold_rows = terms[0][...].astype(f32)
    for term in terms[1:]:
        fold_rows = fold_rows + term[...].astype(f32)
    whole = dot(code_grad[...], fold_rows.astype(bf16), NT)
    for k, out in enumerate(outs):
        out[...] = whole[k * tokens : (k + 1) * tokens, :].astype(bf16)


def laid_kernel(where, ins, outs, scratch):
    (blocks,) = ins
    size = blocks[0].shape[1]
    for k, part in enumerate(blocks):
        at = pl.multiple_of((where[1] ^ k) * size, size)
        outs[0][:, pl.ds(at, size)] = part[...]


def head_kernel(where, ins, outs, scratch):
    heads, (code_grad, proj) = ins
    head_sum, enc_blocks = outs[0], outs[1:]
    (whole,) = scratch
    tokens = heads[0].shape[0]
    together = 4 if len(heads) % 4 == 0 else 1
    sums = None
    for first in range(0, len(heads), together):
        rows = slice(first * tokens, (first + together) * tokens)
        values = jnp.concatenate([h[...] for h in heads[first : first + together]])
        term = dot(code_grad[rows, :], values, TN)
        sums = term if sums is None else sums + term
    head_sum[...] = sums.astype(bf16)
    whole[...] = dot(head_sum[...], proj[...], NN)
    size = enc_blocks[0].shape[0]
    for k, out in enumerate(enc_blocks):
        at = (where[0] ^ k) * size
        out[...] = whole[pl.ds(pl.multiple_of(at, size), size), :].astype(bf16)


def proj_kernel(where, ins, outs, scratch):
    ((head_sum, enc),) = ins
    outs[0][...] = dot(head_sum[...], enc[...], TN).astype(bf16)


def feature_kernel(where, ins, outs, scratch):
    (mix, mix_cols, received, incoming, row_scale, inner, dec, recv, send, gain), = ins
    sums = scratch
    relay = recv.shape[0]
    size = sums[0].shape[0]
    cols = slice(None)
    if mix_cols.shape[1] > size:
        cols = pl.ds(pl.multiple_of(where[1] * size, size), size)
    for ref in sums:
        ref[...] = jnp.zeros_like(ref)

    def step(at):
        received_here = received[at, :relay]
        incoming_here = incoming[at, :relay]
        scale = row_scale[at, :]
        mixed = dot(mix[at, :], dec[...], NN) + dot(received_here, recv[...], NN)
        normed = mixed * scale
        out_rows = (normed * gain[...]).astype(bf16)
        grad_norm = dot(incoming_here, send[...], NT)
        grad_mixed = scale * (grad_norm * gain[...] - normed * inner[at, :])
        grad_mixed = grad_mixed.astype(bf16)
        sums[0][...] += dot(mix_cols[at, cols], grad_mixed, TN)
        sums[1][...] += jnp.sum(grad_norm * normed, axis=0, keepdims=True)
        sums[2][...] += dot(out_rows, incoming_here, TN)
        sums[3][...] += dot(received_here, grad_mixed, TN)

    by_rows(mix.shape[0], step)
    for out, ref in zip(outs, sums):
        out[...] = ref[...].astype(out.dtype)


def on_device(
    heads_out,
    out_proj,
    encoder,
    decoder,
    norm_gain,
    send_encoder,
    recv_decoder,
    input_code,
    code_cotangent,
):
    sections = lax.axis_size("pipe")
    section = lax.axis_index("pipe")
    groups = lax.axis_size("dp")
    parts = lax.axis_size("tensor")
    width = norm_gain.shape[1] * parts
    proj = out_proj[0]
    enc = encoder[0]
    dec = decoder[0]
    gain = norm_gain
    send = send_encoder[0]
    recv = recv_decoder[0]
    tokens, relay = input_code.shape
    codes, features = dec.shape
    cols = codes // parts
    rows = tokens * groups
    head_cols, model_cols = proj.shape
    where = jnp.stack([lax.axis_index("tensor"), lax.axis_index("dp"), section]).astype(jnp.int32)

    heads, pair = line_gathered(heads_out[0], "dp")
    end = jnp.where(section == 0, input_code, code_cotangent)
    ends = gathered(end, "dp")
    packs = run(
        gram_kernel,
        [like((cols * codes // (2 * relay) + codes + relay, 2 * relay))] * parts,
        where,
        [(dec, recv, send, gain)],
        scratch=[pltpu.VMEM((codes, codes), f32)],
        fetch=True,
    )
    half = like((head_cols // 2, codes))
    fold, fold_kept, fold_given = run(
        functools.partial(fold_kernel, groups),
        [like((head_cols, codes)), half, half],
        where,
        [(proj, enc)],
        fetch=True,
    )
    fold, _ = lax.optimization_barrier((fold, packs[0]))
    packs = scattered(packs, "tensor")

    partials = run(
        partial_kernel,
        [like((rows, cols))] * parts + [like((tokens, head_cols))] * (len(pair) // 2),
        where,
        [heads, pair, (fold,)],
        scratch=[pltpu.VMEM((min(groups, 4) * tokens, codes), f32)],
        flops=2 * rows * head_cols * codes,
    )
    partials, heads = list(partials[:parts]), [*heads, *partials[parts:]]
    partials[-1], *_ = lax.optimization_barrier((partials[-1], *packs, *ends))
    code_block = total(scattered(partials, "tensor"), where)
    wide = parts * relay
    packs, _ = lax.optimization_barrier((packs, code_block))
    payload, products, weights = run(
        setup_kernel,
        [
            like((cols * codes // relay + rows, relay)),
            like((wide, 2 * relay)),
            like((codes, 2 * wide)),
        ],
        where,
        [packs, ends],
    )
    payloads = gathered(payload, "tensor")
    mix_block = group_sum(code_block, payloads, "dp", where)
    fold_given, mix_block = lax.optimization_barrier((fold_given, mix_block))
    mix_blocks = gathered(mix_block, "tensor")

    square_flops = 2 * rows * codes * codes
    mix, ends, mix_gram, mix_recv, mix_send, square, sent = run(
        functools.partial(first_kernel, width),
        [
            like((rows, codes)),
            like((rows, wide)),
            like((rows, codes), f32),
            like((rows, wide), f32),
            like((rows, wide), f32),
            like((rows, 1), f32),
            like((rows, wide)),
        ],
        where,
        [mix_blocks, payloads, (products, weights)],
        scratch=[pltpu.VMEM((codes, codes), bf16)],
        flops=3 * square_flops,
    )
    fold_terms, sent = halved_sum(
        fold_kept, fold_given, sent, "dp", head_cols // groups, where
    )
    received = ends
    for turn in range(1, sections):
        last = turn == sections - 1
        shapes = [like((rows, wide)), like((rows, wide))]
        if last:
            shapes += [like((rows, wide), f32)] * 2 + [like((rows, 1), f32), like((rows, wide))]
            shapes += [like((tokens, relay))]
        moved = move(sent, "pipe", 1)
        results = run(
            functools.partial(forward_kernel, width, turn, last),
            shapes,
            where,
            [(moved, received, ends, mix_recv, mix_send, square, products)],
            flops=square_flops,
        )
        received, sent = results[:2]
    mixed, unscaled, row_scale, returned, sent = results[2:]
    incoming = ends
    for turn in range(1, sections):
        last = turn == sections - 1
        shapes = [like((rows, wide)), like((rows, wide))]
        if last:
            shapes += [like((rows, 1), f32), like((rows, codes))]
            shapes += [like((tokens, relay))]
        moved = move(returned, "pipe", -1)
        results = run(
            functools.partial(backward_kernel, width, sections - 1 - turn, last),
            shapes,
            where,
            [
                (
                    moved,
                    incoming,
                    received,
                    mixed,
                    unscaled,
                    row_scale,
                    mix_gram,
                    products,
                    weights,
                )
            ],
            flops=3 * square_flops,
        )
        incoming, returned = results[:2]
    inner, code_grad, returned = results[2:]

    head_sum, *enc_blocks = run(
        head_kernel,
        [like((codes, head_cols))] + [like((cols, model_cols))] * parts,
        where,
        [heads, (code_grad, proj)],
        scratch=[pltpu.VMEM((codes, model_cols), f32)],
        flops=2 * head_cols * codes * (rows + model_cols),
    )
    head_sum, mix, *enc_blocks = lax.optimization_barrier((head_sum, mix, *enc_blocks))
    enc_grad = total(scattered(enc_blocks, "tensor"), where)
    (proj_grad,) = run(proj_kernel, [like((head_cols, model_cols))], where, [(head_sum, enc)])
    shapes = [(codes // groups, features), (1, features), (features, relay), (relay, features)]
    dec_grad, gain_grad, send_grad, recv_grad = run(
        feature_kernel,
        [like(shape, f32 if k == 1 else bf16) for k, shape in enumerate(shapes)],
        where,
        [
            (
                mix,
                mix if codes // groups % 128 == 0 else block(mix, "dp", 1),
                received,
                incoming,
                row_scale,
                inner,
                dec,
                recv,
                send,
                gain,
            )
        ],
        scratch=[pltpu.VMEM(shape, f32) for shape in shapes],
    )
    fold_terms, _, _ = lax.optimization_barrier((fold_terms, proj_grad, dec_grad))
    head_blocks = run(
        heads_kernel,
        [like((tokens, head_cols // groups))] * groups,
        where,
        [(code_grad,), fold_terms],
    )
    head_blocks = scattered(head_blocks, "dp")
    if head_cols // groups % 128 == 0:
        (heads_grad,) = run(laid_kernel, [like((tokens, head_cols))], where, [head_blocks])
    else:
        heads_grad = ordered(head_blocks, "dp")
    return (
        sent[None],
        returned[None],
        heads_grad[None],
        proj_grad[None],
        enc_grad[None],
        dec_grad[None],
        gain_grad,
        send_grad[None],
        recv_grad[None],
    )


def solution(mesh):
    return jax.shard_map(
        on_device,
        mesh=mesh,
        in_specs=(
            P("pipe", "dp", "tensor"),
            P("pipe", "tensor", "dp"),
            P("pipe", None, "dp"),
            P("pipe", None, "tensor"),
            P("pipe", "tensor"),
            P("pipe", "tensor", None),
            P("pipe", None, "tensor"),
            P("dp", "tensor"),
            P("dp", "tensor"),
        ),
        out_specs=(
            P("pipe", "dp", "tensor"),
            P("pipe", "dp", "tensor"),
            P("pipe", "dp", "tensor"),
            P("pipe", "tensor", "dp"),
            P("pipe", "tensor", "dp"),
            P("pipe", "dp", "tensor"),
            P("pipe", "tensor"),
            P("pipe", "tensor", None),
            P("pipe", None, "tensor"),
        ),
        check_vma=False,
    )
```

```python
import functools

import jax
import jax.numpy as jnp
from jax import lax
from jax.experimental import pallas as pl
from jax.experimental.pallas import tpu as pltpu
from jax.sharding import PartitionSpec as P

epsilon = 1e-05
f32 = jnp.float32
bf16 = jnp.bfloat16
NN = ((1,), (0,))
NT = ((1,), (1,))
TN = ((0,), (0,))


def swap(shard, axis, by):
    return lax.ppermute(shard, axis, [(i, i ^ by) for i in range(lax.axis_size(axis))])


def move(shard, axis, by):
    devices = lax.axis_size(axis)
    pairs = [(i, i + by) for i in range(devices) if 0 <= i + by < devices]
    return lax.ppermute(shard, axis, pairs)


def gathered(shard, axis):
    return [shard] + [swap(shard, axis, k) for k in range(1, lax.axis_size(axis))]


def line_gathered(shard, small, axis):
    if lax.axis_size(axis) != 4:
        return gathered(shard, axis), [], gathered(small, axis)
    far, near = swap(shard, axis, 2), swap(shard, axis, 1)
    beside = swap(small, axis, 1)
    shard, far, near, beside = lax.optimization_barrier((shard, far, near, beside))
    across = lax.ppermute(shard, axis, [(1, 2), (2, 1)])
    passed = lax.ppermute(far, axis, [(1, 0), (2, 3)])
    others = swap(jnp.concatenate([small, beside]), axis, 2)
    return [shard, near, far], [across, passed], [small, beside, others]


def scattered(blocks, axis):
    return [blocks[0]] + [swap(blocks[k], axis, k) for k in range(1, len(blocks))]


def group_sum(rows, after, axis, where):
    groups = lax.axis_size(axis)
    step = groups // 2
    while step:
        other = swap(rows, axis, step)
        if step == 1:
            other, *_ = lax.optimization_barrier((other, *after))
        kernel = functools.partial(moved_sum_kernel, groups, step)
        (rows,) = run(kernel, [like(rows.shape)], where, [(rows, other)])
        step //= 2
    return rows


def halved(mine, other, size, where):
    half = like((mine.shape[0] // 2, mine.shape[1]))
    return run(functools.partial(halved_kernel, size), [half, half], where, [(mine, other)])


def total(blocks, where, flops=0):
    return run(total_kernel, [like(blocks[0].shape)], where, [blocks], flops=flops)[0]


def ordered(blocks, axis):
    step = 1
    while step < len(blocks):
        odd = (lax.axis_index(axis) & step) > 0
        blocks = [jnp.where(odd, blocks[k ^ step], part) for k, part in enumerate(blocks)]
        step *= 2
    return jnp.concatenate(blocks, axis=1)


def block(array, axis, dim):
    size = array.shape[dim] // lax.axis_size(axis)
    return lax.dynamic_slice_in_dim(array, lax.axis_index(axis) * size, size, dim)


def dot(left, right, over):
    return lax.dot_general(left, right, (over, ((), ())), preferred_element_type=f32)


def run(kernel, results, where, groups_of_args, scratch=(), flops=0, fetch=False):
    counts = [len(group) for group in groups_of_args]
    flat = [array for group in groups_of_args for array in group]
    out_count = len(results)
    scratch = list(scratch)
    own = len(scratch)
    space = pltpu.HBM if fetch else pltpu.VMEM
    if fetch:
        scratch += [pltpu.VMEM(array.shape, array.dtype) for array in flat]
        scratch.append(pltpu.SemaphoreType.DMA((len(flat),)))

    def body(where_ref, *refs):
        args, refs = refs[: len(flat)], refs[len(flat) :]
        outs, refs = refs[:out_count], refs[out_count:]
        if fetch:
            held, arrived = refs[own:-1], refs[-1]
            copies = [
                pltpu.make_async_copy(arg, here, arrived.at[k])
                for k, (arg, here) in enumerate(zip(args, held))
            ]
            for copy in copies:
                copy.start()
            for copy in copies:
                copy.wait()
            args = held
        ins, at = [], 0
        for count in counts:
            ins.append(args[at : at + count])
            at += count
        kernel(where_ref, ins, outs, refs[:own])

    if fetch:
        flat = [pltpu.with_memory_space_constraint(array, pltpu.HBM) for array in flat]
    size = sum(a.size * a.dtype.itemsize for a in list(flat) + list(results))
    limit = (10 << 20) if size < (10 << 20) else size + (12 << 20)
    return pl.pallas_call(
        body,
        out_shape=[jax.ShapeDtypeStruct(r.shape, r.dtype) for r in results],
        in_specs=[pl.BlockSpec(memory_space=pltpu.SMEM)]
        + [pl.BlockSpec(memory_space=space)] * len(flat),
        out_specs=[pl.BlockSpec(memory_space=pltpu.VMEM)] * out_count,
        scratch_shapes=scratch,
        compiler_params=pltpu.CompilerParams(vmem_limit_bytes=limit),
        cost_estimate=pl.CostEstimate(
            flops=flops, bytes_accessed=size if flops else 0, transcendentals=0
        ),
    )(where, *flat)


def like(shape, dtype=bf16):
    return jax.ShapeDtypeStruct(shape, dtype)


def by_rows(rows, step):
    chunk = min(rows, 512)
    if rows == chunk:
        step(slice(0, rows))
        return

    @pl.loop(0, rows // chunk)
    def _(index):
        step(pl.ds(pl.multiple_of(index * chunk, chunk), chunk))


def total_kernel(where, ins, outs, scratch):
    (blocks,) = ins
    result = blocks[0][...].astype(f32)
    for part in blocks[1:]:
        result = result + part[...].astype(f32)
    outs[0][...] = result.astype(bf16)


def moved_sum_kernel(groups, step, where, ins, outs, scratch):
    ((mine, other),) = ins
    size = mine.shape[0] // groups
    for k in range(groups):
        here = slice(k * size, (k + 1) * size)
        there = slice((k ^ step) * size, ((k ^ step) + 1) * size)
        value = mine[here, :].astype(f32) + other[there, :].astype(f32)
        outs[0][here, :] = value.astype(bf16)


def halved_kernel(size, where, ins, outs, scratch):
    ((mine, other),) = ins
    for k in range(mine.shape[0] // size):
        here = slice(k * size, (k + 1) * size)
        there = slice(k // 2 * size, (k // 2 + 1) * size)
        value = mine[here, :].astype(f32) + other[here, :].astype(f32)
        outs[k % 2][there, :] = value.astype(bf16)


def gram_kernel(where, ins, outs, scratch):
    ((dec, recv, send, gain),) = ins
    (whole,) = scratch
    codes, relay = dec.shape[0], recv.shape[0]
    cols = codes // len(outs)
    wide = 2 * relay
    head = cols * codes // wide
    whole[...] = dot(dec[...], dec[...], NT)
    for k, out in enumerate(outs):
        rows = pl.ds(pl.multiple_of((where[0] ^ k) * cols, cols), cols)
        for j in range(codes // wide):
            piece = whole[rows, j * wide : (j + 1) * wide]
            out[j * cols : (j + 1) * cols, :] = piece.astype(bf16)
    for ref, rows in ((dec, slice(head, head + codes)), (recv, slice(head + codes, None))):
        values = ref[...]
        gained = (values.astype(f32) * gain[...]).astype(bf16)
        plain = dot(values, recv[...], NT).astype(bf16)
        scaled = dot(gained, send[...], NN).astype(bf16)
        for out in outs:
            out[rows, :relay] = plain
            out[rows, relay:] = scaled


def setup_kernel(where, ins, outs, scratch):
    packs, ends = ins
    payload, products, weights = outs
    parts = len(packs)
    wide = products.shape[1]
    relay = wide // 2
    codes = weights.shape[0]
    cols = codes // parts
    head = cols * codes // wide
    for j in range(codes // wide):
        rows = slice(j * cols, (j + 1) * cols)
        gram = packs[0][rows, :].astype(f32)
        for pack in packs[1:]:
            gram = gram + pack[rows, :].astype(f32)
        gram = gram.astype(bf16)
        payload[2 * j * cols : (2 * j + 1) * cols, :] = gram[:, :relay]
        payload[(2 * j + 1) * cols : (2 * j + 2) * cols, :] = gram[:, relay:]
    start = 2 * head
    for end in ends:
        payload[start : start + end.shape[0], :] = end[...]
        start += end.shape[0]
    for k, pack in enumerate(packs):
        here = slice(k * relay, (k + 1) * relay)
        products[here, :] = pack[head + codes :, :]
        weights[:, here] = pack[head : head + codes, :relay]
        there = slice((parts + k) * relay, (parts + k + 1) * relay)
        weights[:, there] = pack[head : head + codes, relay:]


def fold_kernel(groups, where, ins, outs, scratch):
    ((proj, enc),) = ins
    fold = outs[0]
    size = fold.shape[0] // groups
    fold[...] = dot(proj[...], enc[...], NT).astype(bf16)
    for k in range(groups):
        there = slice(k // 2 * size, (k // 2 + 1) * size)
        here = pl.ds(pl.multiple_of((where[1] ^ k) * size, size), size)
        outs[1 + k % 2][there, :] = fold[here, :]


def partial_kernel(where, ins, outs, scratch):
    heads, pair, (fold,) = ins
    (whole,) = scratch
    if pair:
        outs, last = outs[:-1], outs[-1]
        last[...] = pair[0][...] + pair[1][...]
        heads = [*heads, last]
    tokens = heads[0].shape[0]
    cols = outs[0].shape[1]
    parts = len(outs)
    together = 4 if len(heads) % 4 == 0 else 1
    for first in range(0, len(heads), together):
        rows = slice(first * tokens, (first + together) * tokens)
        values = jnp.concatenate([h[...] for h in heads[first : first + together]])
        whole[...] = dot(values, fold[...], NN)
        for k in range(parts):
            at = (where[0] ^ k) * cols
            outs[k][rows, :] = whole[:, pl.ds(pl.multiple_of(at, cols), cols)].astype(bf16)


def forward(received, code_mix, code_send, square, products, width):
    relay = products.shape[1] // 2
    count = received.shape[1] // relay
    mixed, unscaled = [], []
    for k in range(count):
        cols = slice(k * relay, (k + 1) * relay)
        both = dot(received[:, cols], products[cols, :], NN)
        mixed.append(code_mix[:, cols] + both[:, :relay])
        unscaled.append(code_send[:, cols] + both[:, relay:])
    mixed = jnp.concatenate(mixed, axis=1)
    unscaled = jnp.concatenate(unscaled, axis=1)
    totals = square + jnp.sum(received.astype(f32) * (code_mix + mixed), axis=1, keepdims=True)
    row_scale = lax.rsqrt(jnp.maximum(totals, 0.0) / width + epsilon)
    return mixed, unscaled, row_scale


def backward(incoming, mixed, unscaled, row_scale, products, width):
    relay = products.shape[1] // 2
    count = incoming.shape[1] // relay
    inner = row_scale * jnp.sum(incoming.astype(f32) * unscaled, axis=1, keepdims=True) / width
    returned = []
    for k in range(count):
        cols = slice(k * relay, (k + 1) * relay)
        back = dot(incoming[:, cols], products[cols, relay:], NT)
        returned.append(row_scale * (back - row_scale * inner * mixed[:, cols]))
    return inner, jnp.concatenate(returned, axis=1).astype(bf16)


def first_kernel(width, where, ins, outs, scratch):
    mix_blocks, payloads, (products, weights) = ins
    mix, ends, mix_gram, mix_recv, mix_send, square, sent = outs
    (gram,) = scratch
    codes = mix.shape[1]
    relay = products.shape[1] // 2
    parts = len(mix_blocks)
    cols = codes // parts
    for k in range(parts):
        at = pl.multiple_of((where[0] ^ k) * cols, cols)
        mix[:, pl.ds(at, cols)] = mix_blocks[k][...]
        ends[:, k * relay : (k + 1) * relay] = payloads[k][cols * codes // relay :, :]
        for j in range(codes // relay):
            piece = payloads[k][j * cols : (j + 1) * cols, :]
            gram[pl.ds(at, cols), j * relay : (j + 1) * relay] = piece

    def step(at):
        codes_here = mix[at, :]
        in_gram = dot(codes_here, gram[...], NN)
        sums = jnp.sum(in_gram * codes_here.astype(f32), axis=1, keepdims=True)
        in_relay = dot(codes_here, weights[...], NN)
        in_recv = in_relay[:, : parts * relay]
        in_send = in_relay[:, parts * relay :]
        mix_gram[at, :] = in_gram
        mix_recv[at, :] = in_recv
        mix_send[at, :] = in_send
        square[at, :] = sums
        mixed, unscaled, row_scale = forward(
            ends[at, :], in_recv, in_send, sums, products[...], width
        )
        sent[at, :] = (row_scale * unscaled).astype(bf16)

    by_rows(mix.shape[0], step)


def forward_kernel(width, turn, last, where, ins, outs, scratch):
    ((moved, received, ends, mix_recv, mix_send, square, products),) = ins
    live = where[2] == turn

    def step(at):
        values = jnp.where(live, moved[at, :], received[at, :])
        mixed, unscaled, row_scale = forward(
            values, mix_recv[at, :], mix_send[at, :], square[at, :], products[...], width
        )
        outs[0][at, :] = values
        outs[1][at, :] = (row_scale * unscaled).astype(bf16)
        if last:
            inner, returned = backward(
                ends[at, :], mixed, unscaled, row_scale, products[...], width
            )
            outs[2][at, :] = mixed
            outs[3][at, :] = unscaled
            outs[4][at, :] = row_scale
            outs[5][at, :] = returned

    by_rows(moved.shape[0], step)
    if last:
        outs[6][...] = outs[1][: outs[6].shape[0], : outs[6].shape[1]]


def backward_kernel(width, live_section, last, where, ins, outs, scratch):
    (moved, incoming, received, mixed, unscaled, row_scale, mix_gram, products, weights), = ins
    live = where[2] == live_section
    half = weights.shape[1] // 2

    def step(at):
        values = jnp.where(live, moved[at, :], incoming[at, :])
        scale = row_scale[at, :]
        inner, returned = backward(
            values, mixed[at, :], unscaled[at, :], scale, products[...], width
        )
        outs[0][at, :] = values
        outs[1][at, :] = returned
        if last:
            outs[2][at, :] = inner
            in_mixed = mix_gram[at, :] + dot(received[at, :], weights[:, :half], NT)
            back = dot(values, weights[:, half:], NT)
            outs[3][at, :] = (scale * (back - scale * inner * in_mixed)).astype(bf16)

    by_rows(moved.shape[0], step)
    if last:
        outs[4][...] = outs[1][: outs[4].shape[0], : outs[4].shape[1]]


def heads_kernel(where, ins, outs, scratch):
    ((code_grad, fold_rows),) = ins
    tokens = outs[0].shape[0]
    whole = dot(code_grad[...], fold_rows[...], NT)
    for k, out in enumerate(outs):
        out[...] = whole[k * tokens : (k + 1) * tokens, :].astype(bf16)


def laid_kernel(where, ins, outs, scratch):
    (blocks,) = ins
    size = blocks[0].shape[1]
    for k, part in enumerate(blocks):
        at = pl.multiple_of((where[1] ^ k) * size, size)
        outs[0][:, pl.ds(at, size)] = part[...]


def head_kernel(where, ins, outs, scratch):
    heads, (code_grad, proj) = ins
    enc_blocks = outs
    (whole,) = scratch
    tokens = heads[0].shape[0]
    together = 4 if len(heads) % 4 == 0 else 1
    sums = None
    for first in range(0, len(heads), together):
        rows = slice(first * tokens, (first + together) * tokens)
        values = jnp.concatenate([h[...] for h in heads[first : first + together]])
        term = dot(code_grad[rows, :], values, TN)
        sums = term if sums is None else sums + term
    whole[...] = dot(sums.astype(bf16), proj[...], NN)
    size = enc_blocks[0].shape[0]
    for k, out in enumerate(enc_blocks):
        at = (where[0] ^ k) * size
        out[...] = whole[pl.ds(pl.multiple_of(at, size), size), :].astype(bf16)


def turn_kernel(where, ins, outs, scratch):
    (heads,) = ins
    tokens = heads[0].shape[0]
    for k, part in enumerate(heads):
        outs[0][:, k * tokens : (k + 1) * tokens] = part[...].T


def proj_kernel(where, ins, outs, scratch):
    ((turned, code_grad, enc),) = ins
    head_sum = dot(turned[...], code_grad[...], NN).astype(bf16)
    outs[0][...] = dot(head_sum, enc[...], NN).astype(bf16)


def feature_kernel(where, ins, outs, scratch):
    (mix, mix_cols, received, incoming, row_scale, inner, dec, recv, send, gain), = ins
    sums = scratch
    relay = recv.shape[0]
    size = sums[0].shape[0]
    cols = slice(None)
    if mix_cols.shape[1] > size:
        cols = pl.ds(pl.multiple_of(where[1] * size, size), size)
    for ref in sums:
        ref[...] = jnp.zeros_like(ref)

    def step(at):
        received_here = received[at, :relay]
        incoming_here = incoming[at, :relay]
        scale = row_scale[at, :]
        mixed = dot(mix[at, :], dec[...], NN) + dot(received_here, recv[...], NN)
        normed = mixed * scale
        out_rows = (normed * gain[...]).astype(bf16)
        grad_norm = dot(incoming_here, send[...], NT)
        grad_mixed = scale * (grad_norm * gain[...] - normed * inner[at, :])
        grad_mixed = grad_mixed.astype(bf16)
        sums[0][...] += dot(mix_cols[at, cols], grad_mixed, TN)
        sums[1][...] += jnp.sum(grad_norm * normed, axis=0, keepdims=True)
        sums[2][...] += dot(out_rows, incoming_here, TN)
        sums[3][...] += dot(received_here, grad_mixed, TN)

    by_rows(mix.shape[0], step)
    for out, ref in zip(outs, sums):
        out[...] = ref[...].astype(out.dtype)


def on_device(
    heads_out,
    out_proj,
    encoder,
    decoder,
    norm_gain,
    send_encoder,
    recv_decoder,
    input_code,
    code_cotangent,
):
    sections = lax.axis_size("pipe")
    section = lax.axis_index("pipe")
    groups = lax.axis_size("dp")
    parts = lax.axis_size("tensor")
    width = norm_gain.shape[1] * parts
    proj = out_proj[0]
    enc = encoder[0]
    dec = decoder[0]
    gain = norm_gain
    send = send_encoder[0]
    recv = recv_decoder[0]
    tokens, relay = input_code.shape
    codes, features = dec.shape
    cols = codes // parts
    rows = tokens * groups
    head_cols, model_cols = proj.shape
    where = jnp.stack([lax.axis_index("tensor"), lax.axis_index("dp"), section]).astype(jnp.int32)

    end = jnp.where(section == 0, input_code, code_cotangent)
    heads, pair, ends = line_gathered(heads_out[0], end, "dp")
    packs = run(
        gram_kernel,
        [like((cols * codes // (2 * relay) + codes + relay, 2 * relay))] * parts,
        where,
        [(dec, recv, send, gain)],
        scratch=[pltpu.VMEM((codes, codes), f32)],
        fetch=True,
    )
    half = like((head_cols // 2, codes))
    fold, fold_kept, fold_given = run(
        functools.partial(fold_kernel, groups),
        [like((head_cols, codes)), half, half],
        where,
        [(proj, enc)],
        fetch=True,
    )
    fold, _ = lax.optimization_barrier((fold, packs[0]))
    packs = scattered(packs, "tensor")

    partials = run(
        partial_kernel,
        [like((rows, cols))] * parts + [like((tokens, head_cols))] * (len(pair) // 2),
        where,
        [heads, pair, (fold,)],
        scratch=[pltpu.VMEM((min(groups, 4) * tokens, codes), f32)],
        flops=2 * rows * head_cols * codes,
    )
    partials, heads = list(partials[:parts]), [*heads, *partials[parts:]]
    partials[-1], *_ = lax.optimization_barrier((partials[-1], *packs, *ends))
    fold_given, partials = lax.optimization_barrier((fold_given, partials))
    fold_other = swap(fold_given, "dp", 1)
    code_block = total(scattered(partials, "tensor"), where)
    code_block, fold_other = lax.optimization_barrier((code_block, fold_other))
    fold_terms = halved(fold_kept, fold_other, head_cols // groups, where)
    wide = parts * relay
    packs, _ = lax.optimization_barrier((packs, code_block))
    payload, products, weights = run(
        setup_kernel,
        [
            like((cols * codes // relay + rows, relay)),
            like((wide, 2 * relay)),
            like((codes, 2 * wide)),
        ],
        where,
        [packs, ends],
    )
    payloads = gathered(payload, "tensor")
    (turned,) = run(turn_kernel, [like((head_cols, rows))], where, [heads])
    mix_block = group_sum(code_block, [*payloads, *fold_terms, turned], "dp", where)
    mix_block, fold_terms = lax.optimization_barrier((mix_block, fold_terms))
    mix_blocks = gathered(mix_block, "tensor")

    square_flops = 2 * rows * codes * codes
    mix, ends, mix_gram, mix_recv, mix_send, square, sent = run(
        functools.partial(first_kernel, width),
        [
            like((rows, codes)),
            like((rows, wide)),
            like((rows, codes), f32),
            like((rows, wide), f32),
            like((rows, wide), f32),
            like((rows, 1), f32),
            like((rows, wide)),
        ],
        where,
        [mix_blocks, payloads, (products, weights)],
        scratch=[pltpu.VMEM((codes, codes), bf16)],
        flops=3 * square_flops,
    )
    step = 2
    while step < groups:
        kept, given = fold_terms
        other = swap(given, "dp", step)
        step *= 2
        if step < groups:
            fold_terms = halved(kept, other, head_cols // groups, where)
        else:
            fold_rows = total([kept, other], where, flops=1 << 33)
    received = ends
    for turn in range(1, sections):
        last = turn == sections - 1
        shapes = [like((rows, wide)), like((rows, wide))]
        if last:
            shapes += [like((rows, wide), f32)] * 2 + [like((rows, 1), f32), like((rows, wide))]
            shapes += [like((tokens, relay))]
        moved = move(sent, "pipe", 1)
        if turn == 1:
            moved, fold_rows = lax.optimization_barrier((moved, fold_rows))
        results = run(
            functools.partial(forward_kernel, width, turn, last),
            shapes,
            where,
            [(moved, received, ends, mix_recv, mix_send, square, products)],
            flops=square_flops,
        )
        received, sent = results[:2]
    mixed, unscaled, row_scale, returned, sent = results[2:]
    incoming = ends
    for turn in range(1, sections):
        last = turn == sections - 1
        shapes = [like((rows, wide)), like((rows, wide))]
        if last:
            shapes += [like((rows, 1), f32), like((rows, codes))]
            shapes += [like((tokens, relay))]
        moved = move(returned, "pipe", -1)
        results = run(
            functools.partial(backward_kernel, width, sections - 1 - turn, last),
            shapes,
            where,
            [
                (
                    moved,
                    incoming,
                    received,
                    mixed,
                    unscaled,
                    row_scale,
                    mix_gram,
                    products,
                    weights,
                )
            ],
            flops=3 * square_flops,
        )
        incoming, returned = results[:2]
    inner, code_grad, returned = results[2:]

    enc_blocks = run(
        head_kernel,
        [like((cols, model_cols))] * parts,
        where,
        [heads, (code_grad, proj)],
        scratch=[pltpu.VMEM((codes, model_cols), f32)],
        flops=2 * head_cols * codes * (rows + model_cols),
    )
    code_grad, mix, turned, enc_blocks = lax.optimization_barrier(
        (code_grad, mix, turned, enc_blocks)
    )
    enc_blocks = scattered(enc_blocks, "tensor")
    head_blocks = run(
        heads_kernel,
        [like((tokens, head_cols // groups))] * groups,
        where,
        [(code_grad, fold_rows)],
    )
    *head_blocks, mix, turned = lax.optimization_barrier((*head_blocks, mix, turned))
    head_blocks = scattered(head_blocks, "dp")
    (proj_grad,) = run(
        proj_kernel, [like((head_cols, model_cols))], where, [(turned, code_grad, enc)]
    )
    shapes = [(codes // groups, features), (1, features), (features, relay), (relay, features)]
    dec_grad, gain_grad, send_grad, recv_grad = run(
        feature_kernel,
        [like(shape, f32 if k == 1 else bf16) for k, shape in enumerate(shapes)],
        where,
        [
            (
                mix,
                mix if codes // groups % 128 == 0 else block(mix, "dp", 1),
                received,
                incoming,
                row_scale,
                inner,
                dec,
                recv,
                send,
                gain,
            )
        ],
        scratch=[pltpu.VMEM(shape, f32) for shape in shapes],
    )
    enc_grad = total(enc_blocks, where)
    if head_cols // groups % 128 == 0:
        (heads_grad,) = run(laid_kernel, [like((tokens, head_cols))], where, [head_blocks])
    else:
        heads_grad = ordered(head_blocks, "dp")
    return (
        sent[None],
        returned[None],
        heads_grad[None],
        proj_grad[None],
        enc_grad[None],
        dec_grad[None],
        gain_grad,
        send_grad[None],
        recv_grad[None],
    )


def solution(mesh):
    return jax.shard_map(
        on_device,
        mesh=mesh,
        in_specs=(
            P("pipe", "dp", "tensor"),
            P("pipe", "tensor", "dp"),
            P("pipe", None, "dp"),
            P("pipe", None, "tensor"),
            P("pipe", "tensor"),
            P("pipe", "tensor", None),
            P("pipe", None, "tensor"),
            P("dp", "tensor"),
            P("dp", "tensor"),
        ),
        out_specs=(
            P("pipe", "dp", "tensor"),
            P("pipe", "dp", "tensor"),
            P("pipe", "dp", "tensor"),
            P("pipe", "tensor", "dp"),
            P("pipe", "tensor", "dp"),
            P("pipe", "dp", "tensor"),
            P("pipe", "tensor"),
            P("pipe", "tensor", None),
            P("pipe", None, "tensor"),
        ),
        check_vma=False,
    )
```

```python
import functools

import jax
import jax.numpy as jnp
from jax import lax
from jax.experimental import pallas as pl
from jax.experimental.pallas import tpu as pltpu
from jax.sharding import PartitionSpec as P

epsilon = 1e-05
f32 = jnp.float32
bf16 = jnp.bfloat16
NN = ((1,), (0,))
NT = ((1,), (1,))
TN = ((0,), (0,))


def swap(shard, axis, by):
    return lax.ppermute(shard, axis, [(i, i ^ by) for i in range(lax.axis_size(axis))])


def move(shard, axis, by):
    devices = lax.axis_size(axis)
    pairs = [(i, i + by) for i in range(devices) if 0 <= i + by < devices]
    return lax.ppermute(shard, axis, pairs)


def gathered(shard, axis):
    return [shard] + [swap(shard, axis, k) for k in range(1, lax.axis_size(axis))]


def line_gathered(shard, small, axis):
    if lax.axis_size(axis) != 4:
        return gathered(shard, axis), [], gathered(small, axis)
    far, near = swap(shard, axis, 2), swap(shard, axis, 1)
    beside = swap(small, axis, 1)
    shard, far, near, beside = lax.optimization_barrier((shard, far, near, beside))
    across = lax.ppermute(shard, axis, [(1, 2), (2, 1)])
    passed = lax.ppermute(far, axis, [(1, 0), (2, 3)])
    both = jnp.concatenate([small, beside])
    both, across, passed = lax.optimization_barrier((both, across, passed))
    return [shard, near, far], [across, passed], [small, beside, swap(both, axis, 2)]


def scattered(blocks, axis):
    return [blocks[0]] + [swap(blocks[k], axis, k) for k in range(1, len(blocks))]


def group_sum(rows, after, axis, where):
    groups = lax.axis_size(axis)
    step = groups // 2
    while step:
        other = swap(rows, axis, step)
        if step == 1:
            other, *_ = lax.optimization_barrier((other, *after))
        kernel = functools.partial(moved_sum_kernel, groups, step)
        (rows,) = run(kernel, [like(rows.shape)], where, [(rows, other)])
        step //= 2
    return rows


def exchanged(kept, given, size, axis):
    count = lax.axis_size(axis)
    parts = [[(part, 0) for part in kept]]
    step = 1
    while True:
        arrived = swap(given, axis, step)
        left = count // (2 * step)
        parts += [
            [(arrived, (j * left + k) * size) for k in range(left)] for j in range(len(parts))
        ]
        step *= 2
        if step == count:
            return [part[0] for part in parts]
        given = [array[row : row + size] for part in parts for array, row in part[1::2]]
        given = jnp.concatenate(given)
        parts = [part[::2] for part in parts]


def halved(mine, other, size, where):
    half = like((mine.shape[0] // 2, mine.shape[1]))
    return run(functools.partial(halved_kernel, size), [half, half], where, [(mine, other)])


def total(blocks, where, flops=0):
    return run(total_kernel, [like(blocks[0].shape)], where, [blocks], flops=flops)[0]


def ordered(blocks, axis):
    step = 1
    while step < len(blocks):
        odd = (lax.axis_index(axis) & step) > 0
        blocks = [jnp.where(odd, blocks[k ^ step], part) for k, part in enumerate(blocks)]
        step *= 2
    return jnp.concatenate(blocks, axis=1)


def block(array, axis, dim):
    size = array.shape[dim] // lax.axis_size(axis)
    return lax.dynamic_slice_in_dim(array, lax.axis_index(axis) * size, size, dim)


def dot(left, right, over):
    return lax.dot_general(left, right, (over, ((), ())), preferred_element_type=f32)


def run(kernel, results, where, groups_of_args, scratch=(), flops=0, fetch=False, store=False):
    counts = [len(group) for group in groups_of_args]
    flat = [array for group in groups_of_args for array in group]
    out_count = len(results)
    scratch = list(scratch)
    own = len(scratch)
    space = pltpu.HBM if fetch else pltpu.VMEM
    if fetch:
        scratch += [pltpu.VMEM(array.shape, array.dtype) for array in flat]
        scratch.append(pltpu.SemaphoreType.DMA((len(flat),)))

    def body(where_ref, *refs):
        args, refs = refs[: len(flat)], refs[len(flat) :]
        outs, refs = refs[:out_count], refs[out_count:]
        if fetch:
            held, arrived = refs[own:-1], refs[-1]
            copies = [
                pltpu.make_async_copy(arg, here, arrived.at[k])
                for k, (arg, here) in enumerate(zip(args, held))
            ]
            for copy in copies:
                copy.start()
            for copy in copies:
                copy.wait()
            args = held
        ins, at = [], 0
        for count in counts:
            ins.append(args[at : at + count])
            at += count
        kernel(where_ref, ins, outs, refs[:own])

    if fetch:
        flat = [pltpu.with_memory_space_constraint(array, pltpu.HBM) for array in flat]
    size = sum(a.size * a.dtype.itemsize for a in list(flat) + list(results))
    limit = (10 << 20) if size < (10 << 20) else size + (12 << 20)
    return pl.pallas_call(
        body,
        out_shape=[jax.ShapeDtypeStruct(r.shape, r.dtype) for r in results],
        in_specs=[pl.BlockSpec(memory_space=pltpu.SMEM)]
        + [pl.BlockSpec(memory_space=space)] * len(flat),
        out_specs=[pl.BlockSpec(memory_space=pltpu.HBM if store else pltpu.VMEM)] * out_count,
        scratch_shapes=scratch,
        compiler_params=pltpu.CompilerParams(vmem_limit_bytes=limit),
        cost_estimate=pl.CostEstimate(
            flops=flops, bytes_accessed=size if flops else 0, transcendentals=0
        ),
    )(where, *flat)


def like(shape, dtype=bf16):
    return jax.ShapeDtypeStruct(shape, dtype)


def by_rows(rows, step):
    chunk = min(rows, 512)
    if rows == chunk:
        step(slice(0, rows))
        return

    @pl.loop(0, rows // chunk)
    def _(index):
        step(pl.ds(pl.multiple_of(index * chunk, chunk), chunk))


def total_kernel(where, ins, outs, scratch):
    (blocks,) = ins
    result = blocks[0][...].astype(f32)
    for part in blocks[1:]:
        result = result + part[...].astype(f32)
    outs[0][...] = result.astype(bf16)


def moved_sum_kernel(groups, step, where, ins, outs, scratch):
    ((mine, other),) = ins
    size = mine.shape[0] // groups
    for k in range(groups):
        here = slice(k * size, (k + 1) * size)
        there = slice((k ^ step) * size, ((k ^ step) + 1) * size)
        value = mine[here, :].astype(f32) + other[there, :].astype(f32)
        outs[0][here, :] = value.astype(bf16)


def halved_kernel(size, where, ins, outs, scratch):
    ((mine, other),) = ins
    for k in range(mine.shape[0] // size):
        here = slice(k * size, (k + 1) * size)
        there = slice(k // 2 * size, (k // 2 + 1) * size)
        value = mine[here, :].astype(f32) + other[here, :].astype(f32)
        outs[k % 2][there, :] = value.astype(bf16)


def gram_kernel(where, ins, outs, scratch):
    ((dec, recv, send, gain),) = ins
    (whole,) = scratch
    codes, relay = dec.shape[0], recv.shape[0]
    cols = codes // len(outs)
    wide = 2 * relay
    head = cols * codes // wide
    whole[...] = dot(dec[...], dec[...], NT)
    for k, out in enumerate(outs):
        rows = pl.ds(pl.multiple_of((where[0] ^ k) * cols, cols), cols)
        for j in range(codes // wide):
            piece = whole[rows, j * wide : (j + 1) * wide]
            out[j * cols : (j + 1) * cols, :] = piece.astype(bf16)
    for ref, rows in ((dec, slice(head, head + codes)), (recv, slice(head + codes, None))):
        values = ref[...]
        gained = (values.astype(f32) * gain[...]).astype(bf16)
        plain = dot(values, recv[...], NT).astype(bf16)
        scaled = dot(gained, send[...], NN).astype(bf16)
        for out in outs:
            out[rows, :relay] = plain
            out[rows, relay:] = scaled


def setup_kernel(where, ins, outs, scratch):
    packs, ends = ins
    payload, products, weights = outs
    parts = len(packs)
    wide = products.shape[1]
    relay = wide // 2
    codes = weights.shape[0]
    cols = codes // parts
    head = cols * codes // wide
    for j in range(codes // wide):
        rows = slice(j * cols, (j + 1) * cols)
        gram = packs[0][rows, :].astype(f32)
        for pack in packs[1:]:
            gram = gram + pack[rows, :].astype(f32)
        gram = gram.astype(bf16)
        payload[2 * j * cols : (2 * j + 1) * cols, :] = gram[:, :relay]
        payload[(2 * j + 1) * cols : (2 * j + 2) * cols, :] = gram[:, relay:]
    start = 2 * head
    for end in ends:
        payload[start : start + end.shape[0], :] = end[...]
        start += end.shape[0]
    for k, pack in enumerate(packs):
        here = slice(k * relay, (k + 1) * relay)
        products[here, :] = pack[head + codes :, :]
        weights[:, here] = pack[head : head + codes, :relay]
        there = slice((parts + k) * relay, (parts + k + 1) * relay)
        weights[:, there] = pack[head : head + codes, relay:]


def fold_kernel(groups, where, ins, outs, scratch):
    ((proj, enc),) = ins
    fold = outs[0]
    size = fold.shape[0] // groups
    fold[...] = dot(proj[...], enc[...], NT).astype(bf16)
    for k in range(groups):
        there = slice(k // 2 * size, (k // 2 + 1) * size)
        here = pl.ds(pl.multiple_of((where[1] ^ k) * size, size), size)
        outs[1 + k % 2][there, :] = fold[here, :]


def partial_kernel(where, ins, outs, scratch):
    heads, pair, (fold,) = ins
    (whole,) = scratch
    if pair:
        outs, last = outs[:-1], outs[-1]
        last[...] = pair[0][...] + pair[1][...]
        heads = [*heads, last]
    tokens = heads[0].shape[0]
    cols = outs[0].shape[1]
    parts = len(outs)
    together = 4 if len(heads) % 4 == 0 else 1
    for first in range(0, len(heads), together):
        rows = slice(first * tokens, (first + together) * tokens)
        values = jnp.concatenate([h[...] for h in heads[first : first + together]])
        whole[...] = dot(values, fold[...], NN)
        for k in range(parts):
            at = (where[0] ^ k) * cols
            outs[k][rows, :] = whole[:, pl.ds(pl.multiple_of(at, cols), cols)].astype(bf16)


def forward(received, code_mix, code_send, square, products, width):
    relay = products.shape[1] // 2
    count = received.shape[1] // relay
    mixed, unscaled = [], []
    for k in range(count):
        cols = slice(k * relay, (k + 1) * relay)
        both = dot(received[:, cols], products[cols, :], NN)
        mixed.append(code_mix[:, cols] + both[:, :relay])
        unscaled.append(code_send[:, cols] + both[:, relay:])
    mixed = jnp.concatenate(mixed, axis=1)
    unscaled = jnp.concatenate(unscaled, axis=1)
    totals = square + jnp.sum(received.astype(f32) * (code_mix + mixed), axis=1, keepdims=True)
    row_scale = lax.rsqrt(jnp.maximum(totals, 0.0) / width + epsilon)
    return mixed, unscaled, row_scale


def backward(incoming, mixed, unscaled, row_scale, products, width):
    relay = products.shape[1] // 2
    count = incoming.shape[1] // relay
    inner = row_scale * jnp.sum(incoming.astype(f32) * unscaled, axis=1, keepdims=True) / width
    returned = []
    for k in range(count):
        cols = slice(k * relay, (k + 1) * relay)
        back = dot(incoming[:, cols], products[cols, relay:], NT)
        returned.append(row_scale * (back - row_scale * inner * mixed[:, cols]))
    return inner, jnp.concatenate(returned, axis=1).astype(bf16)


def first_kernel(width, where, ins, outs, scratch):
    mix_blocks, payloads, (products, weights) = ins
    mix, ends, mix_gram, mix_recv, mix_send, square, sent = outs
    (gram,) = scratch
    codes = mix.shape[1]
    relay = products.shape[1] // 2
    parts = len(mix_blocks)
    cols = codes // parts
    for k in range(parts):
        at = pl.multiple_of((where[0] ^ k) * cols, cols)
        mix[:, pl.ds(at, cols)] = mix_blocks[k][...]
        ends[:, k * relay : (k + 1) * relay] = payloads[k][cols * codes // relay :, :]
        for j in range(codes // relay):
            piece = payloads[k][j * cols : (j + 1) * cols, :]
            gram[pl.ds(at, cols), j * relay : (j + 1) * relay] = piece

    def step(at):
        codes_here = mix[at, :]
        in_gram = dot(codes_here, gram[...], NN)
        sums = jnp.sum(in_gram * codes_here.astype(f32), axis=1, keepdims=True)
        in_relay = dot(codes_here, weights[...], NN)
        in_recv = in_relay[:, : parts * relay]
        in_send = in_relay[:, parts * relay :]
        mix_gram[at, :] = in_gram
        mix_recv[at, :] = in_recv
        mix_send[at, :] = in_send
        square[at, :] = sums
        mixed, unscaled, row_scale = forward(
            ends[at, :], in_recv, in_send, sums, products[...], width
        )
        sent[at, :] = (row_scale * unscaled).astype(bf16)

    by_rows(mix.shape[0], step)


def forward_kernel(width, turn, last, where, ins, outs, scratch):
    ((moved, received, ends, mix_recv, mix_send, square, products),) = ins
    live = where[2] == turn

    def step(at):
        values = jnp.where(live, moved[at, :], received[at, :])
        mixed, unscaled, row_scale = forward(
            values, mix_recv[at, :], mix_send[at, :], square[at, :], products[...], width
        )
        outs[0][at, :] = values
        outs[1][at, :] = (row_scale * unscaled).astype(bf16)
        if last:
            inner, returned = backward(
                ends[at, :], mixed, unscaled, row_scale, products[...], width
            )
            outs[2][at, :] = mixed
            outs[3][at, :] = unscaled
            outs[4][at, :] = row_scale
            outs[5][at, :] = returned

    by_rows(moved.shape[0], step)
    if last:
        outs[6][...] = outs[1][: outs[6].shape[0], : outs[6].shape[1]]


def backward_kernel(width, live_section, last, where, ins, outs, scratch):
    (moved, incoming, received, mixed, unscaled, row_scale, mix_gram, products, weights), = ins
    live = where[2] == live_section
    half = weights.shape[1] // 2

    def step(at):
        values = jnp.where(live, moved[at, :], incoming[at, :])
        scale = row_scale[at, :]
        inner, returned = backward(
            values, mixed[at, :], unscaled[at, :], scale, products[...], width
        )
        outs[0][at, :] = values
        outs[1][at, :] = returned
        if last:
            outs[2][at, :] = inner
            in_mixed = mix_gram[at, :] + dot(received[at, :], weights[:, :half], NT)
            back = dot(values, weights[:, half:], NT)
            outs[3][at, :] = (scale * (back - scale * inner * in_mixed)).astype(bf16)

    by_rows(moved.shape[0], step)
    if last:
        outs[4][...] = outs[1][: outs[4].shape[0], : outs[4].shape[1]]


def heads_kernel(where, ins, outs, scratch):
    ((code_grad, fold_rows),) = ins
    tokens = outs[0].shape[0]
    whole = dot(code_grad[...], fold_rows[...], NT).astype(bf16)
    for k in range(whole.shape[0] // tokens):
        value = whole[k * tokens : (k + 1) * tokens, :]
        if k % 2:
            outs[-1][k // 2 * tokens : (k // 2 + 1) * tokens, :] = value
        else:
            outs[k // 2][...] = value


def last_kernel(places, where, ins, outs, scratch):
    terms, blocks = ins
    result = terms[0][...].astype(f32)
    for term in terms[1:]:
        result = result + term[...].astype(f32)
    outs[0][...] = result.astype(bf16)
    for k, (index, row) in enumerate(places):
        size = blocks[index].shape[1]
        at = pl.multiple_of((where[1] ^ k) * size, size)
        outs[1][:, pl.ds(at, size)] = blocks[index][row : row + outs[1].shape[0], :]


def head_kernel(where, ins, outs, scratch):
    heads, (code_grad, proj) = ins
    enc_blocks = outs
    (whole,) = scratch
    tokens = heads[0].shape[0]
    together = 4 if len(heads) % 4 == 0 else 1
    sums = None
    for first in range(0, len(heads), together):
        rows = slice(first * tokens, (first + together) * tokens)
        values = jnp.concatenate([h[...] for h in heads[first : first + together]])
        term = dot(code_grad[rows, :], values, TN)
        sums = term if sums is None else sums + term
    whole[...] = dot(sums.astype(bf16), proj[...], NN)
    size = enc_blocks[0].shape[0]
    for k, out in enumerate(enc_blocks):
        at = (where[0] ^ k) * size
        out[...] = whole[pl.ds(pl.multiple_of(at, size), size), :].astype(bf16)


def turn_kernel(where, ins, outs, scratch):
    (heads,) = ins
    tokens = heads[0].shape[0]
    for k, part in enumerate(heads):
        outs[0][:, k * tokens : (k + 1) * tokens] = part[...].T


def proj_kernel(where, ins, outs, scratch):
    ((turned, code_grad, enc),) = ins
    held, sent = scratch
    size = held.shape[1]
    copies = []
    for k in range(held.shape[0]):
        rows = slice(k * size, (k + 1) * size)
        head_sum = dot(turned[rows, :], code_grad[...], NN).astype(bf16)
        held[k, :, :] = dot(head_sum, enc[...], NN).astype(bf16)
        copies.append(pltpu.make_async_copy(held.at[k], outs[0].at[rows, :], sent.at[k]))
        copies[-1].start()
    for copy in copies:
        copy.wait()


def feature_kernel(where, ins, outs, scratch):
    (mix, mix_cols, received, incoming, row_scale, inner, dec, recv, send, gain), = ins
    sums = scratch
    relay = recv.shape[0]
    size = sums[0].shape[0]
    cols = slice(None)
    if mix_cols.shape[1] > size:
        cols = pl.ds(pl.multiple_of(where[1] * size, size), size)
    for ref in sums:
        ref[...] = jnp.zeros_like(ref)

    def step(at):
        received_here = received[at, :relay]
        incoming_here = incoming[at, :relay]
        scale = row_scale[at, :]
        mixed = dot(mix[at, :], dec[...], NN) + dot(received_here, recv[...], NN)
        normed = mixed * scale
        out_rows = (normed * gain[...]).astype(bf16)
        grad_norm = dot(incoming_here, send[...], NT)
        grad_mixed = scale * (grad_norm * gain[...] - normed * inner[at, :])
        grad_mixed = grad_mixed.astype(bf16)
        sums[0][...] += dot(mix_cols[at, cols], grad_mixed, TN)
        sums[1][...] += jnp.sum(grad_norm * normed, axis=0, keepdims=True)
        sums[2][...] += dot(out_rows, incoming_here, TN)
        sums[3][...] += dot(received_here, grad_mixed, TN)

    by_rows(mix.shape[0], step)
    for out, ref in zip(outs, sums):
        out[...] = ref[...].astype(out.dtype)


def on_device(
    heads_out,
    out_proj,
    encoder,
    decoder,
    norm_gain,
    send_encoder,
    recv_decoder,
    input_code,
    code_cotangent,
):
    sections = lax.axis_size("pipe")
    section = lax.axis_index("pipe")
    groups = lax.axis_size("dp")
    parts = lax.axis_size("tensor")
    width = norm_gain.shape[1] * parts
    proj = out_proj[0]
    enc = encoder[0]
    dec = decoder[0]
    gain = norm_gain
    send = send_encoder[0]
    recv = recv_decoder[0]
    tokens, relay = input_code.shape
    codes, features = dec.shape
    cols = codes // parts
    rows = tokens * groups
    head_cols, model_cols = proj.shape
    where = jnp.stack([lax.axis_index("tensor"), lax.axis_index("dp"), section]).astype(jnp.int32)

    end = jnp.where(section == 0, input_code, code_cotangent)
    heads, pair, ends = line_gathered(heads_out[0], end, "dp")
    packs = run(
        gram_kernel,
        [like((cols * codes // (2 * relay) + codes + relay, 2 * relay))] * parts,
        where,
        [(dec, recv, send, gain)],
        scratch=[pltpu.VMEM((codes, codes), f32)],
        fetch=True,
    )
    half = like((head_cols // 2, codes))
    fold, fold_kept, fold_given = run(
        functools.partial(fold_kernel, groups),
        [like((head_cols, codes)), half, half],
        where,
        [(proj, enc)],
        fetch=True,
    )
    fold, _ = lax.optimization_barrier((fold, packs[0]))
    packs = scattered(packs, "tensor")

    partials = run(
        partial_kernel,
        [like((rows, cols))] * parts + [like((tokens, head_cols))] * (len(pair) // 2),
        where,
        [heads, pair, (fold,)],
        scratch=[pltpu.VMEM((min(groups, 4) * tokens, codes), f32)],
        flops=2 * rows * head_cols * codes,
    )
    partials, heads = list(partials[:parts]), [*heads, *partials[parts:]]
    partials[-1], *_ = lax.optimization_barrier((partials[-1], *packs))
    fold_given, partials = lax.optimization_barrier((fold_given, partials))
    fold_other = swap(fold_given, "dp", 1)
    arrived = scattered(partials, "tensor")
    arrived, ends = lax.optimization_barrier((arrived, ends))
    code_block = total(arrived, where)
    fold_terms = halved(fold_kept, fold_other, head_cols // groups, where)
    wide = parts * relay
    packs, _ = lax.optimization_barrier((packs, code_block))
    payload, products, weights = run(
        setup_kernel,
        [
            like((cols * codes // relay + rows, relay)),
            like((wide, 2 * relay)),
            like((codes, 2 * wide)),
        ],
        where,
        [packs, ends],
    )
    payloads = gathered(payload, "tensor")
    (turned,) = run(turn_kernel, [like((head_cols, rows))], where, [heads])
    mix_block = group_sum(code_block, [*payloads, *fold_terms, turned], "dp", where)
    mix_block, fold_terms = lax.optimization_barrier((mix_block, fold_terms))
    mix_blocks = gathered(mix_block, "tensor")

    square_flops = 2 * rows * codes * codes
    mix, ends, mix_gram, mix_recv, mix_send, square, sent = run(
        functools.partial(first_kernel, width),
        [
            like((rows, codes)),
            like((rows, wide)),
            like((rows, codes), f32),
            like((rows, wide), f32),
            like((rows, wide), f32),
            like((rows, 1), f32),
            like((rows, wide)),
        ],
        where,
        [mix_blocks, payloads, (products, weights)],
        scratch=[pltpu.VMEM((codes, codes), bf16)],
        flops=3 * square_flops,
    )
    step = 2
    while step < groups:
        kept, given = fold_terms
        other = swap(given, "dp", step)
        step *= 2
        if step < groups:
            fold_terms = halved(kept, other, head_cols // groups, where)
        else:
            fold_rows = total([kept, other], where, flops=1 << 33)
    received = ends
    for turn in range(1, sections):
        last = turn == sections - 1
        shapes = [like((rows, wide)), like((rows, wide))]
        if last:
            shapes += [like((rows, wide), f32)] * 2 + [like((rows, 1), f32), like((rows, wide))]
            shapes += [like((tokens, relay))]
        moved = move(sent, "pipe", 1)
        if turn == 1:
            moved, fold_rows = lax.optimization_barrier((moved, fold_rows))
        results = run(
            functools.partial(forward_kernel, width, turn, last),
            shapes,
            where,
            [(moved, received, ends, mix_recv, mix_send, square, products)],
            flops=square_flops,
        )
        received, sent = results[:2]
    mixed, unscaled, row_scale, returned, sent = results[2:]
    incoming = ends
    for turn in range(1, sections):
        last = turn == sections - 1
        shapes = [like((rows, wide)), like((rows, wide))]
        if last:
            shapes += [like((rows, 1), f32), like((rows, codes))]
            shapes += [like((tokens, relay))]
        moved = move(returned, "pipe", -1)
        results = run(
            functools.partial(backward_kernel, width, sections - 1 - turn, last),
            shapes,
            where,
            [
                (
                    moved,
                    incoming,
                    received,
                    mixed,
                    unscaled,
                    row_scale,
                    mix_gram,
                    products,
                    weights,
                )
            ],
            flops=3 * square_flops,
        )
        incoming, returned = results[:2]
    inner, code_grad, returned = results[2:]

    enc_blocks = run(
        head_kernel,
        [like((cols, model_cols))] * parts,
        where,
        [heads, (code_grad, proj)],
        scratch=[pltpu.VMEM((codes, model_cols), f32)],
        flops=2 * head_cols * codes * (rows + model_cols),
    )
    code_grad, mix, turned, enc_blocks = lax.optimization_barrier(
        (code_grad, mix, turned, enc_blocks)
    )
    enc_blocks = scattered(enc_blocks, "tensor")
    size = head_cols // groups
    *kept, given = run(
        heads_kernel,
        [like((tokens, size))] * (groups // 2) + [like((rows // 2, size))],
        where,
        [(code_grad, fold_rows)],
    )
    given, mix, turned = lax.optimization_barrier((given, mix, turned))
    head_blocks = exchanged(kept, given, tokens, "dp")
    (proj_grad,) = run(
        proj_kernel,
        [like((head_cols, model_cols))],
        where,
        [(turned, code_grad, enc)],
        scratch=[
            pltpu.VMEM((4, head_cols // 4, model_cols), bf16),
            pltpu.SemaphoreType.DMA((4,)),
        ],
        store=True,
    )
    shapes = [(codes // groups, features), (1, features), (features, relay), (relay, features)]
    dec_grad, gain_grad, send_grad, recv_grad = run(
        feature_kernel,
        [like(shape, f32 if k == 1 else bf16) for k, shape in enumerate(shapes)],
        where,
        [
            (
                mix,
                mix if codes // groups % 128 == 0 else block(mix, "dp", 1),
                received,
                incoming,
                row_scale,
                inner,
                dec,
                recv,
                send,
                gain,
            )
        ],
        scratch=[pltpu.VMEM(shape, f32) for shape in shapes],
    )
    if size % 128 == 0:
        arrays = []
        for array, _ in head_blocks:
            if not any(array is other for other in arrays):
                arrays.append(array)
        places = [
            (next(k for k, other in enumerate(arrays) if other is array), row)
            for array, row in head_blocks
        ]
        enc_grad, heads_grad = run(
            functools.partial(last_kernel, places),
            [like((cols, model_cols)), like((tokens, head_cols))],
            where,
            [enc_blocks, arrays],
        )
    else:
        enc_grad = total(enc_blocks, where)
        blocks = [array[row : row + tokens] for array, row in head_blocks]
        heads_grad = ordered(blocks, "dp")
    return (
        sent[None],
        returned[None],
        heads_grad[None],
        proj_grad[None],
        enc_grad[None],
        dec_grad[None],
        gain_grad,
        send_grad[None],
        recv_grad[None],
    )


def solution(mesh):
    return jax.shard_map(
        on_device,
        mesh=mesh,
        in_specs=(
            P("pipe", "dp", "tensor"),
            P("pipe", "tensor", "dp"),
            P("pipe", None, "dp"),
            P("pipe", None, "tensor"),
            P("pipe", "tensor"),
            P("pipe", "tensor", None),
            P("pipe", None, "tensor"),
            P("dp", "tensor"),
            P("dp", "tensor"),
        ),
        out_specs=(
            P("pipe", "dp", "tensor"),
            P("pipe", "dp", "tensor"),
            P("pipe", "dp", "tensor"),
            P("pipe", "tensor", "dp"),
            P("pipe", "tensor", "dp"),
            P("pipe", "dp", "tensor"),
            P("pipe", "tensor"),
            P("pipe", "tensor", None),
            P("pipe", None, "tensor"),
        ),
        check_vma=False,
    )
```

```python
import functools

import jax
import jax.numpy as jnp
from jax import lax
from jax.experimental import pallas as pl
from jax.experimental.pallas import tpu as pltpu
from jax.sharding import PartitionSpec as P

epsilon = 1e-05
f32 = jnp.float32
bf16 = jnp.bfloat16
NN = ((1,), (0,))
NT = ((1,), (1,))
TN = ((0,), (0,))


def swap(shard, axis, by):
    return lax.ppermute(shard, axis, [(i, i ^ by) for i in range(lax.axis_size(axis))])


def move(shard, axis, by):
    devices = lax.axis_size(axis)
    pairs = [(i, i + by) for i in range(devices) if 0 <= i + by < devices]
    return lax.ppermute(shard, axis, pairs)


def gathered(shard, axis):
    return [shard] + [swap(shard, axis, k) for k in range(1, lax.axis_size(axis))]


def line_gathered(shard, small, after, axis):
    if lax.axis_size(axis) != 4:
        return gathered(shard, axis), [], gathered(small, axis)
    far, near = swap(shard, axis, 2), swap(shard, axis, 1)
    beside = swap(small, axis, 1)
    shard, far, near, beside = lax.optimization_barrier((shard, far, near, beside))
    across = lax.ppermute(shard, axis, [(1, 2), (2, 1)])
    passed = lax.ppermute(far, axis, [(1, 0), (2, 3)])
    both = jnp.concatenate([small, beside])
    both, across, passed, _ = lax.optimization_barrier((both, across, passed, after))
    return [shard, near, far], [across, passed], [small, beside, swap(both, axis, 2)]


def scattered(blocks, axis):
    return [blocks[0]] + [swap(blocks[k], axis, k) for k in range(1, len(blocks))]


def group_sum(rows, after, axis, where):
    groups = lax.axis_size(axis)
    step = groups // 2
    while step:
        other = swap(rows, axis, step)
        if step == 1:
            other, *_ = lax.optimization_barrier((other, *after))
        kernel = functools.partial(moved_sum_kernel, groups, step)
        (rows,) = run(kernel, [like(rows.shape)], where, [(rows, other)])
        step //= 2
    return rows


def exchanged(kept, given, size, axis):
    count = lax.axis_size(axis)
    parts = [[(part, 0) for part in kept]]
    step = 1
    while True:
        arrived = swap(given, axis, step)
        left = count // (2 * step)
        parts += [
            [(arrived, (j * left + k) * size) for k in range(left)] for j in range(len(parts))
        ]
        step *= 2
        if step == count:
            return [part[0] for part in parts]
        given = [array[row : row + size] for part in parts for array, row in part[1::2]]
        given = jnp.concatenate(given)
        parts = [part[::2] for part in parts]


def halved(mine, other, size, where):
    half = like((mine.shape[0] // 2, mine.shape[1]))
    return run(functools.partial(halved_kernel, size), [half, half], where, [(mine, other)])


def total(blocks, where, flops=0):
    return run(total_kernel, [like(blocks[0].shape)], where, [blocks], flops=flops)[0]


def ordered(blocks, axis):
    step = 1
    while step < len(blocks):
        odd = (lax.axis_index(axis) & step) > 0
        blocks = [jnp.where(odd, blocks[k ^ step], part) for k, part in enumerate(blocks)]
        step *= 2
    return jnp.concatenate(blocks, axis=1)


def block(array, axis, dim):
    size = array.shape[dim] // lax.axis_size(axis)
    return lax.dynamic_slice_in_dim(array, lax.axis_index(axis) * size, size, dim)


def dot(left, right, over):
    return lax.dot_general(left, right, (over, ((), ())), preferred_element_type=f32)


def run(kernel, results, where, groups_of_args, scratch=(), flops=0, fetch=False, store=False):
    counts = [len(group) for group in groups_of_args]
    flat = [array for group in groups_of_args for array in group]
    out_count = len(results)
    scratch = list(scratch)
    own = len(scratch)
    space = pltpu.HBM if fetch else pltpu.VMEM
    if fetch:
        scratch += [pltpu.VMEM(array.shape, array.dtype) for array in flat]
        scratch.append(pltpu.SemaphoreType.DMA((len(flat),)))

    def body(where_ref, *refs):
        args, refs = refs[: len(flat)], refs[len(flat) :]
        outs, refs = refs[:out_count], refs[out_count:]
        if fetch:
            held, arrived = refs[own:-1], refs[-1]
            copies = [
                pltpu.make_async_copy(arg, here, arrived.at[k])
                for k, (arg, here) in enumerate(zip(args, held))
            ]
            for copy in copies:
                copy.start()
            for copy in copies:
                copy.wait()
            args = held
        ins, at = [], 0
        for count in counts:
            ins.append(args[at : at + count])
            at += count
        kernel(where_ref, ins, outs, refs[:own])

    if fetch:
        flat = [pltpu.with_memory_space_constraint(array, pltpu.HBM) for array in flat]
    size = sum(a.size * a.dtype.itemsize for a in list(flat) + list(results))
    limit = (10 << 20) if size < (10 << 20) else size + (12 << 20)
    return pl.pallas_call(
        body,
        out_shape=[jax.ShapeDtypeStruct(r.shape, r.dtype) for r in results],
        in_specs=[pl.BlockSpec(memory_space=pltpu.SMEM)]
        + [pl.BlockSpec(memory_space=space)] * len(flat),
        out_specs=[pl.BlockSpec(memory_space=pltpu.HBM if store else pltpu.VMEM)] * out_count,
        scratch_shapes=scratch,
        compiler_params=pltpu.CompilerParams(vmem_limit_bytes=limit),
        cost_estimate=pl.CostEstimate(
            flops=flops, bytes_accessed=size if flops else 0, transcendentals=0
        ),
    )(where, *flat)


def like(shape, dtype=bf16):
    return jax.ShapeDtypeStruct(shape, dtype)


def by_rows(rows, step):
    chunk = min(rows, 512)
    if rows == chunk:
        step(slice(0, rows))
        return

    @pl.loop(0, rows // chunk)
    def _(index):
        step(pl.ds(pl.multiple_of(index * chunk, chunk), chunk))


def total_kernel(where, ins, outs, scratch):
    (blocks,) = ins
    result = blocks[0][...].astype(f32)
    for part in blocks[1:]:
        result = result + part[...].astype(f32)
    outs[0][...] = result.astype(bf16)


def moved_sum_kernel(groups, step, where, ins, outs, scratch):
    ((mine, other),) = ins
    size = mine.shape[0] // groups
    for k in range(groups):
        here = slice(k * size, (k + 1) * size)
        there = slice((k ^ step) * size, ((k ^ step) + 1) * size)
        value = mine[here, :].astype(f32) + other[there, :].astype(f32)
        outs[0][here, :] = value.astype(bf16)


def halved_kernel(size, where, ins, outs, scratch):
    ((mine, other),) = ins
    for k in range(mine.shape[0] // size):
        here = slice(k * size, (k + 1) * size)
        there = slice(k // 2 * size, (k // 2 + 1) * size)
        value = mine[here, :].astype(f32) + other[here, :].astype(f32)
        outs[k % 2][there, :] = value.astype(bf16)


def gram_kernel(where, ins, outs, scratch):
    ((dec, recv, send, gain),) = ins
    (whole,) = scratch
    codes, relay = dec.shape[0], recv.shape[0]
    cols = codes // len(outs)
    wide = 2 * relay
    head = cols * codes // wide
    whole[...] = dot(dec[...], dec[...], NT)
    for k, out in enumerate(outs):
        rows = pl.ds(pl.multiple_of((where[0] ^ k) * cols, cols), cols)
        for j in range(codes // wide):
            piece = whole[rows, j * wide : (j + 1) * wide]
            out[j * cols : (j + 1) * cols, :] = piece.astype(bf16)
    for ref, rows in ((dec, slice(head, head + codes)), (recv, slice(head + codes, None))):
        values = ref[...]
        gained = (values.astype(f32) * gain[...]).astype(bf16)
        plain = dot(values, recv[...], NT).astype(bf16)
        scaled = dot(gained, send[...], NN).astype(bf16)
        for out in outs:
            out[rows, :relay] = plain
            out[rows, relay:] = scaled


def setup_kernel(where, ins, outs, scratch):
    packs, ends = ins
    payload, products, weights = outs
    parts = len(packs)
    wide = products.shape[1]
    relay = wide // 2
    codes = weights.shape[0]
    cols = codes // parts
    head = cols * codes // wide
    for j in range(codes // wide):
        rows = slice(j * cols, (j + 1) * cols)
        gram = packs[0][rows, :].astype(f32)
        for pack in packs[1:]:
            gram = gram + pack[rows, :].astype(f32)
        gram = gram.astype(bf16)
        payload[2 * j * cols : (2 * j + 1) * cols, :] = gram[:, :relay]
        payload[(2 * j + 1) * cols : (2 * j + 2) * cols, :] = gram[:, relay:]
    start = 2 * head
    for end in ends:
        payload[start : start + end.shape[0], :] = end[...]
        start += end.shape[0]
    for k, pack in enumerate(packs):
        here = slice(k * relay, (k + 1) * relay)
        products[here, :] = pack[head + codes :, :]
        weights[:, here] = pack[head : head + codes, :relay]
        there = slice((parts + k) * relay, (parts + k + 1) * relay)
        weights[:, there] = pack[head : head + codes, relay:]


def fold_kernel(groups, where, ins, outs, scratch):
    ((proj, enc),) = ins
    fold = outs[0]
    size = fold.shape[0] // groups
    fold[...] = dot(proj[...], enc[...], NT).astype(bf16)
    for k in range(groups):
        there = slice(k // 2 * size, (k // 2 + 1) * size)
        here = pl.ds(pl.multiple_of((where[1] ^ k) * size, size), size)
        outs[1 + k % 2][there, :] = fold[here, :]


def partial_kernel(where, ins, outs, scratch):
    heads, pair, (fold,) = ins
    (whole,) = scratch
    if pair:
        outs, last = outs[:-1], outs[-1]
        last[...] = pair[0][...] + pair[1][...]
        heads = [*heads, last]
    tokens = heads[0].shape[0]
    cols = outs[0].shape[1]
    parts = len(outs)
    together = 4 if len(heads) % 4 == 0 else 1
    for first in range(0, len(heads), together):
        rows = slice(first * tokens, (first + together) * tokens)
        values = jnp.concatenate([h[...] for h in heads[first : first + together]])
        whole[...] = dot(values, fold[...], NN)
        for k in range(parts):
            at = (where[0] ^ k) * cols
            outs[k][rows, :] = whole[:, pl.ds(pl.multiple_of(at, cols), cols)].astype(bf16)


def forward(received, code_mix, code_send, square, products, width):
    relay = products.shape[1] // 2
    count = received.shape[1] // relay
    mixed, unscaled = [], []
    for k in range(count):
        cols = slice(k * relay, (k + 1) * relay)
        both = dot(received[:, cols], products[cols, :], NN)
        mixed.append(code_mix[:, cols] + both[:, :relay])
        unscaled.append(code_send[:, cols] + both[:, relay:])
    mixed = jnp.concatenate(mixed, axis=1)
    unscaled = jnp.concatenate(unscaled, axis=1)
    totals = square + jnp.sum(received.astype(f32) * (code_mix + mixed), axis=1, keepdims=True)
    row_scale = lax.rsqrt(jnp.maximum(totals, 0.0) / width + epsilon)
    return mixed, unscaled, row_scale


def backward(incoming, mixed, unscaled, row_scale, products, width):
    relay = products.shape[1] // 2
    count = incoming.shape[1] // relay
    inner = row_scale * jnp.sum(incoming.astype(f32) * unscaled, axis=1, keepdims=True) / width
    returned = []
    for k in range(count):
        cols = slice(k * relay, (k + 1) * relay)
        back = dot(incoming[:, cols], products[cols, relay:], NT)
        returned.append(row_scale * (back - row_scale * inner * mixed[:, cols]))
    return inner, jnp.concatenate(returned, axis=1).astype(bf16)


def first_kernel(width, where, ins, outs, scratch):
    mix_blocks, payloads, (products, weights) = ins
    mix, ends, mix_gram, mix_recv, mix_send, square, sent = outs
    (gram,) = scratch
    codes = mix.shape[1]
    relay = products.shape[1] // 2
    parts = len(mix_blocks)
    cols = codes // parts
    for k in range(parts):
        at = pl.multiple_of((where[0] ^ k) * cols, cols)
        mix[:, pl.ds(at, cols)] = mix_blocks[k][...]
        ends[:, k * relay : (k + 1) * relay] = payloads[k][cols * codes // relay :, :]
        for j in range(codes // relay):
            piece = payloads[k][j * cols : (j + 1) * cols, :]
            gram[pl.ds(at, cols), j * relay : (j + 1) * relay] = piece

    def step(at):
        codes_here = mix[at, :]
        in_gram = dot(codes_here, gram[...], NN)
        sums = jnp.sum(in_gram * codes_here.astype(f32), axis=1, keepdims=True)
        in_relay = dot(codes_here, weights[...], NN)
        in_recv = in_relay[:, : parts * relay]
        in_send = in_relay[:, parts * relay :]
        mix_gram[at, :] = in_gram
        mix_recv[at, :] = in_recv
        mix_send[at, :] = in_send
        square[at, :] = sums
        mixed, unscaled, row_scale = forward(
            ends[at, :], in_recv, in_send, sums, products[...], width
        )
        sent[at, :] = (row_scale * unscaled).astype(bf16)

    by_rows(mix.shape[0], step)


def forward_kernel(width, turn, last, where, ins, outs, scratch):
    ((moved, received, ends, mix_recv, mix_send, square, products),) = ins
    live = where[2] == turn

    def step(at):
        values = jnp.where(live, moved[at, :], received[at, :])
        mixed, unscaled, row_scale = forward(
            values, mix_recv[at, :], mix_send[at, :], square[at, :], products[...], width
        )
        outs[0][at, :] = values
        outs[1][at, :] = (row_scale * unscaled).astype(bf16)
        if last:
            inner, returned = backward(
                ends[at, :], mixed, unscaled, row_scale, products[...], width
            )
            outs[2][at, :] = mixed
            outs[3][at, :] = unscaled
            outs[4][at, :] = row_scale
            outs[5][at, :] = returned

    by_rows(moved.shape[0], step)
    if last:
        outs[6][...] = outs[1][: outs[6].shape[0], : outs[6].shape[1]]


def backward_kernel(width, live_section, last, where, ins, outs, scratch):
    (moved, incoming, received, mixed, unscaled, row_scale, mix_gram, products, weights), = ins
    live = where[2] == live_section
    half = weights.shape[1] // 2

    def step(at):
        values = jnp.where(live, moved[at, :], incoming[at, :])
        scale = row_scale[at, :]
        inner, returned = backward(
            values, mixed[at, :], unscaled[at, :], scale, products[...], width
        )
        outs[0][at, :] = values
        outs[1][at, :] = returned
        if last:
            outs[2][at, :] = inner
            in_mixed = mix_gram[at, :] + dot(received[at, :], weights[:, :half], NT)
            back = dot(values, weights[:, half:], NT)
            outs[3][at, :] = (scale * (back - scale * inner * in_mixed)).astype(bf16)

    by_rows(moved.shape[0], step)
    if last:
        outs[4][...] = outs[1][: outs[4].shape[0], : outs[4].shape[1]]


def heads_kernel(where, ins, outs, scratch):
    ((code_grad, fold_rows),) = ins
    tokens = outs[0].shape[0]
    whole = dot(code_grad[...], fold_rows[...], NT).astype(bf16)
    for k in range(whole.shape[0] // tokens):
        value = whole[k * tokens : (k + 1) * tokens, :]
        if k % 2:
            outs[-1][k // 2 * tokens : (k // 2 + 1) * tokens, :] = value
        else:
            outs[k // 2][...] = value


def last_kernel(places, where, ins, outs, scratch):
    terms, blocks = ins
    result = terms[0][...].astype(f32)
    for term in terms[1:]:
        result = result + term[...].astype(f32)
    outs[0][...] = result.astype(bf16)
    for k, (index, row) in enumerate(places):
        size = blocks[index].shape[1]
        at = pl.multiple_of((where[1] ^ k) * size, size)
        outs[1][:, pl.ds(at, size)] = blocks[index][row : row + outs[1].shape[0], :]


def head_kernel(where, ins, outs, scratch):
    heads, (code_grad, proj) = ins
    enc_blocks = outs
    (whole,) = scratch
    tokens = heads[0].shape[0]
    together = 4 if len(heads) % 4 == 0 else 1
    sums = None
    for first in range(0, len(heads), together):
        rows = slice(first * tokens, (first + together) * tokens)
        values = jnp.concatenate([h[...] for h in heads[first : first + together]])
        term = dot(code_grad[rows, :], values, TN)
        sums = term if sums is None else sums + term
    whole[...] = dot(sums.astype(bf16), proj[...], NN)
    size = enc_blocks[0].shape[0]
    for k, out in enumerate(enc_blocks):
        at = (where[0] ^ k) * size
        out[...] = whole[pl.ds(pl.multiple_of(at, size), size), :].astype(bf16)


def turn_kernel(where, ins, outs, scratch):
    (heads,) = ins
    tokens = heads[0].shape[0]
    for k, part in enumerate(heads):
        outs[0][:, k * tokens : (k + 1) * tokens] = part[...].T


def proj_kernel(where, ins, outs, scratch):
    ((turned, code_grad, enc),) = ins
    held, sent = scratch
    size = held.shape[1]
    copies = []
    for k in range(held.shape[0]):
        rows = slice(k * size, (k + 1) * size)
        head_sum = dot(turned[rows, :], code_grad[...], NN).astype(bf16)
        held[k, :, :] = dot(head_sum, enc[...], NN).astype(bf16)
        copies.append(pltpu.make_async_copy(held.at[k], outs[0].at[rows, :], sent.at[k]))
        copies[-1].start()
    for copy in copies:
        copy.wait()


def normed_kernel(where, ins, outs, scratch):
    ((mix, received, row_scale, dec, recv),) = ins
    relay = recv.shape[0]

    def step(at):
        mixed = dot(mix[at, :], dec[...], NN) + dot(received[at, :relay], recv[...], NN)
        outs[0][at, :] = mixed * row_scale[at, :]

    by_rows(mix.shape[0], step)


def feature_kernel(where, ins, outs, scratch):
    ((normed_rows, mix_cols, received, incoming, row_scale, inner, send, gain),) = ins
    sums = scratch
    relay = send.shape[1]
    size = sums[0].shape[0]
    cols = slice(None)
    if mix_cols.shape[1] > size:
        cols = pl.ds(pl.multiple_of(where[1] * size, size), size)
    for ref in sums:
        ref[...] = jnp.zeros_like(ref)

    def step(at):
        received_here = received[at, :relay]
        incoming_here = incoming[at, :relay]
        normed = normed_rows[at, :]
        out_rows = (normed * gain[...]).astype(bf16)
        grad_norm = dot(incoming_here, send[...], NT)
        grad_mixed = row_scale[at, :] * (grad_norm * gain[...] - normed * inner[at, :])
        grad_mixed = grad_mixed.astype(bf16)
        sums[0][...] += dot(mix_cols[at, cols], grad_mixed, TN)
        sums[1][...] += jnp.sum(grad_norm * normed, axis=0, keepdims=True)
        sums[2][...] += dot(out_rows, incoming_here, TN)
        sums[3][...] += dot(received_here, grad_mixed, TN)

    by_rows(normed_rows.shape[0], step)
    for out, ref in zip(outs, sums):
        out[...] = ref[...].astype(out.dtype)


def on_device(
    heads_out,
    out_proj,
    encoder,
    decoder,
    norm_gain,
    send_encoder,
    recv_decoder,
    input_code,
    code_cotangent,
):
    sections = lax.axis_size("pipe")
    section = lax.axis_index("pipe")
    groups = lax.axis_size("dp")
    parts = lax.axis_size("tensor")
    width = norm_gain.shape[1] * parts
    proj = out_proj[0]
    enc = encoder[0]
    dec = decoder[0]
    gain = norm_gain
    send = send_encoder[0]
    recv = recv_decoder[0]
    tokens, relay = input_code.shape
    codes, features = dec.shape
    cols = codes // parts
    rows = tokens * groups
    head_cols, model_cols = proj.shape
    where = jnp.stack([lax.axis_index("tensor"), lax.axis_index("dp"), section]).astype(jnp.int32)

    packs = run(
        gram_kernel,
        [like((cols * codes // (2 * relay) + codes + relay, 2 * relay))] * parts,
        where,
        [(dec, recv, send, gain)],
        scratch=[pltpu.VMEM((codes, codes), f32)],
        fetch=True,
    )
    half = like((head_cols // 2, codes))
    fold, fold_kept, fold_given = run(
        functools.partial(fold_kernel, groups),
        [like((head_cols, codes)), half, half],
        where,
        [(proj, enc)],
        fetch=True,
    )
    fold, _ = lax.optimization_barrier((fold, packs[0]))
    end = jnp.where(section == 0, input_code, code_cotangent)
    heads, pair, ends = line_gathered(heads_out[0], end, fold, "dp")
    packs = scattered(packs, "tensor")

    partials = run(
        partial_kernel,
        [like((rows, cols))] * parts + [like((tokens, head_cols))] * (len(pair) // 2),
        where,
        [heads, pair, (fold,)],
        scratch=[pltpu.VMEM((min(groups, 4) * tokens, codes), f32)],
        flops=2 * rows * head_cols * codes,
    )
    partials, heads = list(partials[:parts]), [*heads, *partials[parts:]]
    partials[-1], *_ = lax.optimization_barrier((partials[-1], *packs))
    fold_given, partials, ends = lax.optimization_barrier((fold_given, partials, ends))
    fold_other = swap(fold_given, "dp", 1)
    arrived = scattered(partials, "tensor")
    arrived, ends = lax.optimization_barrier((arrived, ends))
    code_block = total(arrived, where)
    fold_terms = halved(fold_kept, fold_other, head_cols // groups, where)
    wide = parts * relay
    packs, _ = lax.optimization_barrier((packs, code_block))
    payload, products, weights = run(
        setup_kernel,
        [
            like((cols * codes // relay + rows, relay)),
            like((wide, 2 * relay)),
            like((codes, 2 * wide)),
        ],
        where,
        [packs, ends],
    )
    payloads = gathered(payload, "tensor")
    (turned,) = run(turn_kernel, [like((head_cols, rows))], where, [heads])
    mix_block = group_sum(code_block, [*payloads, *fold_terms, turned], "dp", where)
    mix_block, fold_terms = lax.optimization_barrier((mix_block, fold_terms))
    mix_blocks = gathered(mix_block, "tensor")

    square_flops = 2 * rows * codes * codes
    mix, ends, mix_gram, mix_recv, mix_send, square, sent = run(
        functools.partial(first_kernel, width),
        [
            like((rows, codes)),
            like((rows, wide)),
            like((rows, codes), f32),
            like((rows, wide), f32),
            like((rows, wide), f32),
            like((rows, 1), f32),
            like((rows, wide)),
        ],
        where,
        [mix_blocks, payloads, (products, weights)],
        scratch=[pltpu.VMEM((codes, codes), bf16)],
        flops=3 * square_flops,
    )
    step = 2
    while step < groups:
        kept, given = fold_terms
        other = swap(given, "dp", step)
        step *= 2
        if step < groups:
            fold_terms = halved(kept, other, head_cols // groups, where)
        else:
            fold_rows = total([kept, other], where, flops=1 << 33)
    received = ends
    for turn in range(1, sections):
        last = turn == sections - 1
        shapes = [like((rows, wide)), like((rows, wide))]
        if last:
            shapes += [like((rows, wide), f32)] * 2 + [like((rows, 1), f32), like((rows, wide))]
            shapes += [like((tokens, relay))]
        moved = move(sent, "pipe", 1)
        if turn == 1:
            moved, fold_rows = lax.optimization_barrier((moved, fold_rows))
        results = run(
            functools.partial(forward_kernel, width, turn, last),
            shapes,
            where,
            [(moved, received, ends, mix_recv, mix_send, square, products)],
            flops=square_flops,
        )
        received, sent = results[:2]
    mixed, unscaled, row_scale, returned, sent = results[2:]
    (normed,) = run(
        normed_kernel,
        [like((rows, features), f32)],
        where,
        [(mix, received, row_scale, dec, recv)],
    )
    incoming = ends
    for turn in range(1, sections):
        last = turn == sections - 1
        shapes = [like((rows, wide)), like((rows, wide))]
        if last:
            shapes += [like((rows, 1), f32), like((rows, codes))]
            shapes += [like((tokens, relay))]
        moved = move(returned, "pipe", -1)
        if turn == 1:
            moved, normed = lax.optimization_barrier((moved, normed))
        results = run(
            functools.partial(backward_kernel, width, sections - 1 - turn, last),
            shapes,
            where,
            [
                (
                    moved,
                    incoming,
                    received,
                    mixed,
                    unscaled,
                    row_scale,
                    mix_gram,
                    products,
                    weights,
                )
            ],
            flops=3 * square_flops,
        )
        incoming, returned = results[:2]
    inner, code_grad, returned = results[2:]

    enc_blocks = run(
        head_kernel,
        [like((cols, model_cols))] * parts,
        where,
        [heads, (code_grad, proj)],
        scratch=[pltpu.VMEM((codes, model_cols), f32)],
        flops=2 * head_cols * codes * (rows + model_cols),
    )
    code_grad, mix, turned, enc_blocks = lax.optimization_barrier(
        (code_grad, mix, turned, enc_blocks)
    )
    enc_blocks = scattered(enc_blocks, "tensor")
    size = head_cols // groups
    *kept, given = run(
        heads_kernel,
        [like((tokens, size))] * (groups // 2) + [like((rows // 2, size))],
        where,
        [(code_grad, fold_rows)],
    )
    given, mix, turned = lax.optimization_barrier((given, mix, turned))
    head_blocks = exchanged(kept, given, tokens, "dp")
    (proj_grad,) = run(
        proj_kernel,
        [like((head_cols, model_cols))],
        where,
        [(turned, code_grad, enc)],
        scratch=[
            pltpu.VMEM((4, head_cols // 4, model_cols), bf16),
            pltpu.SemaphoreType.DMA((4,)),
        ],
        store=True,
    )
    shapes = [(codes // groups, features), (1, features), (features, relay), (relay, features)]
    dec_grad, gain_grad, send_grad, recv_grad = run(
        feature_kernel,
        [like(shape, f32 if k == 1 else bf16) for k, shape in enumerate(shapes)],
        where,
        [
            (
                normed,
                mix if codes // groups % 128 == 0 else block(mix, "dp", 1),
                received,
                incoming,
                row_scale,
                inner,
                send,
                gain,
            )
        ],
        scratch=[pltpu.VMEM(shape, f32) for shape in shapes],
    )
    if size % 128 == 0:
        arrays = []
        for array, _ in head_blocks:
            if not any(array is other for other in arrays):
                arrays.append(array)
        places = [
            (next(k for k, other in enumerate(arrays) if other is array), row)
            for array, row in head_blocks
        ]
        enc_grad, heads_grad = run(
            functools.partial(last_kernel, places),
            [like((cols, model_cols)), like((tokens, head_cols))],
            where,
            [enc_blocks, arrays],
        )
    else:
        enc_grad = total(enc_blocks, where)
        blocks = [array[row : row + tokens] for array, row in head_blocks]
        heads_grad = ordered(blocks, "dp")
    return (
        sent[None],
        returned[None],
        heads_grad[None],
        proj_grad[None],
        enc_grad[None],
        dec_grad[None],
        gain_grad,
        send_grad[None],
        recv_grad[None],
    )


def solution(mesh):
    return jax.shard_map(
        on_device,
        mesh=mesh,
        in_specs=(
            P("pipe", "dp", "tensor"),
            P("pipe", "tensor", "dp"),
            P("pipe", None, "dp"),
            P("pipe", None, "tensor"),
            P("pipe", "tensor"),
            P("pipe", "tensor", None),
            P("pipe", None, "tensor"),
            P("dp", "tensor"),
            P("dp", "tensor"),
        ),
        out_specs=(
            P("pipe", "dp", "tensor"),
            P("pipe", "dp", "tensor"),
            P("pipe", "dp", "tensor"),
            P("pipe", "tensor", "dp"),
            P("pipe", "tensor", "dp"),
            P("pipe", "dp", "tensor"),
            P("pipe", "tensor"),
            P("pipe", "tensor", None),
            P("pipe", None, "tensor"),
        ),
        check_vma=False,
    )
```

```python
import functools

import jax
import jax.numpy as jnp
from jax import lax
from jax.experimental import pallas as pl
from jax.experimental.pallas import tpu as pltpu
from jax.sharding import PartitionSpec as P

epsilon = 1e-05
f32 = jnp.float32
bf16 = jnp.bfloat16
NN = ((1,), (0,))
NT = ((1,), (1,))
TN = ((0,), (0,))


def swap(shard, axis, by):
    return lax.ppermute(shard, axis, [(i, i ^ by) for i in range(lax.axis_size(axis))])


def move(shard, axis, by):
    devices = lax.axis_size(axis)
    pairs = [(i, i + by) for i in range(devices) if 0 <= i + by < devices]
    return lax.ppermute(shard, axis, pairs)


def gathered(shard, axis):
    return [shard] + [swap(shard, axis, k) for k in range(1, lax.axis_size(axis))]


def line_gathered(shard, small, after, axis):
    if lax.axis_size(axis) != 4:
        return gathered(shard, axis), [], gathered(small, axis)
    far, near = swap(shard, axis, 2), swap(shard, axis, 1)
    beside = swap(small, axis, 1)
    shard, far, near, beside = lax.optimization_barrier((shard, far, near, beside))
    across = lax.ppermute(shard, axis, [(1, 2), (2, 1)])
    passed = lax.ppermute(far, axis, [(1, 0), (2, 3)])
    both = jnp.concatenate([small, beside])
    both, across, passed, _ = lax.optimization_barrier((both, across, passed, after))
    return [shard, near, far], [across, passed], [small, beside, swap(both, axis, 2)]


def scattered(blocks, axis):
    return [blocks[0]] + [swap(blocks[k], axis, k) for k in range(1, len(blocks))]


def group_sum(rows, after, axis, where):
    groups = lax.axis_size(axis)
    step = groups // 2
    while step:
        other = swap(rows, axis, step)
        if step == 1:
            other, *_ = lax.optimization_barrier((other, *after))
        kernel = functools.partial(moved_sum_kernel, groups, step)
        (rows,) = run(kernel, [like(rows.shape)], where, [(rows, other)])
        step //= 2
    return rows


def exchanged(kept, given, size, axis):
    count = lax.axis_size(axis)
    parts = [[(part, 0) for part in kept]]
    step = 1
    while True:
        arrived = swap(given, axis, step)
        left = count // (2 * step)
        parts += [
            [(arrived, (j * left + k) * size) for k in range(left)] for j in range(len(parts))
        ]
        step *= 2
        if step == count:
            return [part[0] for part in parts]
        given = [array[row : row + size] for part in parts for array, row in part[1::2]]
        given = jnp.concatenate(given)
        parts = [part[::2] for part in parts]


def halved(mine, other, size, where):
    half = like((mine.shape[0] // 2, mine.shape[1]))
    return run(functools.partial(halved_kernel, size), [half, half], where, [(mine, other)])


def total(blocks, where, flops=0):
    return run(total_kernel, [like(blocks[0].shape)], where, [blocks], flops=flops)[0]


def ordered(blocks, axis):
    step = 1
    while step < len(blocks):
        odd = (lax.axis_index(axis) & step) > 0
        blocks = [jnp.where(odd, blocks[k ^ step], part) for k, part in enumerate(blocks)]
        step *= 2
    return jnp.concatenate(blocks, axis=1)


def block(array, axis, dim):
    size = array.shape[dim] // lax.axis_size(axis)
    return lax.dynamic_slice_in_dim(array, lax.axis_index(axis) * size, size, dim)


def dot(left, right, over):
    return lax.dot_general(left, right, (over, ((), ())), preferred_element_type=f32)


def run(kernel, results, where, groups_of_args, scratch=(), flops=0, fetch=False, store=False):
    counts = [len(group) for group in groups_of_args]
    flat = [array for group in groups_of_args for array in group]
    out_count = len(results)
    scratch = list(scratch)
    own = len(scratch)
    space = pltpu.HBM if fetch else pltpu.VMEM
    if fetch:
        scratch += [pltpu.VMEM(array.shape, array.dtype) for array in flat]
        scratch.append(pltpu.SemaphoreType.DMA((len(flat),)))

    def body(where_ref, *refs):
        args, refs = refs[: len(flat)], refs[len(flat) :]
        outs, refs = refs[:out_count], refs[out_count:]
        if fetch:
            held, arrived = refs[own:-1], refs[-1]
            copies = [
                pltpu.make_async_copy(arg, here, arrived.at[k])
                for k, (arg, here) in enumerate(zip(args, held))
            ]
            for copy in copies:
                copy.start()
            for copy in copies:
                copy.wait()
            args = held
        ins, at = [], 0
        for count in counts:
            ins.append(args[at : at + count])
            at += count
        kernel(where_ref, ins, outs, refs[:own])

    if fetch:
        flat = [pltpu.with_memory_space_constraint(array, pltpu.HBM) for array in flat]
    size = sum(a.size * a.dtype.itemsize for a in list(flat) + list(results))
    limit = (10 << 20) if size < (10 << 20) else size + (12 << 20)
    return pl.pallas_call(
        body,
        out_shape=[jax.ShapeDtypeStruct(r.shape, r.dtype) for r in results],
        in_specs=[pl.BlockSpec(memory_space=pltpu.SMEM)]
        + [pl.BlockSpec(memory_space=space)] * len(flat),
        out_specs=[pl.BlockSpec(memory_space=pltpu.HBM if store else pltpu.VMEM)] * out_count,
        scratch_shapes=scratch,
        compiler_params=pltpu.CompilerParams(vmem_limit_bytes=limit),
        cost_estimate=pl.CostEstimate(
            flops=flops, bytes_accessed=size if flops else 0, transcendentals=0
        ),
    )(where, *flat)


def like(shape, dtype=bf16):
    return jax.ShapeDtypeStruct(shape, dtype)


def by_rows(rows, step):
    chunk = min(rows, 512)
    if rows == chunk:
        step(slice(0, rows))
        return

    @pl.loop(0, rows // chunk)
    def _(index):
        step(pl.ds(pl.multiple_of(index * chunk, chunk), chunk))


def total_kernel(where, ins, outs, scratch):
    (blocks,) = ins
    result = blocks[0][...].astype(f32)
    for part in blocks[1:]:
        result = result + part[...].astype(f32)
    outs[0][...] = result.astype(bf16)


def moved_sum_kernel(groups, step, where, ins, outs, scratch):
    ((mine, other),) = ins
    size = mine.shape[0] // groups
    for k in range(groups):
        here = slice(k * size, (k + 1) * size)
        there = slice((k ^ step) * size, ((k ^ step) + 1) * size)
        value = mine[here, :].astype(f32) + other[there, :].astype(f32)
        outs[0][here, :] = value.astype(bf16)


def halved_kernel(size, where, ins, outs, scratch):
    ((mine, other),) = ins
    for k in range(mine.shape[0] // size):
        here = slice(k * size, (k + 1) * size)
        there = slice(k // 2 * size, (k // 2 + 1) * size)
        value = mine[here, :].astype(f32) + other[here, :].astype(f32)
        outs[k % 2][there, :] = value.astype(bf16)


def gram_kernel(where, ins, outs, scratch):
    ((dec, recv, send, gain),) = ins
    (whole,) = scratch
    codes, relay = dec.shape[0], recv.shape[0]
    cols = codes // len(outs)
    wide = 2 * relay
    head = cols * codes // wide
    whole[...] = dot(dec[...], dec[...], NT)
    for k, out in enumerate(outs):
        rows = pl.ds(pl.multiple_of((where[0] ^ k) * cols, cols), cols)
        for j in range(codes // wide):
            piece = whole[rows, j * wide : (j + 1) * wide]
            out[j * cols : (j + 1) * cols, :] = piece.astype(bf16)
    for ref, rows in ((dec, slice(head, head + codes)), (recv, slice(head + codes, None))):
        values = ref[...]
        gained = (values.astype(f32) * gain[...]).astype(bf16)
        plain = dot(values, recv[...], NT).astype(bf16)
        scaled = dot(gained, send[...], NN).astype(bf16)
        for out in outs:
            out[rows, :relay] = plain
            out[rows, relay:] = scaled


def setup_kernel(where, ins, outs, scratch):
    packs, ends = ins
    payload, products, weights = outs
    parts = len(packs)
    wide = products.shape[1]
    relay = wide // 2
    codes = weights.shape[0]
    cols = codes // parts
    head = cols * codes // wide
    for j in range(codes // wide):
        rows = slice(j * cols, (j + 1) * cols)
        gram = packs[0][rows, :].astype(f32)
        for pack in packs[1:]:
            gram = gram + pack[rows, :].astype(f32)
        gram = gram.astype(bf16)
        payload[2 * j * cols : (2 * j + 1) * cols, :] = gram[:, :relay]
        payload[(2 * j + 1) * cols : (2 * j + 2) * cols, :] = gram[:, relay:]
    start = 2 * head
    for end in ends:
        payload[start : start + end.shape[0], :] = end[...]
        start += end.shape[0]
    for k, pack in enumerate(packs):
        here = slice(k * relay, (k + 1) * relay)
        products[here, :] = pack[head + codes :, :]
        weights[:, here] = pack[head : head + codes, :relay]
        there = slice((parts + k) * relay, (parts + k + 1) * relay)
        weights[:, there] = pack[head : head + codes, relay:]


def fold_kernel(groups, where, ins, outs, scratch):
    ((proj, enc),) = ins
    fold = outs[0]
    size = fold.shape[0] // groups
    fold[...] = dot(proj[...], enc[...], NT).astype(bf16)
    for k in range(groups):
        there = slice(k // 2 * size, (k // 2 + 1) * size)
        here = pl.ds(pl.multiple_of((where[1] ^ k) * size, size), size)
        outs[1 + k % 2][there, :] = fold[here, :]


def partial_kernel(where, ins, outs, scratch):
    heads, pair, (fold,) = ins
    (whole,) = scratch
    if pair:
        outs, last = outs[:-1], outs[-1]
        last[...] = pair[0][...] + pair[1][...]
        heads = [*heads, last]
    tokens = heads[0].shape[0]
    cols = outs[0].shape[1]
    parts = len(outs)
    together = 4 if len(heads) % 4 == 0 else 1
    for first in range(0, len(heads), together):
        rows = slice(first * tokens, (first + together) * tokens)
        values = jnp.concatenate([h[...] for h in heads[first : first + together]])
        whole[...] = dot(values, fold[...], NN)
        for k in range(parts):
            at = (where[0] ^ k) * cols
            outs[k][rows, :] = whole[:, pl.ds(pl.multiple_of(at, cols), cols)].astype(bf16)


def forward(received, code_mix, code_send, square, products, width):
    relay = products.shape[1] // 2
    count = received.shape[1] // relay
    mixed, unscaled = [], []
    for k in range(count):
        cols = slice(k * relay, (k + 1) * relay)
        both = dot(received[:, cols], products[cols, :], NN)
        mixed.append(code_mix[:, cols] + both[:, :relay])
        unscaled.append(code_send[:, cols] + both[:, relay:])
    mixed = jnp.concatenate(mixed, axis=1)
    unscaled = jnp.concatenate(unscaled, axis=1)
    totals = square + jnp.sum(received.astype(f32) * (code_mix + mixed), axis=1, keepdims=True)
    row_scale = lax.rsqrt(jnp.maximum(totals, 0.0) / width + epsilon)
    return mixed, unscaled, row_scale


def backward(incoming, mixed, unscaled, row_scale, products, width):
    relay = products.shape[1] // 2
    count = incoming.shape[1] // relay
    inner = row_scale * jnp.sum(incoming.astype(f32) * unscaled, axis=1, keepdims=True) / width
    returned = []
    for k in range(count):
        cols = slice(k * relay, (k + 1) * relay)
        back = dot(incoming[:, cols], products[cols, relay:], NT)
        returned.append(row_scale * (back - row_scale * inner * mixed[:, cols]))
    return inner, jnp.concatenate(returned, axis=1).astype(bf16)


def early_kernel(where, ins, outs, scratch):
    payloads, (products,) = ins
    relay = products.shape[1] // 2
    rows = outs[0].shape[0] - relay
    for k, payload in enumerate(payloads):
        cols = slice(k * relay, (k + 1) * relay)
        end = payload[payload.shape[0] - rows :, :]
        outs[0][:rows, cols] = dot(end, products[cols, relay:], NT).astype(bf16)
        outs[0][rows:, cols] = products[cols, :relay]


def split(column, lane, first):
    high = column.astype(bf16).astype(f32)
    middle = (column - high).astype(bf16).astype(f32)
    low = column - high - middle
    result = jnp.where(lane == first, high, 0.0)
    result = jnp.where(lane == first + 1, middle, result)
    return jnp.where(lane == first + 2, low, result)


def joined(lanes, first):
    return jnp.sum(lanes[:, first : first + 3].astype(f32), axis=1, keepdims=True)


def first_kernel(width, swapped, where, ins, outs, scratch):
    mix_blocks, payloads, (products, weights) = ins
    mix, ends, mix_gram, mix_recv, mix_send, square, sent = outs
    (gram,) = scratch
    codes = mix.shape[1]
    relay = products.shape[1] // 2
    parts = len(mix_blocks)
    cols = codes // parts
    for k in range(parts):
        at = pl.multiple_of((where[0] ^ k) * cols, cols)
        mix[:, pl.ds(at, cols)] = mix_blocks[k][...]
        ends[:, k * relay : (k + 1) * relay] = payloads[k][cols * codes // relay :, :]
        for j in range(codes // relay):
            piece = payloads[k][j * cols : (j + 1) * cols, :]
            gram[pl.ds(at, cols), j * relay : (j + 1) * relay] = piece

    def step(at):
        codes_here = mix[at, :]
        in_gram = dot(codes_here, gram[...], NN)
        sums = jnp.sum(in_gram * codes_here.astype(f32), axis=1, keepdims=True)
        in_relay = dot(codes_here, weights[...], NN)
        in_recv = in_relay[:, : parts * relay]
        in_send = in_relay[:, parts * relay :]
        mix_gram[at, :] = in_gram
        mix_recv[at, :] = in_recv
        mix_send[at, :] = in_send
        square[at, :] = sums
        mixed, unscaled, row_scale = forward(
            ends[at, :], in_recv, in_send, sums, products[...], width
        )
        offer = (row_scale * unscaled).astype(bf16)
        if not swapped:
            sent[at, :] = offer
            return
        wide = parts * relay
        sent[at, :wide] = jnp.where(where[2] == 0, offer, in_recv.astype(bf16))
        dots = jnp.sum(ends[at, :].astype(f32) * in_send, axis=1, keepdims=True)
        lane = lax.broadcasted_iota(jnp.int32, (sums.shape[0], relay), 1)
        sent[at, wide:] = (split(sums, lane, 0) + split(dots, lane, 3)).astype(bf16)

    by_rows(mix.shape[0], step)


def meet_kernel(width, where, ins, outs, scratch):
    ((got, early, ends, mix_recv, mix_send, mix_gram, square, products, weights),) = ins
    received_out, incoming_out, scale_out, inner_out, code_grad, sent_out, returned_out = outs
    relay = products.shape[1] // 2
    wide = ends.shape[1]
    rows = ends.shape[0]
    first = where[2] == 0

    def step(at):
        here = ends[at, :]
        given = got[at, :wide]
        received = jnp.where(first, here, given)
        mixed, unscaled, row_scale = forward(
            received, mix_recv[at, :], mix_send[at, :], square[at, :], products[...], width
        )
        sent = (row_scale * unscaled).astype(bf16)
        sent_rows = sent.astype(f32)
        other_recv = given.astype(f32)
        back = early[at, :].astype(f32)
        other_mixed = []
        for k in range(wide // relay):
            cols = slice(k * relay, (k + 1) * relay)
            other_mixed.append(other_recv[:, cols] + dot(sent[:, cols], early[rows:, cols], NN))
        other_mixed = jnp.concatenate(other_mixed, axis=1)
        lanes = got[at, wide:]
        totals = joined(lanes, 0) + jnp.sum(
            sent_rows * (other_recv + other_mixed), axis=1, keepdims=True
        )
        scale = lax.rsqrt(jnp.maximum(totals, 0.0) / width + epsilon)
        dots = joined(lanes, 3) + jnp.sum(sent_rows * back, axis=1, keepdims=True)
        inner = scale * dots / width
        returned = (scale * (back - scale * inner * other_mixed)).astype(bf16)
        incoming = jnp.where(first, returned, here)
        inner, returned = backward(incoming, mixed, unscaled, row_scale, products[...], width)
        in_mixed = mix_gram[at, :] + dot(received, weights[:, :wide], NT)
        back = dot(incoming, weights[:, wide:], NT)
        code_grad[at, :] = (row_scale * (back - row_scale * inner * in_mixed)).astype(bf16)
        received_out[at, :] = received[:, :relay]
        incoming_out[at, :] = incoming[:, :relay]
        scale_out[at, :] = row_scale
        inner_out[at, :] = inner
        tokens = min(sent_out.shape[0], sent.shape[0])
        if isinstance(at, slice):
            sent_out[...] = sent[:tokens, :relay]
            returned_out[...] = returned[:tokens, :relay]
        else:

            @pl.when(at.start == 0)
            def _():
                sent_out[...] = sent[:tokens, :relay]
                returned_out[...] = returned[:tokens, :relay]

    by_rows(rows, step)


def forward_kernel(width, turn, last, where, ins, outs, scratch):
    ((moved, received, ends, mix_recv, mix_send, square, products),) = ins
    live = where[2] == turn

    def step(at):
        values = jnp.where(live, moved[at, :], received[at, :])
        mixed, unscaled, row_scale = forward(
            values, mix_recv[at, :], mix_send[at, :], square[at, :], products[...], width
        )
        outs[0][at, :] = values
        outs[1][at, :] = (row_scale * unscaled).astype(bf16)
        if last:
            inner, returned = backward(
                ends[at, :], mixed, unscaled, row_scale, products[...], width
            )
            outs[2][at, :] = mixed
            outs[3][at, :] = unscaled
            outs[4][at, :] = row_scale
            outs[5][at, :] = returned

    by_rows(moved.shape[0], step)
    if last:
        outs[6][...] = outs[1][: outs[6].shape[0], : outs[6].shape[1]]


def backward_kernel(width, live_section, last, where, ins, outs, scratch):
    (moved, incoming, received, mixed, unscaled, row_scale, mix_gram, products, weights), = ins
    live = where[2] == live_section
    half = weights.shape[1] // 2

    def step(at):
        values = jnp.where(live, moved[at, :], incoming[at, :])
        scale = row_scale[at, :]
        inner, returned = backward(
            values, mixed[at, :], unscaled[at, :], scale, products[...], width
        )
        outs[0][at, :] = values
        outs[1][at, :] = returned
        if last:
            outs[2][at, :] = inner
            in_mixed = mix_gram[at, :] + dot(received[at, :], weights[:, :half], NT)
            back = dot(values, weights[:, half:], NT)
            outs[3][at, :] = (scale * (back - scale * inner * in_mixed)).astype(bf16)

    by_rows(moved.shape[0], step)
    if last:
        outs[4][...] = outs[1][: outs[4].shape[0], : outs[4].shape[1]]


def heads_kernel(where, ins, outs, scratch):
    ((code_grad, fold_rows),) = ins
    tokens = outs[0].shape[0]
    whole = dot(code_grad[...], fold_rows[...], NT).astype(bf16)
    for k in range(whole.shape[0] // tokens):
        value = whole[k * tokens : (k + 1) * tokens, :]
        if k % 2:
            outs[-1][k // 2 * tokens : (k // 2 + 1) * tokens, :] = value
        else:
            outs[k // 2][...] = value


def last_kernel(places, where, ins, outs, scratch):
    terms, blocks = ins
    result = terms[0][...].astype(f32)
    for term in terms[1:]:
        result = result + term[...].astype(f32)
    outs[0][...] = result.astype(bf16)
    for k, (index, row) in enumerate(places):
        size = blocks[index].shape[1]
        at = pl.multiple_of((where[1] ^ k) * size, size)
        outs[1][:, pl.ds(at, size)] = blocks[index][row : row + outs[1].shape[0], :]


def head_kernel(where, ins, outs, scratch):
    heads, (code_grad, proj) = ins
    enc_blocks = outs
    (whole,) = scratch
    tokens = heads[0].shape[0]
    together = 4 if len(heads) % 4 == 0 else 1
    sums = None
    for first in range(0, len(heads), together):
        rows = slice(first * tokens, (first + together) * tokens)
        values = jnp.concatenate([h[...] for h in heads[first : first + together]])
        term = dot(code_grad[rows, :], values, TN)
        sums = term if sums is None else sums + term
    whole[...] = dot(sums.astype(bf16), proj[...], NN)
    size = enc_blocks[0].shape[0]
    for k, out in enumerate(enc_blocks):
        at = (where[0] ^ k) * size
        out[...] = whole[pl.ds(pl.multiple_of(at, size), size), :].astype(bf16)


def turn_kernel(where, ins, outs, scratch):
    (heads,) = ins
    tokens = heads[0].shape[0]
    for k, part in enumerate(heads):
        outs[0][:, k * tokens : (k + 1) * tokens] = part[...].T


def proj_kernel(where, ins, outs, scratch):
    ((turned, code_grad, enc),) = ins
    held, sent = scratch
    size = held.shape[1]
    copies = []
    for k in range(held.shape[0]):
        rows = slice(k * size, (k + 1) * size)
        head_sum = dot(turned[rows, :], code_grad[...], NN).astype(bf16)
        held[k, :, :] = dot(head_sum, enc[...], NN).astype(bf16)
        copies.append(pltpu.make_async_copy(held.at[k], outs[0].at[rows, :], sent.at[k]))
        copies[-1].start()
    for copy in copies:
        copy.wait()


def attention_kernel(where, ins, outs, scratch):
    ((mix, dec),) = ins

    def step(at):
        outs[0][at, :] = dot(mix[at, :], dec[...], NN)

    by_rows(mix.shape[0], step)


def feature_kernel(where, ins, outs, scratch):
    ((attention, mix_cols, received, incoming, row_scale, inner, recv, send, gain),) = ins
    sums = scratch
    relay = send.shape[1]
    size = sums[0].shape[0]
    cols = slice(None)
    if mix_cols.shape[1] > size:
        cols = pl.ds(pl.multiple_of(where[1] * size, size), size)
    for ref in sums:
        ref[...] = jnp.zeros_like(ref)

    def step(at):
        received_here = received[at, :relay]
        incoming_here = incoming[at, :relay]
        normed = attention[at, :] + dot(received_here, recv[...], NN)
        normed = normed * row_scale[at, :]
        out_rows = (normed * gain[...]).astype(bf16)
        grad_norm = dot(incoming_here, send[...], NT)
        grad_mixed = row_scale[at, :] * (grad_norm * gain[...] - normed * inner[at, :])
        grad_mixed = grad_mixed.astype(bf16)
        sums[0][...] += dot(mix_cols[at, cols], grad_mixed, TN)
        sums[1][...] += jnp.sum(grad_norm * normed, axis=0, keepdims=True)
        sums[2][...] += dot(out_rows, incoming_here, TN)
        sums[3][...] += dot(received_here, grad_mixed, TN)

    by_rows(attention.shape[0], step)
    for out, ref in zip(outs, sums):
        out[...] = ref[...].astype(out.dtype)


def on_device(
    heads_out,
    out_proj,
    encoder,
    decoder,
    norm_gain,
    send_encoder,
    recv_decoder,
    input_code,
    code_cotangent,
):
    sections = lax.axis_size("pipe")
    section = lax.axis_index("pipe")
    groups = lax.axis_size("dp")
    parts = lax.axis_size("tensor")
    width = norm_gain.shape[1] * parts
    proj = out_proj[0]
    enc = encoder[0]
    dec = decoder[0]
    gain = norm_gain
    send = send_encoder[0]
    recv = recv_decoder[0]
    tokens, relay = input_code.shape
    codes, features = dec.shape
    cols = codes // parts
    rows = tokens * groups
    head_cols, model_cols = proj.shape
    where = jnp.stack([lax.axis_index("tensor"), lax.axis_index("dp"), section]).astype(jnp.int32)

    packs = run(
        gram_kernel,
        [like((cols * codes // (2 * relay) + codes + relay, 2 * relay))] * parts,
        where,
        [(dec, recv, send, gain)],
        scratch=[pltpu.VMEM((codes, codes), f32)],
        fetch=True,
    )
    half = like((head_cols // 2, codes))
    fold, fold_kept, fold_given = run(
        functools.partial(fold_kernel, groups),
        [like((head_cols, codes)), half, half],
        where,
        [(proj, enc)],
        fetch=True,
    )
    fold, _ = lax.optimization_barrier((fold, packs[0]))
    end = jnp.where(section == 0, input_code, code_cotangent)
    heads, pair, ends = line_gathered(heads_out[0], end, fold, "dp")
    packs = scattered(packs, "tensor")

    partials = run(
        partial_kernel,
        [like((rows, cols))] * parts + [like((tokens, head_cols))] * (len(pair) // 2),
        where,
        [heads, pair, (fold,)],
        scratch=[pltpu.VMEM((min(groups, 4) * tokens, codes), f32)],
        flops=2 * rows * head_cols * codes,
    )
    partials, heads = list(partials[:parts]), [*heads, *partials[parts:]]
    partials[-1], *_ = lax.optimization_barrier((partials[-1], *packs))
    fold_given, partials, ends = lax.optimization_barrier((fold_given, partials, ends))
    fold_other = swap(fold_given, "dp", 1)
    arrived = scattered(partials, "tensor")
    arrived, ends = lax.optimization_barrier((arrived, ends))
    code_block = total(arrived, where)
    fold_terms = halved(fold_kept, fold_other, head_cols // groups, where)
    wide = parts * relay
    packs, _ = lax.optimization_barrier((packs, code_block))
    payload, products, weights = run(
        setup_kernel,
        [
            like((cols * codes // relay + rows, relay)),
            like((wide, 2 * relay)),
            like((codes, 2 * wide)),
        ],
        where,
        [packs, ends],
    )
    payloads = gathered(payload, "tensor")
    (turned,) = run(turn_kernel, [like((head_cols, rows))], where, [heads])
    mix_block = group_sum(code_block, [*payloads, *fold_terms, turned], "dp", where)
    mix_block, fold_terms = lax.optimization_barrier((mix_block, fold_terms))
    mix_blocks = gathered(mix_block, "tensor")
    if sections == 2:
        (early,) = run(early_kernel, [like((rows + relay, wide))], where, [payloads, (products,)])
        early = move(early, "pipe", -1)

    square_flops = 2 * rows * codes * codes
    mix, ends, mix_gram, mix_recv, mix_send, square, sent = run(
        functools.partial(first_kernel, width, sections == 2),
        [
            like((rows, codes)),
            like((rows, wide)),
            like((rows, codes), f32),
            like((rows, wide), f32),
            like((rows, wide), f32),
            like((rows, 1), f32),
            like((rows, wide + relay if sections == 2 else wide)),
        ],
        where,
        [mix_blocks, payloads, (products, weights)],
        scratch=[pltpu.VMEM((codes, codes), bf16)],
        flops=3 * square_flops,
    )
    step = 2
    while step < groups:
        kept, given = fold_terms
        other = swap(given, "dp", step)
        step *= 2
        if step < groups:
            fold_terms = halved(kept, other, head_cols // groups, where)
        else:
            fold_rows = total([kept, other], where, flops=1 << 33)
    (attention,) = run(
        attention_kernel, [like((rows, features), f32)], where, [(mix, dec)]
    )
    if sections == 2:
        got = lax.ppermute(sent, "pipe", [(0, 1), (1, 0)])
        got, fold_rows, attention = lax.optimization_barrier((got, fold_rows, attention))
        received, incoming, row_scale, inner, code_grad, sent, returned = run(
            functools.partial(meet_kernel, width),
            [
                like((rows, relay)),
                like((rows, relay)),
                like((rows, 1), f32),
                like((rows, 1), f32),
                like((rows, codes)),
                like((tokens, relay)),
                like((tokens, relay)),
            ],
            where,
            [(got, early, ends, mix_recv, mix_send, mix_gram, square, products, weights)],
            flops=4 * square_flops,
        )
    else:
        received = ends
        for turn in range(1, sections):
            last = turn == sections - 1
            shapes = [like((rows, wide)), like((rows, wide))]
            if last:
                shapes += [like((rows, wide), f32)] * 2 + [like((rows, 1), f32), like((rows, wide))]
                shapes += [like((tokens, relay))]
            moved = move(sent, "pipe", 1)
            results = run(
                functools.partial(forward_kernel, width, turn, last),
                shapes,
                where,
                [(moved, received, ends, mix_recv, mix_send, square, products)],
                flops=square_flops,
            )
            received, sent = results[:2]
        mixed, unscaled, row_scale, returned, sent = results[2:]
        incoming = ends
        for turn in range(1, sections):
            last = turn == sections - 1
            shapes = [like((rows, wide)), like((rows, wide))]
            if last:
                shapes += [like((rows, 1), f32), like((rows, codes))]
                shapes += [like((tokens, relay))]
            moved = move(returned, "pipe", -1)
            results = run(
                functools.partial(backward_kernel, width, sections - 1 - turn, last),
                shapes,
                where,
                [
                    (
                        moved,
                        incoming,
                        received,
                        mixed,
                        unscaled,
                        row_scale,
                        mix_gram,
                        products,
                        weights,
                    )
                ],
                flops=3 * square_flops,
            )
            incoming, returned = results[:2]
        inner, code_grad, returned = results[2:]

    enc_blocks = run(
        head_kernel,
        [like((cols, model_cols))] * parts,
        where,
        [heads, (code_grad, proj)],
        scratch=[pltpu.VMEM((codes, model_cols), f32)],
        flops=2 * head_cols * codes * (rows + model_cols),
    )
    code_grad, mix, turned, enc_blocks = lax.optimization_barrier(
        (code_grad, mix, turned, enc_blocks)
    )
    enc_blocks = scattered(enc_blocks, "tensor")
    size = head_cols // groups
    *kept, given = run(
        heads_kernel,
        [like((tokens, size))] * (groups // 2) + [like((rows // 2, size))],
        where,
        [(code_grad, fold_rows)],
    )
    given, mix, turned = lax.optimization_barrier((given, mix, turned))
    head_blocks = exchanged(kept, given, tokens, "dp")
    (proj_grad,) = run(
        proj_kernel,
        [like((head_cols, model_cols))],
        where,
        [(turned, code_grad, enc)],
        scratch=[
            pltpu.VMEM((4, head_cols // 4, model_cols), bf16),
            pltpu.SemaphoreType.DMA((4,)),
        ],
        store=True,
    )
    shapes = [(codes // groups, features), (1, features), (features, relay), (relay, features)]
    dec_grad, gain_grad, send_grad, recv_grad = run(
        feature_kernel,
        [like(shape, f32 if k == 1 else bf16) for k, shape in enumerate(shapes)],
        where,
        [
            (
                attention,
                mix if codes // groups % 128 == 0 else block(mix, "dp", 1),
                received,
                incoming,
                row_scale,
                inner,
                recv,
                send,
                gain,
            )
        ],
        scratch=[pltpu.VMEM(shape, f32) for shape in shapes],
    )
    if size % 128 == 0:
        arrays = []
        for array, _ in head_blocks:
            if not any(array is other for other in arrays):
                arrays.append(array)
        places = [
            (next(k for k, other in enumerate(arrays) if other is array), row)
            for array, row in head_blocks
        ]
        enc_grad, heads_grad = run(
            functools.partial(last_kernel, places),
            [like((cols, model_cols)), like((tokens, head_cols))],
            where,
            [enc_blocks, arrays],
        )
    else:
        enc_grad = total(enc_blocks, where)
        blocks = [array[row : row + tokens] for array, row in head_blocks]
        heads_grad = ordered(blocks, "dp")
    return (
        sent[None],
        returned[None],
        heads_grad[None],
        proj_grad[None],
        enc_grad[None],
        dec_grad[None],
        gain_grad,
        send_grad[None],
        recv_grad[None],
    )


def solution(mesh):
    return jax.shard_map(
        on_device,
        mesh=mesh,
        in_specs=(
            P("pipe", "dp", "tensor"),
            P("pipe", "tensor", "dp"),
            P("pipe", None, "dp"),
            P("pipe", None, "tensor"),
            P("pipe", "tensor"),
            P("pipe", "tensor", None),
            P("pipe", None, "tensor"),
            P("dp", "tensor"),
            P("dp", "tensor"),
        ),
        out_specs=(
            P("pipe", "dp", "tensor"),
            P("pipe", "dp", "tensor"),
            P("pipe", "dp", "tensor"),
            P("pipe", "tensor", "dp"),
            P("pipe", "tensor", "dp"),
            P("pipe", "dp", "tensor"),
            P("pipe", "tensor"),
            P("pipe", "tensor", None),
            P("pipe", None, "tensor"),
        ),
        check_vma=False,
    )
```

```python
import functools

import jax
import jax.numpy as jnp
from jax import lax
from jax.experimental import pallas as pl
from jax.experimental.pallas import tpu as pltpu
from jax.sharding import PartitionSpec as P

epsilon = 1e-05
f32 = jnp.float32
bf16 = jnp.bfloat16
NN = ((1,), (0,))
NT = ((1,), (1,))
TN = ((0,), (0,))


def swap(shard, axis, by):
    return lax.ppermute(shard, axis, [(i, i ^ by) for i in range(lax.axis_size(axis))])


def move(shard, axis, by):
    devices = lax.axis_size(axis)
    pairs = [(i, i + by) for i in range(devices) if 0 <= i + by < devices]
    return lax.ppermute(shard, axis, pairs)


def gathered(shard, axis):
    return [shard] + [swap(shard, axis, k) for k in range(1, lax.axis_size(axis))]


def line_gathered(shard, small, after, axis):
    if lax.axis_size(axis) != 4:
        return gathered(shard, axis), [], gathered(small, axis)
    far, near = swap(shard, axis, 2), swap(shard, axis, 1)
    beside = swap(small, axis, 1)
    shard, far, near, beside = lax.optimization_barrier((shard, far, near, beside))
    across = lax.ppermute(shard, axis, [(1, 2), (2, 1)])
    passed = lax.ppermute(far, axis, [(1, 0), (2, 3)])
    both = jnp.concatenate([small, beside])
    both, across, passed, _ = lax.optimization_barrier((both, across, passed, after))
    return [shard, near, far], [across, passed], [small, beside, swap(both, axis, 2)]


def scattered(blocks, axis):
    return [blocks[0]] + [swap(blocks[k], axis, k) for k in range(1, len(blocks))]


def group_sum(rows, after, axis, where):
    groups = lax.axis_size(axis)
    step = groups // 2
    while step:
        other = swap(rows, axis, step)
        if step == 1:
            other, *_ = lax.optimization_barrier((other, *after))
        kernel = functools.partial(moved_sum_kernel, groups, step)
        (rows,) = run(kernel, [like(rows.shape)], where, [(rows, other)])
        step //= 2
    return rows


def exchanged(kept, given, size, axis):
    count = lax.axis_size(axis)
    parts = [[(part, 0) for part in kept]]
    step = 1
    while True:
        arrived = swap(given, axis, step)
        left = count // (2 * step)
        parts += [
            [(arrived, (j * left + k) * size) for k in range(left)] for j in range(len(parts))
        ]
        step *= 2
        if step == count:
            return [part[0] for part in parts]
        given = [array[row : row + size] for part in parts for array, row in part[1::2]]
        given = jnp.concatenate(given)
        parts = [part[::2] for part in parts]


def halved(mine, other, size, where):
    half = like((mine.shape[0] // 2, mine.shape[1]))
    return run(functools.partial(halved_kernel, size), [half, half], where, [(mine, other)])


def total(blocks, where, flops=0):
    return run(total_kernel, [like(blocks[0].shape)], where, [blocks], flops=flops)[0]


def ordered(blocks, axis):
    step = 1
    while step < len(blocks):
        odd = (lax.axis_index(axis) & step) > 0
        blocks = [jnp.where(odd, blocks[k ^ step], part) for k, part in enumerate(blocks)]
        step *= 2
    return jnp.concatenate(blocks, axis=1)


def block(array, axis, dim):
    size = array.shape[dim] // lax.axis_size(axis)
    return lax.dynamic_slice_in_dim(array, lax.axis_index(axis) * size, size, dim)


def dot(left, right, over):
    return lax.dot_general(left, right, (over, ((), ())), preferred_element_type=f32)


def run(kernel, results, where, groups_of_args, scratch=(), flops=0, fetch=False, store=False):
    counts = [len(group) for group in groups_of_args]
    flat = [array for group in groups_of_args for array in group]
    out_count = len(results)
    scratch = list(scratch)
    own = len(scratch)
    space = pltpu.HBM if fetch else pltpu.VMEM
    if fetch:
        scratch += [pltpu.VMEM(array.shape, array.dtype) for array in flat]
        scratch.append(pltpu.SemaphoreType.DMA((len(flat),)))

    def body(where_ref, *refs):
        args, refs = refs[: len(flat)], refs[len(flat) :]
        outs, refs = refs[:out_count], refs[out_count:]
        if fetch:
            held, arrived = refs[own:-1], refs[-1]
            copies = [
                pltpu.make_async_copy(arg, here, arrived.at[k])
                for k, (arg, here) in enumerate(zip(args, held))
            ]
            for copy in copies:
                copy.start()
            for copy in copies:
                copy.wait()
            args = held
        ins, at = [], 0
        for count in counts:
            ins.append(args[at : at + count])
            at += count
        kernel(where_ref, ins, outs, refs[:own])

    if fetch:
        flat = [pltpu.with_memory_space_constraint(array, pltpu.HBM) for array in flat]
    size = sum(a.size * a.dtype.itemsize for a in list(flat) + list(results))
    limit = (10 << 20) if size < (10 << 20) else size + (12 << 20)
    return pl.pallas_call(
        body,
        out_shape=[jax.ShapeDtypeStruct(r.shape, r.dtype) for r in results],
        in_specs=[pl.BlockSpec(memory_space=pltpu.SMEM)]
        + [pl.BlockSpec(memory_space=space)] * len(flat),
        out_specs=[pl.BlockSpec(memory_space=pltpu.HBM if store else pltpu.VMEM)] * out_count,
        scratch_shapes=scratch,
        compiler_params=pltpu.CompilerParams(vmem_limit_bytes=limit),
        cost_estimate=pl.CostEstimate(
            flops=flops, bytes_accessed=size if flops else 0, transcendentals=0
        ),
    )(where, *flat)


def like(shape, dtype=bf16):
    return jax.ShapeDtypeStruct(shape, dtype)


def by_rows(rows, step):
    chunk = min(rows, 512)
    if rows == chunk:
        step(slice(0, rows))
        return

    @pl.loop(0, rows // chunk)
    def _(index):
        step(pl.ds(pl.multiple_of(index * chunk, chunk), chunk))


def total_kernel(where, ins, outs, scratch):
    (blocks,) = ins
    result = blocks[0][...].astype(f32)
    for part in blocks[1:]:
        result = result + part[...].astype(f32)
    outs[0][...] = result.astype(bf16)


def moved_sum_kernel(groups, step, where, ins, outs, scratch):
    ((mine, other),) = ins
    size = mine.shape[0] // groups
    for k in range(groups):
        here = slice(k * size, (k + 1) * size)
        there = slice((k ^ step) * size, ((k ^ step) + 1) * size)
        value = mine[here, :].astype(f32) + other[there, :].astype(f32)
        outs[0][here, :] = value.astype(bf16)


def halved_kernel(size, where, ins, outs, scratch):
    ((mine, other),) = ins
    for k in range(mine.shape[0] // size):
        here = slice(k * size, (k + 1) * size)
        there = slice(k // 2 * size, (k // 2 + 1) * size)
        value = mine[here, :].astype(f32) + other[here, :].astype(f32)
        outs[k % 2][there, :] = value.astype(bf16)


def gram_kernel(where, ins, outs, scratch):
    ((dec, recv, send, gain),) = ins
    (whole,) = scratch
    codes, relay = dec.shape[0], recv.shape[0]
    cols = codes // len(outs)
    wide = 2 * relay
    head = cols * codes // wide
    whole[...] = dot(dec[...], dec[...], NT)
    for k, out in enumerate(outs):
        rows = pl.ds(pl.multiple_of((where[0] ^ k) * cols, cols), cols)
        for j in range(codes // wide):
            piece = whole[rows, j * wide : (j + 1) * wide]
            out[j * cols : (j + 1) * cols, :] = piece.astype(bf16)
    for ref, rows in ((dec, slice(head, head + codes)), (recv, slice(head + codes, None))):
        values = ref[...]
        gained = (values.astype(f32) * gain[...]).astype(bf16)
        plain = dot(values, recv[...], NT).astype(bf16)
        scaled = dot(gained, send[...], NN).astype(bf16)
        for out in outs:
            out[rows, :relay] = plain
            out[rows, relay:] = scaled


def setup_kernel(where, ins, outs, scratch):
    packs, ends = ins
    payload, products, weights = outs
    parts = len(packs)
    wide = products.shape[1]
    relay = wide // 2
    codes = weights.shape[0]
    cols = codes // parts
    head = cols * codes // wide
    for j in range(codes // wide):
        rows = slice(j * cols, (j + 1) * cols)
        gram = packs[0][rows, :].astype(f32)
        for pack in packs[1:]:
            gram = gram + pack[rows, :].astype(f32)
        gram = gram.astype(bf16)
        payload[2 * j * cols : (2 * j + 1) * cols, :] = gram[:, :relay]
        payload[(2 * j + 1) * cols : (2 * j + 2) * cols, :] = gram[:, relay:]
    start = 2 * head
    for end in ends:
        payload[start : start + end.shape[0], :] = end[...]
        start += end.shape[0]
    for k, pack in enumerate(packs):
        here = slice(k * relay, (k + 1) * relay)
        products[here, :] = pack[head + codes :, :]
        weights[:, here] = pack[head : head + codes, :relay]
        there = slice((parts + k) * relay, (parts + k + 1) * relay)
        weights[:, there] = pack[head : head + codes, relay:]


def fold_kernel(groups, where, ins, outs, scratch):
    ((proj, enc),) = ins
    fold = outs[0]
    size = fold.shape[0] // groups
    fold[...] = dot(proj[...], enc[...], NT).astype(bf16)
    for k in range(groups):
        there = slice(k // 2 * size, (k // 2 + 1) * size)
        here = pl.ds(pl.multiple_of((where[1] ^ k) * size, size), size)
        outs[1 + k % 2][there, :] = fold[here, :]


def partial_kernel(where, ins, outs, scratch):
    heads, pair, (fold,) = ins
    (whole,) = scratch
    if pair:
        outs, last = outs[:-1], outs[-1]
        last[...] = pair[0][...] + pair[1][...]
        heads = [*heads, last]
    tokens = heads[0].shape[0]
    cols = outs[0].shape[1]
    parts = len(outs)
    together = 4 if len(heads) % 4 == 0 else 1
    for first in range(0, len(heads), together):
        rows = slice(first * tokens, (first + together) * tokens)
        values = jnp.concatenate([h[...] for h in heads[first : first + together]])
        whole[...] = dot(values, fold[...], NN)
        for k in range(parts):
            at = (where[0] ^ k) * cols
            outs[k][rows, :] = whole[:, pl.ds(pl.multiple_of(at, cols), cols)].astype(bf16)


def forward(received, code_mix, code_send, square, products, width):
    relay = products.shape[1] // 2
    count = received.shape[1] // relay
    mixed, unscaled = [], []
    for k in range(count):
        cols = slice(k * relay, (k + 1) * relay)
        both = dot(received[:, cols], products[cols, :], NN)
        mixed.append(code_mix[:, cols] + both[:, :relay])
        unscaled.append(code_send[:, cols] + both[:, relay:])
    mixed = jnp.concatenate(mixed, axis=1)
    unscaled = jnp.concatenate(unscaled, axis=1)
    totals = square + jnp.sum(received.astype(f32) * (code_mix + mixed), axis=1, keepdims=True)
    row_scale = lax.rsqrt(jnp.maximum(totals, 0.0) / width + epsilon)
    return mixed, unscaled, row_scale


def backward(incoming, mixed, unscaled, row_scale, products, width):
    relay = products.shape[1] // 2
    count = incoming.shape[1] // relay
    inner = row_scale * jnp.sum(incoming.astype(f32) * unscaled, axis=1, keepdims=True) / width
    returned = []
    for k in range(count):
        cols = slice(k * relay, (k + 1) * relay)
        back = dot(incoming[:, cols], products[cols, relay:], NT)
        returned.append(row_scale * (back - row_scale * inner * mixed[:, cols]))
    return inner, jnp.concatenate(returned, axis=1).astype(bf16)


def early_kernel(where, ins, outs, scratch):
    payloads, (products,) = ins
    relay = products.shape[1] // 2
    rows = outs[0].shape[0] - relay
    for k, payload in enumerate(payloads):
        cols = slice(k * relay, (k + 1) * relay)
        end = payload[payload.shape[0] - rows :, :]
        outs[0][:rows, cols] = dot(end, products[cols, relay:], NT).astype(bf16)
        outs[0][rows:, cols] = products[cols, :relay]


def split(column, lane, first):
    high = column.astype(bf16).astype(f32)
    middle = (column - high).astype(bf16).astype(f32)
    low = column - high - middle
    result = jnp.where(lane == first, high, 0.0)
    result = jnp.where(lane == first + 1, middle, result)
    return jnp.where(lane == first + 2, low, result)


def joined(lanes, first):
    return jnp.sum(lanes[:, first : first + 3].astype(f32), axis=1, keepdims=True)


def first_kernel(width, swapped, where, ins, outs, scratch):
    mix_blocks, payloads, (products, weights) = ins
    mix, ends, mix_gram, mix_recv, mix_send, square, sent = outs
    (gram,) = scratch
    codes = mix.shape[1]
    relay = products.shape[1] // 2
    parts = len(mix_blocks)
    cols = codes // parts
    for k in range(parts):
        at = pl.multiple_of((where[0] ^ k) * cols, cols)
        mix[:, pl.ds(at, cols)] = mix_blocks[k][...]
        ends[:, k * relay : (k + 1) * relay] = payloads[k][cols * codes // relay :, :]
        for j in range(codes // relay):
            piece = payloads[k][j * cols : (j + 1) * cols, :]
            gram[pl.ds(at, cols), j * relay : (j + 1) * relay] = piece

    def step(at):
        codes_here = mix[at, :]
        in_gram = dot(codes_here, gram[...], NN)
        sums = jnp.sum(in_gram * codes_here.astype(f32), axis=1, keepdims=True)
        in_relay = dot(codes_here, weights[...], NN)
        in_recv = in_relay[:, : parts * relay]
        in_send = in_relay[:, parts * relay :]
        mix_gram[at, :] = in_gram
        mix_recv[at, :] = in_recv
        mix_send[at, :] = in_send
        square[at, :] = sums
        mixed, unscaled, row_scale = forward(
            ends[at, :], in_recv, in_send, sums, products[...], width
        )
        offer = (row_scale * unscaled).astype(bf16)
        if not swapped:
            sent[at, :] = offer
            return
        wide = parts * relay
        sent[at, :wide] = jnp.where(where[2] == 0, offer, in_recv.astype(bf16))
        dots = jnp.sum(ends[at, :].astype(f32) * in_send, axis=1, keepdims=True)
        lane = lax.broadcasted_iota(jnp.int32, (sums.shape[0], relay), 1)
        sent[at, wide:] = (split(sums, lane, 0) + split(dots, lane, 3)).astype(bf16)

    by_rows(mix.shape[0], step)


def meet_kernel(width, where, ins, outs, scratch):
    ((got, early, ends, mix_recv, mix_send, mix_gram, square, products, weights),) = ins
    received_out, incoming_out, scale_out, inner_out, code_grad, sent_out, returned_out = outs
    relay = products.shape[1] // 2
    wide = ends.shape[1]
    rows = ends.shape[0]
    first = where[2] == 0

    def step(at):
        here = ends[at, :]
        given = got[at, :wide]
        received = jnp.where(first, here, given)
        mixed, unscaled, row_scale = forward(
            received, mix_recv[at, :], mix_send[at, :], square[at, :], products[...], width
        )
        sent = (row_scale * unscaled).astype(bf16)
        sent_rows = sent.astype(f32)
        other_recv = given.astype(f32)
        back = early[at, :].astype(f32)
        other_mixed = []
        for k in range(wide // relay):
            cols = slice(k * relay, (k + 1) * relay)
            other_mixed.append(other_recv[:, cols] + dot(sent[:, cols], early[rows:, cols], NN))
        other_mixed = jnp.concatenate(other_mixed, axis=1)
        lanes = got[at, wide:]
        totals = joined(lanes, 0) + jnp.sum(
            sent_rows * (other_recv + other_mixed), axis=1, keepdims=True
        )
        scale = lax.rsqrt(jnp.maximum(totals, 0.0) / width + epsilon)
        dots = joined(lanes, 3) + jnp.sum(sent_rows * back, axis=1, keepdims=True)
        inner = scale * dots / width
        returned = (scale * (back - scale * inner * other_mixed)).astype(bf16)
        incoming = jnp.where(first, returned, here)
        inner, returned = backward(incoming, mixed, unscaled, row_scale, products[...], width)
        in_mixed = mix_gram[at, :] + dot(received, weights[:, :wide], NT)
        back = dot(incoming, weights[:, wide:], NT)
        code_grad[at, :] = (row_scale * (back - row_scale * inner * in_mixed)).astype(bf16)
        received_out[at, :] = received[:, :relay]
        incoming_out[at, :] = incoming[:, :relay]
        scale_out[at, :] = row_scale
        inner_out[at, :] = inner
        tokens = min(sent_out.shape[0], sent.shape[0])
        if isinstance(at, slice):
            sent_out[...] = sent[:tokens, :relay]
            returned_out[...] = returned[:tokens, :relay]
        else:

            @pl.when(at.start == 0)
            def _():
                sent_out[...] = sent[:tokens, :relay]
                returned_out[...] = returned[:tokens, :relay]

    by_rows(rows, step)


def forward_kernel(width, turn, last, where, ins, outs, scratch):
    ((moved, received, ends, mix_recv, mix_send, square, products),) = ins
    live = where[2] == turn

    def step(at):
        values = jnp.where(live, moved[at, :], received[at, :])
        mixed, unscaled, row_scale = forward(
            values, mix_recv[at, :], mix_send[at, :], square[at, :], products[...], width
        )
        outs[0][at, :] = values
        outs[1][at, :] = (row_scale * unscaled).astype(bf16)
        if last:
            inner, returned = backward(
                ends[at, :], mixed, unscaled, row_scale, products[...], width
            )
            outs[2][at, :] = mixed
            outs[3][at, :] = unscaled
            outs[4][at, :] = row_scale
            outs[5][at, :] = returned

    by_rows(moved.shape[0], step)
    if last:
        outs[6][...] = outs[1][: outs[6].shape[0], : outs[6].shape[1]]


def backward_kernel(width, live_section, last, where, ins, outs, scratch):
    (moved, incoming, received, mixed, unscaled, row_scale, mix_gram, products, weights), = ins
    live = where[2] == live_section
    half = weights.shape[1] // 2

    def step(at):
        values = jnp.where(live, moved[at, :], incoming[at, :])
        scale = row_scale[at, :]
        inner, returned = backward(
            values, mixed[at, :], unscaled[at, :], scale, products[...], width
        )
        outs[0][at, :] = values
        outs[1][at, :] = returned
        if last:
            outs[2][at, :] = inner
            in_mixed = mix_gram[at, :] + dot(received[at, :], weights[:, :half], NT)
            back = dot(values, weights[:, half:], NT)
            outs[3][at, :] = (scale * (back - scale * inner * in_mixed)).astype(bf16)

    by_rows(moved.shape[0], step)
    if last:
        outs[4][...] = outs[1][: outs[4].shape[0], : outs[4].shape[1]]


def heads_kernel(where, ins, outs, scratch):
    ((code_grad, fold_rows),) = ins
    tokens = outs[0].shape[0]
    whole = dot(code_grad[...], fold_rows[...], NT).astype(bf16)
    for k in range(whole.shape[0] // tokens):
        value = whole[k * tokens : (k + 1) * tokens, :]
        if k % 2:
            outs[-1][k // 2 * tokens : (k // 2 + 1) * tokens, :] = value
        else:
            outs[k // 2][...] = value


def last_kernel(places, where, ins, outs, scratch):
    terms, blocks = ins
    result = terms[0][...].astype(f32)
    for term in terms[1:]:
        result = result + term[...].astype(f32)
    outs[0][...] = result.astype(bf16)
    for k, (index, row) in enumerate(places):
        size = blocks[index].shape[1]
        at = pl.multiple_of((where[1] ^ k) * size, size)
        outs[1][:, pl.ds(at, size)] = blocks[index][row : row + outs[1].shape[0], :]


def head_kernel(where, ins, outs, scratch):
    heads, (code_grad, proj) = ins
    enc_blocks = outs
    (whole,) = scratch
    tokens = heads[0].shape[0]
    together = 4 if len(heads) % 4 == 0 else 1
    sums = None
    for first in range(0, len(heads), together):
        rows = slice(first * tokens, (first + together) * tokens)
        values = jnp.concatenate([h[...] for h in heads[first : first + together]])
        term = dot(code_grad[rows, :], values, TN)
        sums = term if sums is None else sums + term
    whole[...] = dot(sums.astype(bf16), proj[...], NN)
    size = enc_blocks[0].shape[0]
    for k, out in enumerate(enc_blocks):
        at = (where[0] ^ k) * size
        out[...] = whole[pl.ds(pl.multiple_of(at, size), size), :].astype(bf16)


def turn_kernel(where, ins, outs, scratch):
    (heads,) = ins
    tokens = heads[0].shape[0]
    for k, part in enumerate(heads):
        outs[0][:, k * tokens : (k + 1) * tokens] = part[...].T


def proj_kernel(where, ins, outs, scratch):
    ((turned, code_grad, enc),) = ins
    held, sent = scratch
    size = held.shape[1]
    copies = []
    for k in range(held.shape[0]):
        rows = slice(k * size, (k + 1) * size)
        head_sum = dot(turned[rows, :], code_grad[...], NN).astype(bf16)
        held[k, :, :] = dot(head_sum, enc[...], NN).astype(bf16)
        copies.append(pltpu.make_async_copy(held.at[k], outs[0].at[rows, :], sent.at[k]))
        copies[-1].start()
    for copy in copies:
        copy.wait()


def attention_kernel(where, ins, outs, scratch):
    ((mix, dec),) = ins

    def step(at):
        outs[0][at, :] = dot(mix[at, :], dec[...], NN)

    by_rows(mix.shape[0], step)


def feature_kernel(where, ins, outs, scratch):
    ((attention, mix_cols, received, incoming, row_scale, inner, recv, send, gain),) = ins
    sums = scratch
    relay = send.shape[1]
    size = sums[0].shape[0]
    cols = slice(None)
    if mix_cols.shape[1] > size:
        cols = pl.ds(pl.multiple_of(where[1] * size, size), size)
    for ref in sums:
        ref[...] = jnp.zeros_like(ref)

    def step(at):
        received_here = received[at, :relay]
        incoming_here = incoming[at, :relay]
        normed = attention[at, :] + dot(received_here, recv[...], NN)
        normed = normed * row_scale[at, :]
        out_rows = (normed * gain[...]).astype(bf16)
        grad_norm = dot(incoming_here, send[...], NT)
        grad_mixed = row_scale[at, :] * (grad_norm * gain[...] - normed * inner[at, :])
        grad_mixed = grad_mixed.astype(bf16)
        sums[0][...] += dot(mix_cols[at, cols], grad_mixed, TN)
        sums[1][...] += jnp.sum(grad_norm * normed, axis=0, keepdims=True)
        sums[2][...] += dot(out_rows, incoming_here, TN)
        sums[3][...] += dot(received_here, grad_mixed, TN)

    by_rows(attention.shape[0], step)
    for out, ref in zip(outs, sums):
        out[...] = ref[...].astype(out.dtype)


def on_device(
    heads_out,
    out_proj,
    encoder,
    decoder,
    norm_gain,
    send_encoder,
    recv_decoder,
    input_code,
    code_cotangent,
):
    sections = lax.axis_size("pipe")
    section = lax.axis_index("pipe")
    groups = lax.axis_size("dp")
    parts = lax.axis_size("tensor")
    width = norm_gain.shape[1] * parts
    proj = out_proj[0]
    enc = encoder[0]
    dec = decoder[0]
    gain = norm_gain
    send = send_encoder[0]
    recv = recv_decoder[0]
    tokens, relay = input_code.shape
    codes, features = dec.shape
    cols = codes // parts
    rows = tokens * groups
    head_cols, model_cols = proj.shape
    where = jnp.stack([lax.axis_index("tensor"), lax.axis_index("dp"), section]).astype(jnp.int32)

    packs = run(
        gram_kernel,
        [like((cols * codes // (2 * relay) + codes + relay, 2 * relay))] * parts,
        where,
        [(dec, recv, send, gain)],
        scratch=[pltpu.VMEM((codes, codes), f32)],
        fetch=True,
    )
    half = like((head_cols // 2, codes))
    fold, fold_kept, fold_given = run(
        functools.partial(fold_kernel, groups),
        [like((head_cols, codes)), half, half],
        where,
        [(proj, enc)],
        fetch=True,
    )
    fold, _ = lax.optimization_barrier((fold, packs[0]))
    end = jnp.where(section == 0, input_code, code_cotangent)
    heads, pair, ends = line_gathered(heads_out[0], end, fold, "dp")
    packs = scattered(packs, "tensor")

    partials = run(
        partial_kernel,
        [like((rows, cols))] * parts + [like((tokens, head_cols))] * (len(pair) // 2),
        where,
        [heads, pair, (fold,)],
        scratch=[pltpu.VMEM((min(groups, 4) * tokens, codes), f32)],
        flops=2 * rows * head_cols * codes,
    )
    partials, heads = list(partials[:parts]), [*heads, *partials[parts:]]
    partials[-1], *_ = lax.optimization_barrier((partials[-1], *packs))
    fold_given, partials, ends = lax.optimization_barrier((fold_given, partials, ends))
    fold_other = swap(fold_given, "dp", 1)
    arrived = scattered(partials, "tensor")
    arrived, ends = lax.optimization_barrier((arrived, ends))
    code_block = total(arrived, where)
    fold_terms = halved(fold_kept, fold_other, head_cols // groups, where)
    wide = parts * relay
    packs, _ = lax.optimization_barrier((packs, code_block))
    payload, products, weights = run(
        setup_kernel,
        [
            like((cols * codes // relay + rows, relay)),
            like((wide, 2 * relay)),
            like((codes, 2 * wide)),
        ],
        where,
        [packs, ends],
    )
    payloads = gathered(payload, "tensor")
    (turned,) = run(turn_kernel, [like((head_cols, rows))], where, [heads])
    mix_block = group_sum(code_block, [*payloads, *fold_terms, turned], "dp", where)
    mix_block, fold_terms = lax.optimization_barrier((mix_block, fold_terms))
    mix_blocks = gathered(mix_block, "tensor")
    if sections == 2:
        (early,) = run(early_kernel, [like((rows + relay, wide))], where, [payloads, (products,)])
        early = move(early, "pipe", -1)

    square_flops = 2 * rows * codes * codes
    mix, ends, mix_gram, mix_recv, mix_send, square, sent = run(
        functools.partial(first_kernel, width, sections == 2),
        [
            like((rows, codes)),
            like((rows, wide)),
            like((rows, codes), f32),
            like((rows, wide), f32),
            like((rows, wide), f32),
            like((rows, 1), f32),
            like((rows, wide + relay if sections == 2 else wide)),
        ],
        where,
        [mix_blocks, payloads, (products, weights)],
        scratch=[pltpu.VMEM((codes, codes), bf16)],
        flops=3 * square_flops,
    )
    step = 2
    while step < groups:
        kept, given = fold_terms
        other = swap(given, "dp", step)
        step *= 2
        if step < groups:
            fold_terms = halved(kept, other, head_cols // groups, where)
        else:
            fold_rows = total([kept, other], where, flops=1 << 32)
    (attention,) = run(
        attention_kernel, [like((rows, features), f32)], where, [(mix, dec)]
    )
    if sections == 2:
        got = lax.ppermute(sent, "pipe", [(0, 1), (1, 0)])
        got, fold_rows, attention = lax.optimization_barrier((got, fold_rows, attention))
        received, incoming, row_scale, inner, code_grad, sent, returned = run(
            functools.partial(meet_kernel, width),
            [
                like((rows, relay)),
                like((rows, relay)),
                like((rows, 1), f32),
                like((rows, 1), f32),
                like((rows, codes)),
                like((tokens, relay)),
                like((tokens, relay)),
            ],
            where,
            [(got, early, ends, mix_recv, mix_send, mix_gram, square, products, weights)],
            flops=4 * square_flops,
        )
    else:
        received = ends
        for turn in range(1, sections):
            last = turn == sections - 1
            shapes = [like((rows, wide)), like((rows, wide))]
            if last:
                shapes += [like((rows, wide), f32)] * 2 + [like((rows, 1), f32), like((rows, wide))]
                shapes += [like((tokens, relay))]
            moved = move(sent, "pipe", 1)
            results = run(
                functools.partial(forward_kernel, width, turn, last),
                shapes,
                where,
                [(moved, received, ends, mix_recv, mix_send, square, products)],
                flops=square_flops,
            )
            received, sent = results[:2]
        mixed, unscaled, row_scale, returned, sent = results[2:]
        incoming = ends
        for turn in range(1, sections):
            last = turn == sections - 1
            shapes = [like((rows, wide)), like((rows, wide))]
            if last:
                shapes += [like((rows, 1), f32), like((rows, codes))]
                shapes += [like((tokens, relay))]
            moved = move(returned, "pipe", -1)
            results = run(
                functools.partial(backward_kernel, width, sections - 1 - turn, last),
                shapes,
                where,
                [
                    (
                        moved,
                        incoming,
                        received,
                        mixed,
                        unscaled,
                        row_scale,
                        mix_gram,
                        products,
                        weights,
                    )
                ],
                flops=3 * square_flops,
            )
            incoming, returned = results[:2]
        inner, code_grad, returned = results[2:]

    enc_blocks = run(
        head_kernel,
        [like((cols, model_cols))] * parts,
        where,
        [heads, (code_grad, proj)],
        scratch=[pltpu.VMEM((codes, model_cols), f32)],
        flops=2 * head_cols * codes * (rows + model_cols),
    )
    code_grad, mix, turned, enc_blocks = lax.optimization_barrier(
        (code_grad, mix, turned, enc_blocks)
    )
    enc_blocks = scattered(enc_blocks, "tensor")
    size = head_cols // groups
    *kept, given = run(
        heads_kernel,
        [like((tokens, size))] * (groups // 2) + [like((rows // 2, size))],
        where,
        [(code_grad, fold_rows)],
    )
    given, mix, turned = lax.optimization_barrier((given, mix, turned))
    head_blocks = exchanged(kept, given, tokens, "dp")
    (proj_grad,) = run(
        proj_kernel,
        [like((head_cols, model_cols))],
        where,
        [(turned, code_grad, enc)],
        scratch=[
            pltpu.VMEM((2, head_cols // 2, model_cols), bf16),
            pltpu.SemaphoreType.DMA((2,)),
        ],
        store=True,
    )
    shapes = [(codes // groups, features), (1, features), (features, relay), (relay, features)]
    dec_grad, gain_grad, send_grad, recv_grad = run(
        feature_kernel,
        [like(shape, f32 if k == 1 else bf16) for k, shape in enumerate(shapes)],
        where,
        [
            (
                attention,
                mix if codes // groups % 128 == 0 else block(mix, "dp", 1),
                received,
                incoming,
                row_scale,
                inner,
                recv,
                send,
                gain,
            )
        ],
        scratch=[pltpu.VMEM(shape, f32) for shape in shapes],
    )
    if size % 128 == 0:
        arrays = []
        for array, _ in head_blocks:
            if not any(array is other for other in arrays):
                arrays.append(array)
        places = [
            (next(k for k, other in enumerate(arrays) if other is array), row)
            for array, row in head_blocks
        ]
        enc_grad, heads_grad = run(
            functools.partial(last_kernel, places),
            [like((cols, model_cols)), like((tokens, head_cols))],
            where,
            [enc_blocks, arrays],
        )
    else:
        enc_grad = total(enc_blocks, where)
        blocks = [array[row : row + tokens] for array, row in head_blocks]
        heads_grad = ordered(blocks, "dp")
    return (
        sent[None],
        returned[None],
        heads_grad[None],
        proj_grad[None],
        enc_grad[None],
        dec_grad[None],
        gain_grad,
        send_grad[None],
        recv_grad[None],
    )


def solution(mesh):
    return jax.shard_map(
        on_device,
        mesh=mesh,
        in_specs=(
            P("pipe", "dp", "tensor"),
            P("pipe", "tensor", "dp"),
            P("pipe", None, "dp"),
            P("pipe", None, "tensor"),
            P("pipe", "tensor"),
            P("pipe", "tensor", None),
            P("pipe", None, "tensor"),
            P("dp", "tensor"),
            P("dp", "tensor"),
        ),
        out_specs=(
            P("pipe", "dp", "tensor"),
            P("pipe", "dp", "tensor"),
            P("pipe", "dp", "tensor"),
            P("pipe", "tensor", "dp"),
            P("pipe", "tensor", "dp"),
            P("pipe", "dp", "tensor"),
            P("pipe", "tensor"),
            P("pipe", "tensor", None),
            P("pipe", None, "tensor"),
        ),
        check_vma=False,
    )
```

```python
import functools

import jax
import jax.numpy as jnp
from jax import lax
from jax.experimental import pallas as pl
from jax.experimental.pallas import tpu as pltpu
from jax.sharding import PartitionSpec as P

epsilon = 1e-05
f32 = jnp.float32
bf16 = jnp.bfloat16
NN = ((1,), (0,))
NT = ((1,), (1,))
TN = ((0,), (0,))


def swap(shard, axis, by):
    return lax.ppermute(shard, axis, [(i, i ^ by) for i in range(lax.axis_size(axis))])


def move(shard, axis, by):
    devices = lax.axis_size(axis)
    pairs = [(i, i + by) for i in range(devices) if 0 <= i + by < devices]
    return lax.ppermute(shard, axis, pairs)


def gathered(shard, axis):
    return [shard] + [swap(shard, axis, k) for k in range(1, lax.axis_size(axis))]


def line_gathered(shard, small, after, axis):
    if lax.axis_size(axis) != 4:
        return gathered(shard, axis), [], gathered(small, axis)
    far, near = swap(shard, axis, 2), swap(shard, axis, 1)
    beside = swap(small, axis, 1)
    shard, far, near, beside = lax.optimization_barrier((shard, far, near, beside))
    across = lax.ppermute(shard, axis, [(1, 2), (2, 1)])
    passed = lax.ppermute(far, axis, [(1, 0), (2, 3)])
    both = jnp.concatenate([small, beside])
    both, across, passed, _ = lax.optimization_barrier((both, across, passed, after))
    return [shard, near, far], [across, passed], [small, beside, swap(both, axis, 2)]


def scattered(blocks, axis):
    return [blocks[0]] + [swap(blocks[k], axis, k) for k in range(1, len(blocks))]


def group_sum(rows, after, axis, where):
    groups = lax.axis_size(axis)
    step = groups // 2
    while step:
        other = swap(rows, axis, step)
        if step == 1:
            other, *_ = lax.optimization_barrier((other, *after))
        kernel = functools.partial(moved_sum_kernel, groups, step)
        (rows,) = run(kernel, [like(rows.shape)], where, [(rows, other)])
        step //= 2
    return rows


def exchanged(kept, given, after, size, axis):
    count = lax.axis_size(axis)
    parts = [[(part, 0) for part in kept]]
    step = 1
    while True:
        arrived = swap(given, axis, step)
        left = count // (2 * step)
        parts += [
            [(arrived, (j * left + k) * size) for k in range(left)] for j in range(len(parts))
        ]
        step *= 2
        if step == count:
            return [part[0] for part in parts], after
        given = [array[row : row + size] for part in parts for array, row in part[1::2]]
        given, after = lax.optimization_barrier((jnp.concatenate(given), after))
        parts = [part[::2] for part in parts]


def halved(mine, other, size, where):
    half = like((mine.shape[0] // 2, mine.shape[1]))
    return run(functools.partial(halved_kernel, size), [half, half], where, [(mine, other)])


def total(blocks, where, flops=0):
    return run(total_kernel, [like(blocks[0].shape)], where, [blocks], flops=flops)[0]


def ordered(blocks, axis):
    step = 1
    while step < len(blocks):
        odd = (lax.axis_index(axis) & step) > 0
        blocks = [jnp.where(odd, blocks[k ^ step], part) for k, part in enumerate(blocks)]
        step *= 2
    return jnp.concatenate(blocks, axis=1)


def block(array, axis, dim):
    size = array.shape[dim] // lax.axis_size(axis)
    return lax.dynamic_slice_in_dim(array, lax.axis_index(axis) * size, size, dim)


def dot(left, right, over):
    return lax.dot_general(left, right, (over, ((), ())), preferred_element_type=f32)


def run(kernel, results, where, groups_of_args, scratch=(), flops=0, fetch=False, store=False):
    counts = [len(group) for group in groups_of_args]
    flat = [array for group in groups_of_args for array in group]
    out_count = len(results)
    scratch = list(scratch)
    own = len(scratch)
    space = pltpu.HBM if fetch else pltpu.VMEM
    if fetch:
        scratch += [pltpu.VMEM(array.shape, array.dtype) for array in flat]
        scratch.append(pltpu.SemaphoreType.DMA((len(flat),)))

    def body(where_ref, *refs):
        args, refs = refs[: len(flat)], refs[len(flat) :]
        outs, refs = refs[:out_count], refs[out_count:]
        if fetch:
            held, arrived = refs[own:-1], refs[-1]
            copies = [
                pltpu.make_async_copy(arg, here, arrived.at[k])
                for k, (arg, here) in enumerate(zip(args, held))
            ]
            for copy in copies:
                copy.start()
            for copy in copies:
                copy.wait()
            args = held
        ins, at = [], 0
        for count in counts:
            ins.append(args[at : at + count])
            at += count
        kernel(where_ref, ins, outs, refs[:own])

    if fetch:
        flat = [pltpu.with_memory_space_constraint(array, pltpu.HBM) for array in flat]
    size = sum(a.size * a.dtype.itemsize for a in list(flat) + list(results))
    limit = (10 << 20) if size < (10 << 20) else size + (12 << 20)
    return pl.pallas_call(
        body,
        out_shape=[jax.ShapeDtypeStruct(r.shape, r.dtype) for r in results],
        in_specs=[pl.BlockSpec(memory_space=pltpu.SMEM)]
        + [pl.BlockSpec(memory_space=space)] * len(flat),
        out_specs=[pl.BlockSpec(memory_space=pltpu.HBM if store else pltpu.VMEM)] * out_count,
        scratch_shapes=scratch,
        compiler_params=pltpu.CompilerParams(vmem_limit_bytes=limit),
        cost_estimate=pl.CostEstimate(
            flops=flops, bytes_accessed=size if flops else 0, transcendentals=0
        ),
    )(where, *flat)


def like(shape, dtype=bf16):
    return jax.ShapeDtypeStruct(shape, dtype)


def by_rows(rows, step):
    chunk = min(rows, 512)
    if rows == chunk:
        step(slice(0, rows))
        return

    @pl.loop(0, rows // chunk)
    def _(index):
        step(pl.ds(pl.multiple_of(index * chunk, chunk), chunk))


def total_kernel(where, ins, outs, scratch):
    (blocks,) = ins
    result = blocks[0][...].astype(f32)
    for part in blocks[1:]:
        result = result + part[...].astype(f32)
    outs[0][...] = result.astype(bf16)


def moved_sum_kernel(groups, step, where, ins, outs, scratch):
    ((mine, other),) = ins
    size = mine.shape[0] // groups
    for k in range(groups):
        here = slice(k * size, (k + 1) * size)
        there = slice((k ^ step) * size, ((k ^ step) + 1) * size)
        value = mine[here, :].astype(f32) + other[there, :].astype(f32)
        outs[0][here, :] = value.astype(bf16)


def halved_kernel(size, where, ins, outs, scratch):
    ((mine, other),) = ins
    for k in range(mine.shape[0] // size):
        here = slice(k * size, (k + 1) * size)
        there = slice(k // 2 * size, (k // 2 + 1) * size)
        value = mine[here, :].astype(f32) + other[here, :].astype(f32)
        outs[k % 2][there, :] = value.astype(bf16)


def gram_kernel(where, ins, outs, scratch):
    ((dec, recv, send, gain),) = ins
    (whole,) = scratch
    codes, relay = dec.shape[0], recv.shape[0]
    cols = codes // len(outs)
    wide = 2 * relay
    head = cols * codes // wide
    whole[...] = dot(dec[...], dec[...], NT)
    for k, out in enumerate(outs):
        rows = pl.ds(pl.multiple_of((where[0] ^ k) * cols, cols), cols)
        for j in range(codes // wide):
            piece = whole[rows, j * wide : (j + 1) * wide]
            out[j * cols : (j + 1) * cols, :] = piece.astype(bf16)
    for ref, rows in ((dec, slice(head, head + codes)), (recv, slice(head + codes, None))):
        values = ref[...]
        gained = (values.astype(f32) * gain[...]).astype(bf16)
        plain = dot(values, recv[...], NT).astype(bf16)
        scaled = dot(gained, send[...], NN).astype(bf16)
        for out in outs:
            out[rows, :relay] = plain
            out[rows, relay:] = scaled


def setup_kernel(where, ins, outs, scratch):
    packs, ends = ins
    payload, products, weights = outs
    parts = len(packs)
    wide = products.shape[1]
    relay = wide // 2
    codes = weights.shape[0]
    cols = codes // parts
    head = cols * codes // wide
    for j in range(codes // wide):
        rows = slice(j * cols, (j + 1) * cols)
        gram = packs[0][rows, :].astype(f32)
        for pack in packs[1:]:
            gram = gram + pack[rows, :].astype(f32)
        gram = gram.astype(bf16)
        payload[2 * j * cols : (2 * j + 1) * cols, :] = gram[:, :relay]
        payload[(2 * j + 1) * cols : (2 * j + 2) * cols, :] = gram[:, relay:]
    start = 2 * head
    for end in ends:
        payload[start : start + end.shape[0], :] = end[...]
        start += end.shape[0]
    for k, pack in enumerate(packs):
        here = slice(k * relay, (k + 1) * relay)
        products[here, :] = pack[head + codes :, :]
        weights[:, here] = pack[head : head + codes, :relay]
        there = slice((parts + k) * relay, (parts + k + 1) * relay)
        weights[:, there] = pack[head : head + codes, relay:]


def fold_kernel(groups, where, ins, outs, scratch):
    ((proj, enc),) = ins
    fold = outs[0]
    size = fold.shape[0] // groups
    fold[...] = dot(proj[...], enc[...], NT).astype(bf16)
    for k in range(groups):
        there = slice(k // 2 * size, (k // 2 + 1) * size)
        here = pl.ds(pl.multiple_of((where[1] ^ k) * size, size), size)
        outs[1 + k % 2][there, :] = fold[here, :]


def partial_kernel(where, ins, outs, scratch):
    heads, pair, (fold,) = ins
    (whole,) = scratch
    if pair:
        outs, last = outs[:-1], outs[-1]
        last[...] = pair[0][...] + pair[1][...]
        heads = [*heads, last]
    tokens = heads[0].shape[0]
    cols = outs[0].shape[1]
    parts = len(outs)
    together = 4 if len(heads) % 4 == 0 else 1
    for first in range(0, len(heads), together):
        rows = slice(first * tokens, (first + together) * tokens)
        values = jnp.concatenate([h[...] for h in heads[first : first + together]])
        whole[...] = dot(values, fold[...], NN)
        for k in range(parts):
            at = (where[0] ^ k) * cols
            outs[k][rows, :] = whole[:, pl.ds(pl.multiple_of(at, cols), cols)].astype(bf16)


def forward(received, code_mix, code_send, square, products, width):
    relay = products.shape[1] // 2
    count = received.shape[1] // relay
    mixed, unscaled = [], []
    for k in range(count):
        cols = slice(k * relay, (k + 1) * relay)
        both = dot(received[:, cols], products[cols, :], NN)
        mixed.append(code_mix[:, cols] + both[:, :relay])
        unscaled.append(code_send[:, cols] + both[:, relay:])
    mixed = jnp.concatenate(mixed, axis=1)
    unscaled = jnp.concatenate(unscaled, axis=1)
    totals = square + jnp.sum(received.astype(f32) * (code_mix + mixed), axis=1, keepdims=True)
    row_scale = lax.rsqrt(jnp.maximum(totals, 0.0) / width + epsilon)
    return mixed, unscaled, row_scale


def backward(incoming, mixed, unscaled, row_scale, products, width):
    relay = products.shape[1] // 2
    count = incoming.shape[1] // relay
    inner = row_scale * jnp.sum(incoming.astype(f32) * unscaled, axis=1, keepdims=True) / width
    returned = []
    for k in range(count):
        cols = slice(k * relay, (k + 1) * relay)
        back = dot(incoming[:, cols], products[cols, relay:], NT)
        returned.append(row_scale * (back - row_scale * inner * mixed[:, cols]))
    return inner, jnp.concatenate(returned, axis=1).astype(bf16)


def early_kernel(where, ins, outs, scratch):
    payloads, (products,) = ins
    relay = products.shape[1] // 2
    rows = outs[0].shape[0] - relay
    for k, payload in enumerate(payloads):
        cols = slice(k * relay, (k + 1) * relay)
        end = payload[payload.shape[0] - rows :, :]
        outs[0][:rows, cols] = dot(end, products[cols, relay:], NT).astype(bf16)
        outs[0][rows:, cols] = products[cols, :relay]


def split(column, lane, first):
    high = column.astype(bf16).astype(f32)
    middle = (column - high).astype(bf16).astype(f32)
    low = column - high - middle
    result = jnp.where(lane == first, high, 0.0)
    result = jnp.where(lane == first + 1, middle, result)
    return jnp.where(lane == first + 2, low, result)


def joined(lanes, first):
    return jnp.sum(lanes[:, first : first + 3].astype(f32), axis=1, keepdims=True)


def first_kernel(width, swapped, where, ins, outs, scratch):
    mix_blocks, payloads, (products, weights) = ins
    mix, ends, mix_gram, mix_recv, mix_send, square, sent = outs
    (gram,) = scratch
    codes = mix.shape[1]
    relay = products.shape[1] // 2
    parts = len(mix_blocks)
    cols = codes // parts
    for k in range(parts):
        at = pl.multiple_of((where[0] ^ k) * cols, cols)
        mix[:, pl.ds(at, cols)] = mix_blocks[k][...]
        ends[:, k * relay : (k + 1) * relay] = payloads[k][cols * codes // relay :, :]
        for j in range(codes // relay):
            piece = payloads[k][j * cols : (j + 1) * cols, :]
            gram[pl.ds(at, cols), j * relay : (j + 1) * relay] = piece

    def step(at):
        codes_here = mix[at, :]
        in_gram = dot(codes_here, gram[...], NN)
        sums = jnp.sum(in_gram * codes_here.astype(f32), axis=1, keepdims=True)
        in_relay = dot(codes_here, weights[...], NN)
        in_recv = in_relay[:, : parts * relay]
        in_send = in_relay[:, parts * relay :]
        mix_gram[at, :] = in_gram
        mix_recv[at, :] = in_recv
        mix_send[at, :] = in_send
        square[at, :] = sums
        mixed, unscaled, row_scale = forward(
            ends[at, :], in_recv, in_send, sums, products[...], width
        )
        offer = (row_scale * unscaled).astype(bf16)
        if not swapped:
            sent[at, :] = offer
            return
        wide = parts * relay
        sent[at, :wide] = jnp.where(where[2] == 0, offer, in_recv.astype(bf16))
        dots = jnp.sum(ends[at, :].astype(f32) * in_send, axis=1, keepdims=True)
        lane = lax.broadcasted_iota(jnp.int32, (sums.shape[0], relay), 1)
        sent[at, wide:] = (split(sums, lane, 0) + split(dots, lane, 3)).astype(bf16)

    by_rows(mix.shape[0], step)


def meet_kernel(width, where, ins, outs, scratch):
    ((got, early, ends, mix_recv, mix_send, mix_gram, square, products, weights),) = ins
    received_out, incoming_out, scale_out, inner_out, code_grad, sent_out, returned_out = outs
    relay = products.shape[1] // 2
    wide = ends.shape[1]
    rows = ends.shape[0]
    first = where[2] == 0

    def step(at):
        here = ends[at, :]
        given = got[at, :wide]
        received = jnp.where(first, here, given)
        mixed, unscaled, row_scale = forward(
            received, mix_recv[at, :], mix_send[at, :], square[at, :], products[...], width
        )
        sent = (row_scale * unscaled).astype(bf16)
        sent_rows = sent.astype(f32)
        other_recv = given.astype(f32)
        back = early[at, :].astype(f32)
        other_mixed = []
        for k in range(wide // relay):
            cols = slice(k * relay, (k + 1) * relay)
            other_mixed.append(other_recv[:, cols] + dot(sent[:, cols], early[rows:, cols], NN))
        other_mixed = jnp.concatenate(other_mixed, axis=1)
        lanes = got[at, wide:]
        totals = joined(lanes, 0) + jnp.sum(
            sent_rows * (other_recv + other_mixed), axis=1, keepdims=True
        )
        scale = lax.rsqrt(jnp.maximum(totals, 0.0) / width + epsilon)
        dots = joined(lanes, 3) + jnp.sum(sent_rows * back, axis=1, keepdims=True)
        inner = scale * dots / width
        returned = (scale * (back - scale * inner * other_mixed)).astype(bf16)
        incoming = jnp.where(first, returned, here)
        inner, returned = backward(incoming, mixed, unscaled, row_scale, products[...], width)
        in_mixed = mix_gram[at, :] + dot(received, weights[:, :wide], NT)
        back = dot(incoming, weights[:, wide:], NT)
        code_grad[at, :] = (row_scale * (back - row_scale * inner * in_mixed)).astype(bf16)
        received_out[at, :] = received[:, :relay]
        incoming_out[at, :] = incoming[:, :relay]
        scale_out[at, :] = row_scale
        inner_out[at, :] = inner
        tokens = min(sent_out.shape[0], sent.shape[0])
        if isinstance(at, slice):
            sent_out[...] = sent[:tokens, :relay]
            returned_out[...] = returned[:tokens, :relay]
        else:

            @pl.when(at.start == 0)
            def _():
                sent_out[...] = sent[:tokens, :relay]
                returned_out[...] = returned[:tokens, :relay]

    by_rows(rows, step)


def forward_kernel(width, turn, last, where, ins, outs, scratch):
    ((moved, received, ends, mix_recv, mix_send, square, products),) = ins
    live = where[2] == turn

    def step(at):
        values = jnp.where(live, moved[at, :], received[at, :])
        mixed, unscaled, row_scale = forward(
            values, mix_recv[at, :], mix_send[at, :], square[at, :], products[...], width
        )
        outs[0][at, :] = values
        outs[1][at, :] = (row_scale * unscaled).astype(bf16)
        if last:
            inner, returned = backward(
                ends[at, :], mixed, unscaled, row_scale, products[...], width
            )
            outs[2][at, :] = mixed
            outs[3][at, :] = unscaled
            outs[4][at, :] = row_scale
            outs[5][at, :] = returned

    by_rows(moved.shape[0], step)
    if last:
        outs[6][...] = outs[1][: outs[6].shape[0], : outs[6].shape[1]]


def backward_kernel(width, live_section, last, where, ins, outs, scratch):
    (moved, incoming, received, mixed, unscaled, row_scale, mix_gram, products, weights), = ins
    live = where[2] == live_section
    half = weights.shape[1] // 2

    def step(at):
        values = jnp.where(live, moved[at, :], incoming[at, :])
        scale = row_scale[at, :]
        inner, returned = backward(
            values, mixed[at, :], unscaled[at, :], scale, products[...], width
        )
        outs[0][at, :] = values
        outs[1][at, :] = returned
        if last:
            outs[2][at, :] = inner
            in_mixed = mix_gram[at, :] + dot(received[at, :], weights[:, :half], NT)
            back = dot(values, weights[:, half:], NT)
            outs[3][at, :] = (scale * (back - scale * inner * in_mixed)).astype(bf16)

    by_rows(moved.shape[0], step)
    if last:
        outs[4][...] = outs[1][: outs[4].shape[0], : outs[4].shape[1]]


def heads_kernel(where, ins, outs, scratch):
    ((code_grad, fold_rows),) = ins
    tokens = outs[0].shape[0]
    whole = dot(code_grad[...], fold_rows[...], NT).astype(bf16)
    for k in range(whole.shape[0] // tokens):
        value = whole[k * tokens : (k + 1) * tokens, :]
        if k % 2:
            outs[-1][k // 2 * tokens : (k // 2 + 1) * tokens, :] = value
        else:
            outs[k // 2][...] = value


def last_kernel(places, where, ins, outs, scratch):
    (blocks,) = ins
    for k, (index, row) in enumerate(places):
        size = blocks[index].shape[1]
        at = pl.multiple_of((where[1] ^ k) * size, size)
        outs[0][:, pl.ds(at, size)] = blocks[index][row : row + outs[0].shape[0], :]


def head_kernel(where, ins, outs, scratch):
    heads, (code_grad, proj) = ins
    enc_blocks = outs
    (whole,) = scratch
    tokens = heads[0].shape[0]
    together = 4 if len(heads) % 4 == 0 else 1
    sums = None
    for first in range(0, len(heads), together):
        rows = slice(first * tokens, (first + together) * tokens)
        values = jnp.concatenate([h[...] for h in heads[first : first + together]])
        term = dot(code_grad[rows, :], values, TN)
        sums = term if sums is None else sums + term
    whole[...] = dot(sums.astype(bf16), proj[...], NN)
    size = enc_blocks[0].shape[0]
    for k, out in enumerate(enc_blocks):
        at = (where[0] ^ k) * size
        out[...] = whole[pl.ds(pl.multiple_of(at, size), size), :].astype(bf16)


def turn_kernel(where, ins, outs, scratch):
    (heads,) = ins
    tokens = heads[0].shape[0]
    for k, part in enumerate(heads):
        outs[0][:, k * tokens : (k + 1) * tokens] = part[...].T


def proj_kernel(where, ins, outs, scratch):
    ((turned, code_grad, enc),) = ins
    held, sent = scratch
    size = held.shape[1]
    copies = []
    for k in range(held.shape[0]):
        rows = slice(k * size, (k + 1) * size)
        head_sum = dot(turned[rows, :], code_grad[...], NN).astype(bf16)
        held[k, :, :] = dot(head_sum, enc[...], NN).astype(bf16)
        copies.append(pltpu.make_async_copy(held.at[k], outs[0].at[rows, :], sent.at[k]))
        copies[-1].start()
    for copy in copies:
        copy.wait()


def attention_kernel(where, ins, outs, scratch):
    ((mix, dec),) = ins

    def step(at):
        outs[0][at, :] = dot(mix[at, :], dec[...], NN)

    by_rows(mix.shape[0], step)


def feature_kernel(where, ins, outs, scratch):
    ((attention, mix_cols, received, incoming, row_scale, inner, recv, send, gain),) = ins
    sums = scratch
    relay = send.shape[1]
    size = sums[0].shape[0]
    cols = slice(None)
    if mix_cols.shape[1] > size:
        cols = pl.ds(pl.multiple_of(where[1] * size, size), size)
    for ref in sums:
        ref[...] = jnp.zeros_like(ref)

    def step(at):
        received_here = received[at, :relay]
        incoming_here = incoming[at, :relay]
        normed = attention[at, :] + dot(received_here, recv[...], NN)
        normed = normed * row_scale[at, :]
        out_rows = (normed * gain[...]).astype(bf16)
        grad_norm = dot(incoming_here, send[...], NT)
        grad_mixed = row_scale[at, :] * (grad_norm * gain[...] - normed * inner[at, :])
        grad_mixed = grad_mixed.astype(bf16)
        sums[0][...] += dot(mix_cols[at, cols], grad_mixed, TN)
        sums[1][...] += jnp.sum(grad_norm * normed, axis=0, keepdims=True)
        sums[2][...] += dot(out_rows, incoming_here, TN)
        sums[3][...] += dot(received_here, grad_mixed, TN)

    by_rows(attention.shape[0], step)
    for out, ref in zip(outs, sums):
        out[...] = ref[...].astype(out.dtype)


def on_device(
    heads_out,
    out_proj,
    encoder,
    decoder,
    norm_gain,
    send_encoder,
    recv_decoder,
    input_code,
    code_cotangent,
):
    sections = lax.axis_size("pipe")
    section = lax.axis_index("pipe")
    groups = lax.axis_size("dp")
    parts = lax.axis_size("tensor")
    width = norm_gain.shape[1] * parts
    proj = out_proj[0]
    enc = encoder[0]
    dec = decoder[0]
    gain = norm_gain
    send = send_encoder[0]
    recv = recv_decoder[0]
    tokens, relay = input_code.shape
    codes, features = dec.shape
    cols = codes // parts
    rows = tokens * groups
    head_cols, model_cols = proj.shape
    where = jnp.stack([lax.axis_index("tensor"), lax.axis_index("dp"), section]).astype(jnp.int32)

    packs = run(
        gram_kernel,
        [like((cols * codes // (2 * relay) + codes + relay, 2 * relay))] * parts,
        where,
        [(dec, recv, send, gain)],
        scratch=[pltpu.VMEM((codes, codes), f32)],
        fetch=True,
    )
    half = like((head_cols // 2, codes))
    fold, fold_kept, fold_given = run(
        functools.partial(fold_kernel, groups),
        [like((head_cols, codes)), half, half],
        where,
        [(proj, enc)],
        fetch=True,
    )
    fold, _ = lax.optimization_barrier((fold, packs[0]))
    end = jnp.where(section == 0, input_code, code_cotangent)
    heads, pair, ends = line_gathered(heads_out[0], end, fold, "dp")
    packs = scattered(packs, "tensor")

    partials = run(
        partial_kernel,
        [like((rows, cols))] * parts + [like((tokens, head_cols))] * (len(pair) // 2),
        where,
        [heads, pair, (fold,)],
        scratch=[pltpu.VMEM((min(groups, 4) * tokens, codes), f32)],
        flops=2 * rows * head_cols * codes,
    )
    partials, heads = list(partials[:parts]), [*heads, *partials[parts:]]
    partials[-1], *_ = lax.optimization_barrier((partials[-1], *packs))
    fold_given, partials, ends = lax.optimization_barrier((fold_given, partials, ends))
    fold_other = swap(fold_given, "dp", 1)
    arrived = scattered(partials, "tensor")
    arrived, ends = lax.optimization_barrier((arrived, ends))
    code_block = total(arrived, where)
    fold_terms = halved(fold_kept, fold_other, head_cols // groups, where)
    wide = parts * relay
    packs, _ = lax.optimization_barrier((packs, code_block))
    payload, products, weights = run(
        setup_kernel,
        [
            like((cols * codes // relay + rows, relay)),
            like((wide, 2 * relay)),
            like((codes, 2 * wide)),
        ],
        where,
        [packs, ends],
    )
    payloads = gathered(payload, "tensor")
    (turned,) = run(turn_kernel, [like((head_cols, rows))], where, [heads])
    mix_block = group_sum(code_block, [*payloads, *fold_terms, turned], "dp", where)
    mix_block, fold_terms = lax.optimization_barrier((mix_block, fold_terms))
    mix_blocks = gathered(mix_block, "tensor")
    if sections == 2:
        (early,) = run(early_kernel, [like((rows + relay, wide))], where, [payloads, (products,)])
        early = move(early, "pipe", -1)

    square_flops = 2 * rows * codes * codes
    mix, ends, mix_gram, mix_recv, mix_send, square, sent = run(
        functools.partial(first_kernel, width, sections == 2),
        [
            like((rows, codes)),
            like((rows, wide)),
            like((rows, codes), f32),
            like((rows, wide), f32),
            like((rows, wide), f32),
            like((rows, 1), f32),
            like((rows, wide + relay if sections == 2 else wide)),
        ],
        where,
        [mix_blocks, payloads, (products, weights)],
        scratch=[pltpu.VMEM((codes, codes), bf16)],
        flops=3 * square_flops,
    )
    step = 2
    while step < groups:
        kept, given = fold_terms
        other = swap(given, "dp", step)
        step *= 2
        if step < groups:
            fold_terms = halved(kept, other, head_cols // groups, where)
        else:
            fold_rows = total([kept, other], where, flops=1 << 33)
    (attention,) = run(
        attention_kernel, [like((rows, features), f32)], where, [(mix, dec)]
    )
    if sections == 2:
        got = lax.ppermute(sent, "pipe", [(0, 1), (1, 0)])
        got, fold_rows, attention = lax.optimization_barrier((got, fold_rows, attention))
        received, incoming, row_scale, inner, code_grad, sent, returned = run(
            functools.partial(meet_kernel, width),
            [
                like((rows, relay)),
                like((rows, relay)),
                like((rows, 1), f32),
                like((rows, 1), f32),
                like((rows, codes)),
                like((tokens, relay)),
                like((tokens, relay)),
            ],
            where,
            [(got, early, ends, mix_recv, mix_send, mix_gram, square, products, weights)],
            flops=4 * square_flops,
        )
    else:
        received = ends
        for turn in range(1, sections):
            last = turn == sections - 1
            shapes = [like((rows, wide)), like((rows, wide))]
            if last:
                shapes += [like((rows, wide), f32)] * 2 + [like((rows, 1), f32), like((rows, wide))]
                shapes += [like((tokens, relay))]
            moved = move(sent, "pipe", 1)
            results = run(
                functools.partial(forward_kernel, width, turn, last),
                shapes,
                where,
                [(moved, received, ends, mix_recv, mix_send, square, products)],
                flops=square_flops,
            )
            received, sent = results[:2]
        mixed, unscaled, row_scale, returned, sent = results[2:]
        incoming = ends
        for turn in range(1, sections):
            last = turn == sections - 1
            shapes = [like((rows, wide)), like((rows, wide))]
            if last:
                shapes += [like((rows, 1), f32), like((rows, codes))]
                shapes += [like((tokens, relay))]
            moved = move(returned, "pipe", -1)
            results = run(
                functools.partial(backward_kernel, width, sections - 1 - turn, last),
                shapes,
                where,
                [
                    (
                        moved,
                        incoming,
                        received,
                        mixed,
                        unscaled,
                        row_scale,
                        mix_gram,
                        products,
                        weights,
                    )
                ],
                flops=3 * square_flops,
            )
            incoming, returned = results[:2]
        inner, code_grad, returned = results[2:]

    enc_blocks = run(
        head_kernel,
        [like((cols, model_cols))] * parts,
        where,
        [heads, (code_grad, proj)],
        scratch=[pltpu.VMEM((codes, model_cols), f32)],
        flops=2 * head_cols * codes * (rows + model_cols),
    )
    code_grad, mix, turned, enc_blocks = lax.optimization_barrier(
        (code_grad, mix, turned, enc_blocks)
    )
    enc_blocks = scattered(enc_blocks, "tensor")
    size = head_cols // groups
    *kept, given = run(
        heads_kernel,
        [like((tokens, size))] * (groups // 2) + [like((rows // 2, size))],
        where,
        [(code_grad, fold_rows)],
    )
    given, mix, turned = lax.optimization_barrier((given, mix, turned))
    head_blocks, attention = exchanged(kept, given, attention, tokens, "dp")
    (proj_grad,) = run(
        proj_kernel,
        [like((head_cols, model_cols))],
        where,
        [(turned, code_grad, enc)],
        scratch=[
            pltpu.VMEM((2, head_cols // 2, model_cols), bf16),
            pltpu.SemaphoreType.DMA((2,)),
        ],
        store=True,
    )
    shapes = [(codes // groups, features), (1, features), (features, relay), (relay, features)]
    dec_grad, gain_grad, send_grad, recv_grad = run(
        feature_kernel,
        [like(shape, f32 if k == 1 else bf16) for k, shape in enumerate(shapes)],
        where,
        [
            (
                attention,
                mix if codes // groups % 128 == 0 else block(mix, "dp", 1),
                received,
                incoming,
                row_scale,
                inner,
                recv,
                send,
                gain,
            )
        ],
        scratch=[pltpu.VMEM(shape, f32) for shape in shapes],
    )
    if size % 128 == 0:
        arrays = []
        for array, _ in head_blocks:
            if not any(array is other for other in arrays):
                arrays.append(array)
        places = [
            (next(k for k, other in enumerate(arrays) if other is array), row)
            for array, row in head_blocks
        ]
        (heads_grad,) = run(
            functools.partial(last_kernel, places),
            [like((tokens, head_cols))],
            where,
            [arrays],
        )
    else:
        blocks = [array[row : row + tokens] for array, row in head_blocks]
        heads_grad = ordered(blocks, "dp")
    enc_grad = total(enc_blocks, where, flops=1 << 33)
    return (
        sent[None],
        returned[None],
        heads_grad[None],
        proj_grad[None],
        enc_grad[None],
        dec_grad[None],
        gain_grad,
        send_grad[None],
        recv_grad[None],
    )


def solution(mesh):
    return jax.shard_map(
        on_device,
        mesh=mesh,
        in_specs=(
            P("pipe", "dp", "tensor"),
            P("pipe", "tensor", "dp"),
            P("pipe", None, "dp"),
            P("pipe", None, "tensor"),
            P("pipe", "tensor"),
            P("pipe", "tensor", None),
            P("pipe", None, "tensor"),
            P("dp", "tensor"),
            P("dp", "tensor"),
        ),
        out_specs=(
            P("pipe", "dp", "tensor"),
            P("pipe", "dp", "tensor"),
            P("pipe", "dp", "tensor"),
            P("pipe", "tensor", "dp"),
            P("pipe", "tensor", "dp"),
            P("pipe", "dp", "tensor"),
            P("pipe", "tensor"),
            P("pipe", "tensor", None),
            P("pipe", None, "tensor"),
        ),
        check_vma=False,
    )
```
